128 devices in a mesh: slab: 8 (over z, core), patch: 16 (over y, x).
Axes of the slice: x: 4, y: 4, z: 4, core: 2. Of those that a mesh axis runs over, the one named last changes fastest.
Arguments:
- temp_start: float32 [128, 512, 512], P('slab', 'patch'), may hold values from -6 to 6
- conduct: float32 [128, 512, 512], P('slab', 'patch'), may hold values from 0.03 to 0.15
- face_cell: int32 [2097152], P(('slab', 'patch')), may hold values from 0 to 262143, as said below
- patch_of_face: int32 [2097152, 1], P(('slab', 'patch')), may hold values from 0 to 255; in each aligned block of 16384 rows (0 to 16383, 16384 to 32767, ...) at most 128 rows name the same one
- face_u: float32 [2097152], P(('slab', 'patch')), may hold values from 0 to 1
- face_v: float32 [2097152], P(('slab', 'patch')), may hold values from 0 to 1
- observed: float32 [2097152], P(('slab', 'patch')), may hold values from -6 to 6
- control_points: float32 [256, 256], P(('slab', 'patch')), may hold values from 0.25 to 2
Outputs:
- temp_final: float32 [128, 512, 512], P('slab', 'patch')
- adjoint_start: float32 [128, 512, 512], P('slab', 'patch')
- grad_points: float32 [256, 256], P(('slab', 'patch'))
The draws below stay inside these ranges and needn't reach their ends.
Inputs may be any that keep to these rules, and one draw needn't show every extreme that they name: `face_cell`: Row-major index of a cell in the block of the device that holds the face; the face with index f within its device lies in the line of 512 cells numbered f // 32, so every line of cells holds the same number of faces (faces are exchange sites spread through the body, not only on its outer boundary). `patch_of_face`: among the faces of one device no patch is named more than 128 times, a bound that some block reaches.
All inputs are finite; a program needn't handle non-finite values.
Results may differ from the reference program's by a relative error of at most 0.0003.
Values sent between devices are 32-bit elements; how exact they have to be, the bound alone decides.
A program may use at most 128 MiB of HBM per device.

```python
import math
import jax
import jax.numpy as jnp
import numpy as np
from jax import lax

CZ = 16
CY = 32
NX = 512
F_DEV = 16384
SIDE = 16
STEPS = 2
CONTROL_POINTS = 256
PATCHES = 256
CAPP = 128
FACES = 2097152
NZ = 128
NY = 512
N_PATCH = 16


def draw_face_cell(key, part):
    key = jax.random.fold_in(key, 11)
    index = jnp.arange(FACES, dtype=jnp.int32)
    per_line = F_DEV // (CZ * CY)
    line = index % F_DEV // per_line
    column = jax.random.randint(key, (FACES,), 0, NX, dtype=jnp.int32)
    cells = line * NX + column
    cells = cells.at[0].set(0)
    cells = cells.at[FACES - 1].set(CZ * CY * NX - 1)
    return cells


def block_levels(stream_key, shape, split, low, largest):
    def one(dim, shards_of):
        draws = jax.random.uniform(jax.random.fold_in(jax.random.fold_in(stream_key, 6), dim), (shards_of,), jnp.float32, low / len(split), largest / len(split))
        return jnp.repeat(jnp.exp(draws), shape[dim] // shards_of).reshape((-1,) + (1,) * (len(shape) - dim - 1))

    gain = one(*split[0])
    for cut in split[1:]:
        gain = gain * one(*cut)
    return gain


def shared_out(rng, own, number, rows, amount, top, limit, lean):
    sequence = jax.random.permutation(rng, amount)
    heavy_load, ordinary = load_shares(amount, rows * top, limit, lean, True), load_shares(amount, rows * top, limit, lean, False)
    places = jnp.arange(amount)

    def named(tallies, rotation):
        used = int((tallies > 0).sum())
        fixed = max(1, used // 4)
        passed = fixed + (places - fixed + rotation * (used - fixed)) % max(1, amount - fixed)
        return jnp.zeros((amount,), jnp.int32).at[sequence[jnp.where(places < fixed, places, passed)]].set(jnp.asarray(tallies, jnp.int32))

    tallies = jnp.where(number % 4 == 0, named(heavy_load, number // 4), named(ordinary, number - number // 4 - 1))
    mixed = jax.random.permutation(jax.random.fold_in(own, 3), amount)
    donor, receiver = mixed[0:amount // 2 * 2:2], mixed[1:amount // 2 * 2:2]
    room = jnp.minimum(tallies[donor] - 1, limit - tallies[receiver]) // 2
    room = jnp.where((donor == sequence[0]) | (receiver == sequence[0]) | (tallies[receiver] == 0), 0, jnp.maximum(room, 0))
    passed = jax.random.randint(jax.random.fold_in(own, 4), (amount // 2,), 0, 1 << 20) % (room + 1)
    tallies = tallies.at[donor].add(-passed).at[receiver].add(passed)
    items = jnp.searchsorted(jnp.cumsum(tallies), jnp.arange(rows * top), side="right").astype(jnp.int32)
    listing = items.reshape(top, rows).T
    listing = listing[jax.random.permutation(jax.random.fold_in(own, 1), rows)]
    rotation = jax.random.randint(jax.random.fold_in(own, 2), (rows, 1), 0, top)
    return jnp.take_along_axis(listing, (jnp.arange(top)[None, :] + rotation) % top, axis=1)


def load_shares(count, total, bound, lean, full):
    portions = [(1 << 20) // math.isqrt(grade ** lean) + 1 for grade in range(1, count + 1)]
    largest = bound if full else min(bound, max(-(-total // count), total * portions[0] // sum(portions)))
    least = 1 if total - largest >= count - 1 else 0
    holding, surplus = [largest] + [least] * (count - 1), total - largest - least * (count - 1)
    while surplus > 0:
        candidates = [i for i in range(1, count) if holding[i] < largest] or [i for i in range(1, count) if holding[i] < bound]
        whole, left = sum([portions[i] for i in candidates]), surplus
        for i in candidates:
            addition = min(bound - holding[i], max(1, left * portions[i] // whole), surplus)
            holding[i] = holding[i] + addition
            surplus = surplus - addition
    return np.array(holding)


def normal_values(stream_key, extent, scale, reach, shards=(), kind=jnp.bfloat16):
    entries = jax.random.normal(stream_key, extent, jnp.float32) * scale
    if len(shards) > 0:
        entries = block_levels(stream_key, extent, shards, -0.22, 0.18) * entries
    return jnp.clip(entries, min=-reach, max=reach).astype(kind)


def setup_inputs(seed: int = 0) -> dict:
    key_list = jax.random.split(jax.random.key(seed), 9)
    temp_start = normal_values(key_list[0], (NZ, NY, NX), 1.0, 6.0, ((0, 8), (1, 16)), jnp.float32)
    conduct = jnp.clip(jnp.exp(math.log(0.15) - 1.609438 * jax.random.uniform(key_list[1], (NZ, NY, NX), jnp.float32) ** block_levels(key_list[1], (NZ, NY, NX), ((0, 8), (1, 16)), -0.2, 0.2)), 0.03, 0.15)
    face_cell = draw_face_cell(jax.random.fold_in(key_list[8], 71), 0)
    patch_of_face_keys = jax.random.split(jax.random.fold_in(key_list[3], 1), FACES // F_DEV)
    patch_of_face_turns = jax.random.permutation(jax.random.fold_in(key_list[3], 3), FACES // F_DEV)
    patch_of_face = jax.vmap(lambda own, number: shared_out(jax.random.fold_in(key_list[3], 2), own, number, F_DEV, PATCHES, 1, CAPP, 2))(patch_of_face_keys, patch_of_face_turns).reshape((FACES, 1))
    face_u = jnp.clip(1.0 * jax.random.uniform(key_list[4], (FACES,), jnp.float32) ** block_levels(key_list[4], (FACES,), ((0, 128),), -0.2, 0.2), 0.0, 1.0)
    face_v = jnp.clip(1.0 * jax.random.uniform(key_list[5], (FACES,), jnp.float32) ** block_levels(key_list[5], (FACES,), ((0, 128),), -0.2, 0.2), 0.0, 1.0)
    observed = normal_values(key_list[6], (FACES,), 1.0, 6.0, ((0, 128),), jnp.float32)
    control_points = jnp.clip(jnp.exp(math.log(2.0) - 2.0794415 * jax.random.uniform(key_list[7], (PATCHES, CONTROL_POINTS), jnp.float32) ** block_levels(key_list[7], (PATCHES, CONTROL_POINTS), ((0, 128),), -0.2, 0.2)), 0.25, 2.0)
    return dict(temp_start=temp_start, conduct=conduct, face_cell=face_cell, patch_of_face=patch_of_face, face_u=face_u, face_v=face_v, observed=observed, control_points=control_points)


HIGH_PRECISION = lax.Precision.HIGHEST


def basis_weights(param):
    knots = 3.0 + 13.0 * param
    place = jnp.arange(16, dtype=jnp.float32)
    xval = jnp.clip(knots[None, :] - place[:, None], 0.0, 4.0)
    one = jax.nn.relu(xval - 1.0)
    two = jax.nn.relu(xval - 2.0)
    three = jax.nn.relu(xval - 3.0)
    return (xval * xval * xval - 4.0 * one * one * one + 6.0 * two * two * two - 4.0 * three * three * three) / 6.0


def neighbours(field):
    padded = jnp.pad(field, 1)
    total = padded[2:, 1:-1, 1:-1] + padded[:-2, 1:-1, 1:-1]
    total = total + padded[1:-1, 2:, 1:-1] + padded[1:-1, :-2, 1:-1]
    return total + padded[1:-1, 1:-1, 2:] + padded[1:-1, 1:-1, :-2]


def reference(temp_start, conduct, face_cell, patch_of_face, face_u, face_v, observed, control_points):
    device = jnp.arange(FACES, dtype=jnp.int32) // F_DEV
    slab_at = device // N_PATCH
    patch_at = device % N_PATCH
    zpos = face_cell // (CY * NX)
    ypos = (face_cell // NX) % CY
    xpos = face_cell % NX
    flat = ((slab_at * CZ + zpos) * NY + patch_at * CY + ypos) * NX + xpos
    pid = patch_of_face[:, 0]

    def pick(field):
        return field.reshape(-1)[flat]

    def spread(values):
        return jnp.zeros((NZ * NY * NX,), jnp.float32).at[flat].add(values).reshape(NZ, NY, NX)

    def htc_block(single_entry):
        patch_indices, u_coordinates, v_coordinates = single_entry
        surface_grid = control_points[patch_indices].reshape(-1, SIDE, SIDE)
        return jnp.einsum("cdx,dc,xc->c", surface_grid, basis_weights(u_coordinates), basis_weights(v_coordinates), precision=HIGH_PRECISION)

    blocks = (pid.reshape(-1, F_DEV), face_u.reshape(-1, F_DEV), face_v.reshape(-1, F_DEV))
    htc = lax.map(htc_block, blocks).reshape(-1)

    temp = temp_start
    at_faces = []
    for step in range(STEPS):
        tface = pick(temp)
        at_faces.append(tface)
        temp = temp + conduct * (neighbours(temp) - 6.0 * temp) - 0.3 * spread(htc * tface)
    adjoint = spread(pick(temp) - observed)
    sens = jnp.zeros((FACES,), jnp.float32)
    for step in range(STEPS - 1, -1, -1):
        aface = pick(adjoint)
        sens = sens - 0.3 * aface * at_faces[step]
        weighted = conduct * adjoint
        adjoint = adjoint + neighbours(weighted) - 6.0 * weighted - 0.3 * spread(htc * aface)

    def grad_block(carry, single_entry):
        patch_indices, u_coordinates, v_coordinates, spline_values = single_entry
        outer_product = (basis_weights(u_coordinates)[:, None, :] * basis_weights(v_coordinates)[None, :, :]).reshape(CONTROL_POINTS, -1)
        basis_terms = outer_product.T * spline_values[:, None]
        return carry + jax.ops.segment_sum(basis_terms, patch_indices, PATCHES), None

    grad_points, unused = lax.scan(grad_block, jnp.zeros((PATCHES, CONTROL_POINTS), jnp.float32), blocks + (sens.reshape(-1, F_DEV),))
    return temp, adjoint, grad_points
```

```python
import functools

import jax
import jax.numpy as jnp
from jax import lax
from jax.experimental import pallas as pl
from jax.experimental.pallas import tpu as pltpu
from jax.sharding import PartitionSpec as P

MESH = pl.DeviceIdType.MESH
F32 = jnp.float32
BF16 = jnp.bfloat16
NZ = 16
NQ = 4
NC = 4
PLANE = (NQ, NC, 8, 128)
ROWS = 128
CHUNK = 1024
PER = CHUNK // 128
NCHUNK = ROWS * 128 // CHUNK


def iota(shape, dim):
    return lax.broadcasted_iota(jnp.int32, shape, dim)


def lanes(x, index):
    return jnp.take_along_axis(x, index, axis=1, mode="promise_in_bounds")


def basis_weights(param):
    knots = 3.0 + 13.0 * param
    xval = jnp.clip(knots - iota((16, 128), 0).astype(F32), 0.0, 4.0)
    one = jnp.maximum(xval - 1.0, 0.0)
    two = jnp.maximum(xval - 2.0, 0.0)
    three = jnp.maximum(xval - 3.0, 0.0)
    return (
        xval * xval * xval
        - 4.0 * one * one * one
        + 6.0 * two * two * two
        - 4.0 * three * three * three
    ) / 6.0


def split(x):
    high = x.astype(BF16)
    return high, (x - high.astype(F32)).astype(BF16)


def kernel(
    n_slab,
    n_patch,
    temp_hbm,
    cond_hbm,
    cell_ref,
    pid_ref,
    u_ref,
    v_ref,
    obs_ref,
    cp_ref,
    tout_hbm,
    aout_hbm,
    gout_ref,
    tin,
    cin,
    tst,
    ast,
    t0,
    t1,
    w2,
    w1,
    cond,
    hfld,
    cntf,
    obsf,
    pre1,
    adj2,
    adj1,
    inv,
    same,
    ysend,
    yrecv,
    cp_src,
    cp_row,
    cp_all,
    lhs,
    onehot,
    bu,
    bv,
    wbuf,
    htc,
    sens,
    acc,
    grad,
    part1,
    part2_src,
    part2,
    in_sem,
    out_sem,
    ag1_send,
    ag1_recv,
    ag2_send,
    ag2_recv,
    rs1_send,
    rs1_recv,
    rs2_send,
    rs2_recv,
    halo_send,
    halo_recv,
):
    s = lax.axis_index("slab")
    t = lax.axis_index("patch")

    def on_slab(k):
        return (lax.rem(s + k, n_slab), t)

    def on_patch(k):
        return (s, lax.rem(t + k, n_patch))

    loads = []
    for a, (src, dst) in enumerate(((temp_hbm, tin), (cond_hbm, cin))):
        for c in range(NC):
            copy = pltpu.make_async_copy(
                src.at[:, :, pl.ds(128 * c, 128)], dst.at[c], in_sem.at[a, c]
            )
            copy.start()
            loads.append(copy)

    barrier = pltpu.get_barrier_semaphore()
    for k in range(1, n_slab):
        pl.semaphore_signal(barrier, inc=1, device_id=on_slab(k), device_id_type=MESH)
    for k in range(1, n_patch):
        pl.semaphore_signal(barrier, inc=1, device_id=on_patch(k), device_id_type=MESH)
    cp_src[0:2, :] = cp_ref[:, 0:128]
    cp_src[2:4, :] = cp_ref[:, 128:256]
    cp_row[t] = cp_src[...]
    pl.semaphore_wait(barrier, n_slab + n_patch - 2)

    ag1 = []
    for k in range(1, n_patch):
        copy = pltpu.make_async_remote_copy(
            cp_src, cp_row.at[t], ag1_send.at[k], ag1_recv.at[k], on_patch(k), MESH
        )
        copy.start()
        ag1.append(copy)

    def halo_copies(e, field):
        return [
            pltpu.make_async_remote_copy(
                field.at[NZ],
                field.at[0],
                halo_send.at[e, 0],
                halo_recv.at[e, 0],
                on_slab(1),
                MESH,
            ),
            pltpu.make_async_remote_copy(
                field.at[1],
                field.at[NZ + 1],
                halo_send.at[e, 1],
                halo_recv.at[e, 1],
                on_slab(n_slab - 1),
                MESH,
            ),
            pltpu.make_async_remote_copy(
                ysend.at[e, 1],
                yrecv.at[e, 0],
                halo_send.at[e, 2],
                halo_recv.at[e, 2],
                on_patch(1),
                MESH,
            ),
            pltpu.make_async_remote_copy(
                ysend.at[e, 0],
                yrecv.at[e, 1],
                halo_send.at[e, 3],
                halo_recv.at[e, 3],
                on_patch(n_patch - 1),
                MESH,
            ),
        ]

    def halo_start(e, field):
        copies = halo_copies(e, field)
        for copy in copies:
            copy.start()
        return copies

    def halo_wait(e, field, copies):
        for copy in copies:
            copy.wait()

        @pl.when(s == 0)
        def _():
            field[0] = jnp.zeros(PLANE, F32)

        @pl.when(s == n_slab - 1)
        def _():
            field[NZ + 1] = jnp.zeros(PLANE, F32)

        @pl.when(t == 0)
        def _():
            yrecv[e, 0] = jnp.zeros((NZ * NC, 128), F32)

        @pl.when(t == n_patch - 1)
        def _():
            yrecv[e, 1] = jnp.zeros((NZ * NC, 128), F32)

    def put(e, field, z, plane):
        for q in range(NQ):
            for c in range(NC):
                field[z + 1, q, c] = plane[q][c]
        for c in range(NC):
            ysend[e, 0, pl.ds(z * NC + c, 1), :] = plane[0][c][0:1, :]
            ysend[e, 1, pl.ds(z * NC + c, 1), :] = plane[NQ - 1][c][7:8, :]

    lane = iota((8, 128), 1)
    row8 = iota((8, 128), 0)

    def around(e, field, z):
        centre = [[field[z + 1, q, c] for c in range(NC)] for q in range(NQ)]
        total = [[None] * NC for _ in range(NQ)]
        for q in range(NQ):
            right = [pltpu.roll(centre[q][c], 127, 1) for c in range(NC)]
            left = [pltpu.roll(centre[q][c], 1, 1) for c in range(NC)]
            for c in range(NC):
                after = right[c + 1] if c + 1 < NC else 0.0
                before = left[c - 1] if c else 0.0
                x = jnp.where(lane == 127, after, right[c]) + jnp.where(
                    lane == 0, before, left[c]
                )
                if q + 1 < NQ:
                    y_up = centre[q + 1][c]
                else:
                    edge = yrecv[e, 1, pl.ds(z * NC + c, 1), :]
                    y_up = jnp.where(
                        row8 == 7, jnp.broadcast_to(edge, (8, 128)), pltpu.roll(centre[0][c], 7, 0)
                    )
                if q:
                    y_down = centre[q - 1][c]
                else:
                    edge = yrecv[e, 0, pl.ds(z * NC + c, 1), :]
                    y_down = jnp.where(
                        row8 == 0,
                        jnp.broadcast_to(edge, (8, 128)),
                        pltpu.roll(centre[NQ - 1][c], 1, 0),
                    )
                total[q][c] = (field[z, q, c] + field[z + 2, q, c]) + (y_up + y_down) + x
        return centre, total

    for copy in loads[:NC]:
        copy.wait()

    @pl.loop(0, NZ)
    def _(z):
        put(
            0,
            t0,
            z,
            [
                [tin[c, z, pl.ds(q, 8, stride=NQ), :] for c in range(NC)]
                for q in range(NQ)
            ],
        )

    halo0 = halo_start(0, t0)

    for copy in ag1:
        copy.wait()
    mine = pl.ds(pl.multiple_of(s * (4 * n_patch), 4 * n_patch), 4 * n_patch)
    cp_all[mine, :] = cp_row[...].reshape(4 * n_patch, 128)
    ag2 = []
    for k in range(1, n_slab):
        copy = pltpu.make_async_remote_copy(
            cp_all.at[mine], cp_all.at[mine], ag2_send.at[k], ag2_recv.at[k], on_slab(k), MESH
        )
        copy.start()
        ag2.append(copy)

    for copy in loads[NC:]:
        copy.wait()

    rotations = [(lane & 96) | ((lane + k) & 31) for k in range(1, 32)]
    group = lane >> 5

    def combine(z, value):
        total = value
        for k in range(31):
            total = total + same[k, pl.ds(pl.multiple_of(z * 8, 8), 8), :] * lanes(value, rotations[k])
        return total

    def spread(z, values, dst):
        for q in range(NQ):
            src = jnp.where(group == q, values, 0.0)
            for c in range(NC):
                dst[z, q, c] = lanes(src, inv[z, q, c])

    @pl.loop(0, NZ)
    def _(z):
        rows = pl.ds(pl.multiple_of(z * 8, 8), 8)
        for q in range(NQ):
            for c in range(NC):
                cond[z, q, c] = cin[c, z, pl.ds(q, 8, stride=NQ), :]
        column = cell_ref[rows, :] & 511
        for q in range(NQ):
            found = [jnp.full((8, 128), 32 * ((q + 1) % NQ), jnp.int32) for _ in range(NC)]
            for j in range(32):
                which = 32 * q + j
                off = jnp.broadcast_to(column[:, which : which + 1], (8, 128)) - lane
                for c in range(NC):
                    found[c] = jnp.where(off == 128 * c, which, found[c])
            for c in range(NC):
                inv[z, q, c] = found[c]
        count = jnp.ones((8, 128), F32)
        observed = obs_ref[rows, :]
        seen = observed
        for k in range(31):
            equal = (lanes(column, rotations[k]) == column).astype(F32)
            same[k, rows, :] = equal
            count = count + equal
            seen = seen + equal * lanes(observed, rotations[k])
        spread(z, count, cntf)
        spread(z, seen, obsf)

    @pl.loop(0, NCHUNK)
    def _(i):
        rows = pl.ds(pl.multiple_of(i * PER, PER), PER)
        pid = pid_ref[rows, :]
        pid = (pid & 1) * 128 + (pid >> 1)
        uu = u_ref[rows, :]
        vv = v_ref[rows, :]
        for r in range(PER):
            at = slice(128 * r, 128 * r + 128)
            onehot[i, :, at] = jnp.where(
                iota((256, 128), 0) == pid[r : r + 1, :], 1.0, 0.0
            ).astype(BF16)
            bu[i, :, at] = basis_weights(uu[r : r + 1, :])
            bv[i, :, at] = basis_weights(vv[r : r + 1, :])

    halo_wait(0, t0, halo0)

    @pl.loop(0, NZ)
    def _(z):
        centre, total = around(0, t0, z)
        for q in range(NQ):
            for c in range(NC):
                pre1[z, q, c] = centre[q][c] + cond[z, q, c] * (total[q][c] - 6.0 * centre[q][c])

    for copy in ag2:
        copy.wait()
    for c in range(2):
        for k in range(2):
            block = cp_all[pl.ds(2 * c + k, 128, stride=4), :].T
            high, low = split(block)
            lhs[128 * c : 128 * c + 128, 128 * k : 128 * k + 128] = high
            lhs[256 + 128 * c : 384 + 128 * c, 128 * k : 128 * k + 128] = low

    @pl.loop(0, NCHUNK)
    def _(i):
        for h in range(CHUNK // 256):
            at = slice(256 * h, 256 * h + 256)
            both = jnp.dot(lhs[...], onehot[i, :, at], preferred_element_type=F32)
            own = both[0:256] + both[256:512]
            total = own[0:16] * bu[i, 0:1, at]
            for a in range(1, 16):
                total = total + own[16 * a : 16 * a + 16] * bu[i, a : a + 1, at]
            value = -0.3 * jnp.sum(total * bv[i, :, at], axis=0, keepdims=True)
            for r in range(2):
                htc[pl.ds(i * PER + 2 * h + r, 1), :] = value[:, 128 * r : 128 * r + 128]

    @pl.loop(0, NZ)
    def _(z):
        spread(z, combine(z, htc[pl.ds(pl.multiple_of(z * 8, 8), 8), :]), hfld)
        put(
            1,
            t1,
            z,
            [
                [pre1[z, q, c] + hfld[z, q, c] * t0[z + 1, q, c] for c in range(NC)]
                for q in range(NQ)
            ],
        )

    halo1 = halo_start(1, t1)
    halo_wait(1, t1, halo1)

    @pl.loop(0, NZ)
    def _(z):
        centre, total = around(1, t1, z)
        weighted = [[None] * NC for _ in range(NQ)]
        for q in range(NQ):
            for c in range(NC):
                here = cond[z, q, c]
                last = (
                    centre[q][c]
                    + here * (total[q][c] - 6.0 * centre[q][c])
                    + hfld[z, q, c] * centre[q][c]
                )
                tst[c, z, pl.ds(q, 8, stride=NQ), :] = last
                adjoint = cntf[z, q, c] * last - obsf[z, q, c]
                adj2[z, q, c] = adjoint
                weighted[q][c] = here * adjoint
        put(2, w2, z, weighted)

    halo2 = halo_start(2, w2)
    stores = []
    for c in range(NC):
        copy = pltpu.make_async_copy(
            tst.at[c], tout_hbm.at[:, :, pl.ds(128 * c, 128)], out_sem.at[0, c]
        )
        copy.start()
        stores.append(copy)
    halo_wait(2, w2, halo2)

    @pl.loop(0, NZ)
    def _(z):
        centre, total = around(2, w2, z)
        rows = pl.ds(pl.multiple_of(z * 8, 8), 8)
        column = cell_ref[rows, :] & 511
        key = group * NC + (column >> 7)
        spot = column & 127
        picked = jnp.zeros((8, 128), F32)
        weighted = [[None] * NC for _ in range(NQ)]
        for q in range(NQ):
            for c in range(NC):
                later = adj2[z, q, c]
                adjoint = later + total[q][c] - 6.0 * centre[q][c] + hfld[z, q, c] * later
                adj1[z, q, c] = adjoint
                weighted[q][c] = cond[z, q, c] * adjoint
                product = later * t1[z + 1, q, c] + adjoint * t0[z + 1, q, c]
                picked = jnp.where(key == NC * q + c, lanes(product, spot), picked)
        sens[rows, :] = -0.3 * picked
        put(3, w1, z, weighted)

    halo3 = halo_start(3, w1)

    acc[...] = jnp.zeros((512, 256), F32)

    @pl.loop(0, NCHUNK)
    def _(i):
        value = sens[pl.ds(pl.multiple_of(i * PER, PER), PER), :]
        for r in range(PER):
            at = slice(128 * r, 128 * r + 128)
            right = bv[i, :, at] * value[r : r + 1, :]
            for a in range(16):
                high, low = split(right * bu[i, a : a + 1, at])
                wbuf[16 * a : 16 * a + 16, at] = high
                wbuf[256 + 16 * a : 272 + 16 * a, at] = low
        acc[...] += lax.dot_general(
            wbuf[...], onehot[i], (((1,), (1,)), ((), ())), preferred_element_type=F32
        )

    for c in range(2):
        for k in range(2):
            cols = slice(128 * k, 128 * k + 128)
            block = acc[128 * c : 128 * c + 128, cols] + acc[256 + 128 * c : 384 + 128 * c, cols]
            grad[pl.ds(2 * c + k, 128, stride=4), :] = block.T

    rs1 = []
    for k in range(1, n_slab):
        their = lax.rem(s + k, n_slab)
        copy = pltpu.make_async_remote_copy(
            grad.at[pl.ds(pl.multiple_of(their * (4 * n_patch), 4 * n_patch), 4 * n_patch)],
            part1.at[k],
            rs1_send.at[k],
            rs1_recv.at[k],
            on_slab(k),
            MESH,
        )
        copy.start()
        rs1.append(copy)

    halo_wait(3, w1, halo3)

    @pl.loop(0, NZ)
    def _(z):
        centre, total = around(3, w1, z)
        for q in range(NQ):
            for c in range(NC):
                later = adj1[z, q, c]
                ast[c, z, pl.ds(q, 8, stride=NQ), :] = (
                    later + total[q][c] - 6.0 * centre[q][c] + hfld[z, q, c] * later
                )

    for c in range(NC):
        copy = pltpu.make_async_copy(
            ast.at[c], aout_hbm.at[:, :, pl.ds(128 * c, 128)], out_sem.at[1, c]
        )
        copy.start()
        stores.append(copy)

    for copy in rs1:
        copy.wait()
    total = grad[mine, :]
    for k in range(1, n_slab):
        total = total + part1[k]
    part2_src[...] = total.reshape(n_patch, 4, 128)
    rs2 = []
    for k in range(1, n_patch):
        copy = pltpu.make_async_remote_copy(
            part2_src.at[lax.rem(t + k, n_patch)],
            part2.at[k],
            rs2_send.at[k],
            rs2_recv.at[k],
            on_patch(k),
            MESH,
        )
        copy.start()
        rs2.append(copy)
    for copy in rs2:
        copy.wait()
    total = part2_src[t]
    for k in range(1, n_patch):
        total = total + part2[k]
    gout_ref[:, 0:128] = total[0:2]
    gout_ref[:, 128:256] = total[2:4]
    for copy in stores:
        copy.wait()


def local(n_slab, n_patch, temp, cond, cell, pid, u, v, observed, points):
    field = (NZ,) + PLANE
    padded = (NZ + 2,) + PLANE
    natural = (NC, NZ, 32, 128)
    vmem = pltpu.VMEM
    dma = pltpu.SemaphoreType.DMA
    scratch = [
        vmem(natural, F32),
        vmem(natural, F32),
        vmem(natural, F32),
        vmem(natural, F32),
        vmem(padded, F32),
        vmem(padded, F32),
        vmem(padded, F32),
        vmem(padded, F32),
        vmem(field, F32),
        vmem(field, F32),
        vmem(field, F32),
        vmem(field, F32),
        vmem(field, F32),
        vmem(field, F32),
        vmem(field, F32),
        vmem(field, jnp.int32),
        vmem((31, ROWS, 128), F32),
        vmem((4, 2, NZ * NC, 128), F32),
        vmem((4, 2, NZ * NC, 128), F32),
        vmem((4, 128), F32),
        vmem((n_patch, 4, 128), F32),
        vmem((4 * n_slab * n_patch, 128), F32),
        vmem((512, 256), BF16),
        vmem((NCHUNK, 256, CHUNK), BF16),
        vmem((NCHUNK, 16, CHUNK), F32),
        vmem((NCHUNK, 16, CHUNK), F32),
        vmem((512, CHUNK), BF16),
        vmem((ROWS, 128), F32),
        vmem((ROWS, 128), F32),
        vmem((512, 256), F32),
        vmem((4 * n_slab * n_patch, 128), F32),
        vmem((n_slab, 4 * n_patch, 128), F32),
        vmem((n_patch, 4, 128), F32),
        vmem((n_patch, 4, 128), F32),
        dma((2, NC)),
        dma((2, NC)),
        dma((n_patch,)),
        dma((n_patch,)),
        dma((n_slab,)),
        dma((n_slab,)),
        dma((n_slab,)),
        dma((n_slab,)),
        dma((n_patch,)),
        dma((n_patch,)),
        dma((4, 4)),
        dma((4, 4)),
    ]
    whole = pl.BlockSpec(memory_space=pltpu.VMEM)
    anywhere = pl.BlockSpec(memory_space=pl.ANY)
    rows = (ROWS, 128)
    return pl.pallas_call(
        functools.partial(kernel, n_slab, n_patch),
        out_shape=(
            jax.ShapeDtypeStruct(temp.shape, F32),
            jax.ShapeDtypeStruct(temp.shape, F32),
            jax.ShapeDtypeStruct(points.shape, F32),
        ),
        in_specs=[anywhere, anywhere] + [whole] * 6,
        out_specs=(anywhere, anywhere, whole),
        scratch_shapes=scratch,
        compiler_params=pltpu.CompilerParams(
            collective_id=0, has_side_effects=True, vmem_limit_bytes=56 * 1024 * 1024
        ),
        name="adjoint",
    )(
        temp,
        cond,
        cell.reshape(rows),
        pid.reshape(rows),
        u.reshape(rows),
        v.reshape(rows),
        observed.reshape(rows),
        points,
    )


def solution(mesh):
    in_specs = (
        P("slab", "patch", None),
        P("slab", "patch", None),
        P(("slab", "patch")),
        P(("slab", "patch"), None),
        P(("slab", "patch")),
        P(("slab", "patch")),
        P(("slab", "patch")),
        P(("slab", "patch"), None),
    )
    out_specs = (P("slab", "patch", None), P("slab", "patch", None), P(("slab", "patch"), None))
    return jax.shard_map(
        functools.partial(local, mesh.shape["slab"], mesh.shape["patch"]),
        mesh=mesh,
        in_specs=in_specs,
        out_specs=out_specs,
        check_vma=False,
    )
```

```python
import functools

import jax
import jax.numpy as jnp
from jax import lax
from jax.experimental import pallas as pl
from jax.experimental.pallas import tpu as pltpu
from jax.sharding import PartitionSpec as P

MESH = pl.DeviceIdType.MESH
F32 = jnp.float32
BF16 = jnp.bfloat16
NZ = 16
NQ = 4
NC = 4
PLANE = (NQ, NC, 8, 128)
ROWS = 128
CHUNK = 1024
PER = CHUNK // 128
NCHUNK = ROWS * 128 // CHUNK


def iota(shape, dim):
    return lax.broadcasted_iota(jnp.int32, shape, dim)


def lanes(x, index):
    return jnp.take_along_axis(x, index, axis=1, mode="promise_in_bounds")


def basis_weights(param):
    y = jnp.abs((3.0 + 13.0 * param) - (iota((16, 128), 0) + 2).astype(F32))
    wide = jnp.maximum(2.0 - y, 0.0)
    narrow = jnp.maximum(1.0 - y, 0.0)
    return wide * wide * wide * (1.0 / 6.0) - narrow * narrow * narrow * (4.0 / 6.0)


def split(x):
    high = x.astype(BF16)
    return high, (x - high.astype(F32)).astype(BF16)


def kernel(
    n_slab,
    n_patch,
    temp_hbm,
    cond_hbm,
    cell_ref,
    pid_ref,
    u_ref,
    v_ref,
    obs_ref,
    cp_ref,
    tout_hbm,
    aout_hbm,
    gout_ref,
    tin,
    cin,
    tst,
    ast,
    t0,
    t1,
    w2,
    w1,
    cond,
    hfld,
    cntf,
    obsf,
    pre1,
    adj2,
    adj1,
    inv,
    chain,
    summed,
    ysend,
    yrecv,
    cp_src,
    cp_row,
    cp_all,
    lhs,
    onehot,
    bu,
    bv,
    wbuf,
    htc,
    sens,
    acc,
    grad,
    part1,
    part2_src,
    part2,
    in_sem,
    out_sem,
    ag1_send,
    ag1_recv,
    ag2_send,
    ag2_recv,
    rs1_send,
    rs1_recv,
    rs2_send,
    rs2_recv,
    halo_send,
    halo_recv,
):
    s = lax.axis_index("slab")
    t = lax.axis_index("patch")

    def on_slab(k):
        return (lax.rem(s + k, n_slab), t)

    def on_patch(k):
        return (s, lax.rem(t + k, n_patch))

    loads = []
    for a, (src, dst) in enumerate(((temp_hbm, tin), (cond_hbm, cin))):
        for c in range(NC):
            copy = pltpu.make_async_copy(
                src.at[:, :, pl.ds(128 * c, 128)], dst.at[c], in_sem.at[a, c]
            )
            copy.start()
            loads.append(copy)

    barrier = pltpu.get_barrier_semaphore()
    for k in range(1, n_slab):
        pl.semaphore_signal(barrier, inc=1, device_id=on_slab(k), device_id_type=MESH)
    for k in range(1, n_patch):
        pl.semaphore_signal(barrier, inc=1, device_id=on_patch(k), device_id_type=MESH)
    cp_src[0:2, :] = cp_ref[:, 0:128]
    cp_src[2:4, :] = cp_ref[:, 128:256]
    cp_row[t] = cp_src[...]
    pl.semaphore_wait(barrier, n_slab + n_patch - 2)

    ag1 = []
    for k in range(1, n_patch):
        copy = pltpu.make_async_remote_copy(
            cp_src, cp_row.at[t], ag1_send.at[k], ag1_recv.at[k], on_patch(k), MESH
        )
        copy.start()
        ag1.append(copy)

    def halo_copies(e, field):
        return [
            pltpu.make_async_remote_copy(
                field.at[NZ],
                field.at[0],
                halo_send.at[e, 0],
                halo_recv.at[e, 0],
                on_slab(1),
                MESH,
            ),
            pltpu.make_async_remote_copy(
                field.at[1],
                field.at[NZ + 1],
                halo_send.at[e, 1],
                halo_recv.at[e, 1],
                on_slab(n_slab - 1),
                MESH,
            ),
            pltpu.make_async_remote_copy(
                ysend.at[e, 1],
                yrecv.at[e, 0],
                halo_send.at[e, 2],
                halo_recv.at[e, 2],
                on_patch(1),
                MESH,
            ),
            pltpu.make_async_remote_copy(
                ysend.at[e, 0],
                yrecv.at[e, 1],
                halo_send.at[e, 3],
                halo_recv.at[e, 3],
                on_patch(n_patch - 1),
                MESH,
            ),
        ]

    def halo_start(e, field):
        copies = halo_copies(e, field)
        for copy in copies:
            copy.start()
        return copies

    def halo_wait(e, field, copies):
        for copy in copies:
            copy.wait()

        @pl.when(s == 0)
        def _():
            field[0] = jnp.zeros(PLANE, F32)

        @pl.when(s == n_slab - 1)
        def _():
            field[NZ + 1] = jnp.zeros(PLANE, F32)

        @pl.when(t == 0)
        def _():
            yrecv[e, 0] = jnp.zeros((NZ * NC, 128), F32)

        @pl.when(t == n_patch - 1)
        def _():
            yrecv[e, 1] = jnp.zeros((NZ * NC, 128), F32)

    def put(e, field, z, plane):
        for q in range(NQ):
            for c in range(NC):
                field[z + 1, q, c] = plane[q][c]
        for c in range(NC):
            ysend[e, 0, pl.ds(z * NC + c, 1), :] = plane[0][c][0:1, :]
            ysend[e, 1, pl.ds(z * NC + c, 1), :] = plane[NQ - 1][c][7:8, :]

    lane = iota((8, 128), 1)
    row8 = iota((8, 128), 0)

    def around(e, field, z):
        centre = [[field[z + 1, q, c] for c in range(NC)] for q in range(NQ)]
        total = [[None] * NC for _ in range(NQ)]
        for q in range(NQ):
            right = [pltpu.roll(centre[q][c], 127, 1) for c in range(NC)]
            left = [pltpu.roll(centre[q][c], 1, 1) for c in range(NC)]
            for c in range(NC):
                after = right[c + 1] if c + 1 < NC else 0.0
                before = left[c - 1] if c else 0.0
                x = jnp.where(lane == 127, after, right[c]) + jnp.where(
                    lane == 0, before, left[c]
                )
                if q + 1 < NQ:
                    y_up = centre[q + 1][c]
                else:
                    edge = yrecv[e, 1, pl.ds(z * NC + c, 1), :]
                    y_up = jnp.where(
                        row8 == 7, jnp.broadcast_to(edge, (8, 128)), pltpu.roll(centre[0][c], 7, 0)
                    )
                if q:
                    y_down = centre[q - 1][c]
                else:
                    edge = yrecv[e, 0, pl.ds(z * NC + c, 1), :]
                    y_down = jnp.where(
                        row8 == 0,
                        jnp.broadcast_to(edge, (8, 128)),
                        pltpu.roll(centre[NQ - 1][c], 1, 0),
                    )
                total[q][c] = (field[z, q, c] + field[z + 2, q, c]) + (y_up + y_down) + x
        return centre, total

    for copy in loads[:NC]:
        copy.wait()

    @pl.loop(0, NZ)
    def _(z):
        put(
            0,
            t0,
            z,
            [
                [tin[c, z, pl.ds(q, 8, stride=NQ), :] for c in range(NC)]
                for q in range(NQ)
            ],
        )

    halo0 = halo_start(0, t0)

    @pl.loop(0, NCHUNK)
    def _(i):
        rows = pl.ds(pl.multiple_of(i * PER, PER), PER)
        pid = pid_ref[rows, :]
        pid = ((pid & 1) * 128 + (pid >> 1)).astype(F32)
        uu = u_ref[rows, :]
        vv = v_ref[rows, :]
        places = iota((256, 128), 0).astype(F32).astype(BF16)
        for r in range(PER):
            at = slice(128 * r, 128 * r + 128)
            row = jnp.broadcast_to(pid[r : r + 1, :], (16, 128)).astype(BF16)
            for k in range(16):
                onehot[i, 16 * k : 16 * k + 16, at] = jnp.where(
                    places[16 * k : 16 * k + 16] == row, jnp.ones((), BF16), jnp.zeros((), BF16)
                )
            bu[i, :, at] = basis_weights(uu[r : r + 1, :])
            bv[i, :, at] = basis_weights(vv[r : r + 1, :])

    for copy in ag1:
        copy.wait()
    mine = pl.ds(pl.multiple_of(s * (4 * n_patch), 4 * n_patch), 4 * n_patch)
    cp_all[mine, :] = cp_row[...].reshape(4 * n_patch, 128)
    ag2 = []
    for k in range(1, n_slab):
        copy = pltpu.make_async_remote_copy(
            cp_all.at[mine], cp_all.at[mine], ag2_send.at[k], ag2_recv.at[k], on_slab(k), MESH
        )
        copy.start()
        ag2.append(copy)

    group = lane >> 5
    within = lane & 31
    for g in range(NZ):
        rows = slice(8 * g, 8 * g + 8)
        column = cell_ref[rows, :] & 511
        back = jnp.full((8, 128), -1, jnp.int32)
        for k in range(31, 0, -1):
            back = jnp.where(
                (pltpu.roll(column, k, 1) == column) & (within >= k), lane - k, back
            )
        chain[0, rows, :] = back
    for r in range(5):
        for g in range(NZ):
            rows = slice(8 * g, 8 * g + 8)
            back = chain[r, rows, :]
            index = back & 127
            count = jnp.ones((8, 128), F32) if r == 0 else summed[0, rows, :]
            seen = obs_ref[rows, :] if r == 0 else summed[1, rows, :]
            summed[0, rows, :] = count + jnp.where(back >= 0, lanes(count, index), 0.0)
            summed[1, rows, :] = seen + jnp.where(back >= 0, lanes(seen, index), 0.0)
            if r < 4:
                chain[r + 1, rows, :] = jnp.where(back >= 0, lanes(back, index), -1)

    def spread(z, values, dst):
        for q in range(NQ):
            src = jnp.where(group == q, values, 0.0)
            for c in range(NC):
                dst[z, q, c] = lanes(src, inv[z, q, c])

    lane16 = iota((16, 128), 1).astype(jnp.int16)

    @pl.loop(0, NZ // 2)
    def _(h):
        column = (cell_ref[pl.ds(pl.multiple_of(h * 16, 16), 16), :] & 511).astype(jnp.int16)
        for q in range(NQ):
            found = [jnp.full((16, 128), 32 * ((q + 1) % NQ), jnp.int16) for _ in range(NC)]
            for j in range(32):
                which = 32 * q + j
                off = jnp.broadcast_to(column[:, which : which + 1], (16, 128)) - lane16
                for c in range(NC):
                    found[c] = jnp.where(
                        off == jnp.int16(128 * c), jnp.int16(which), found[c]
                    )
            for c in range(NC):
                both = found[c].astype(jnp.int32)
                inv[2 * h, q, c] = both[0:8]
                inv[2 * h + 1, q, c] = both[8:16]
        for d in range(2):
            z = 2 * h + d
            rows = pl.ds(pl.multiple_of(z * 8, 8), 8)
            spread(z, summed[0, rows, :], cntf)
            spread(z, summed[1, rows, :], obsf)

    for copy in loads[NC:]:
        copy.wait()

    @pl.loop(0, NZ)
    def _(z):
        for q in range(NQ):
            for c in range(NC):
                cond[z, q, c] = cin[c, z, pl.ds(q, 8, stride=NQ), :]

    halo_wait(0, t0, halo0)

    @pl.loop(0, NZ)
    def _(z):
        centre, total = around(0, t0, z)
        for q in range(NQ):
            for c in range(NC):
                pre1[z, q, c] = centre[q][c] + cond[z, q, c] * (total[q][c] - 6.0 * centre[q][c])

    for copy in ag2:
        copy.wait()
    for c in range(2):
        for k in range(2):
            block = cp_all[pl.ds(2 * c + k, 128, stride=4), :].T
            high, low = split(block)
            lhs[128 * c : 128 * c + 128, 128 * k : 128 * k + 128] = high
            lhs[256 + 128 * c : 384 + 128 * c, 128 * k : 128 * k + 128] = low

    @pl.loop(0, NCHUNK)
    def _(i):
        for h in range(CHUNK // 256):
            at = slice(256 * h, 256 * h + 256)
            both = jnp.dot(lhs[...], onehot[i, :, at], preferred_element_type=F32)
            own = both[0:256] + both[256:512]
            total = own[0:16] * bu[i, 0:1, at]
            for a in range(1, 16):
                total = total + own[16 * a : 16 * a + 16] * bu[i, a : a + 1, at]
            value = -0.3 * jnp.sum(total * bv[i, :, at], axis=0, keepdims=True)
            for r in range(2):
                htc[pl.ds(i * PER + 2 * h + r, 1), :] = value[:, 128 * r : 128 * r + 128]

    for r in range(5):
        for g in range(NZ):
            rows = slice(8 * g, 8 * g + 8)
            back = chain[r, rows, :]
            value = htc[rows, :]
            htc[rows, :] = value + jnp.where(back >= 0, lanes(value, back & 127), 0.0)

    @pl.loop(0, NZ // 4)
    def _(h):
        for d in range(4):
            z = 4 * h + d
            spread(z, htc[pl.ds(pl.multiple_of(z * 8, 8), 8), :], hfld)
            put(
                1,
                t1,
                z,
                [
                    [pre1[z, q, c] + hfld[z, q, c] * t0[z + 1, q, c] for c in range(NC)]
                    for q in range(NQ)
                ],
            )

    halo1 = halo_start(1, t1)
    halo_wait(1, t1, halo1)

    @pl.loop(0, NZ)
    def _(z):
        centre, total = around(1, t1, z)
        weighted = [[None] * NC for _ in range(NQ)]
        for q in range(NQ):
            for c in range(NC):
                here = cond[z, q, c]
                last = (
                    centre[q][c]
                    + here * (total[q][c] - 6.0 * centre[q][c])
                    + hfld[z, q, c] * centre[q][c]
                )
                tst[c, z, pl.ds(q, 8, stride=NQ), :] = last
                adjoint = cntf[z, q, c] * last - obsf[z, q, c]
                adj2[z, q, c] = adjoint
                weighted[q][c] = here * adjoint
        put(2, w2, z, weighted)

    halo2 = halo_start(2, w2)
    stores = []
    for c in range(NC):
        copy = pltpu.make_async_copy(
            tst.at[c], tout_hbm.at[:, :, pl.ds(128 * c, 128)], out_sem.at[0, c]
        )
        copy.start()
        stores.append(copy)
    halo_wait(2, w2, halo2)

    @pl.loop(0, NZ)
    def _(z):
        centre, total = around(2, w2, z)
        rows = pl.ds(pl.multiple_of(z * 8, 8), 8)
        column = cell_ref[rows, :] & 511
        key = group * NC + (column >> 7)
        spot = column & 127
        picked = jnp.zeros((8, 128), F32)
        weighted = [[None] * NC for _ in range(NQ)]
        for q in range(NQ):
            for c in range(NC):
                later = adj2[z, q, c]
                adjoint = later + total[q][c] - 6.0 * centre[q][c] + hfld[z, q, c] * later
                adj1[z, q, c] = adjoint
                weighted[q][c] = cond[z, q, c] * adjoint
                product = later * t1[z + 1, q, c] + adjoint * t0[z + 1, q, c]
                picked = jnp.where(key == NC * q + c, lanes(product, spot), picked)
        sens[rows, :] = -0.3 * picked
        put(3, w1, z, weighted)

    halo3 = halo_start(3, w1)

    acc[...] = jnp.zeros((512, 256), F32)

    @pl.loop(0, NCHUNK)
    def _(i):
        value = sens[pl.ds(pl.multiple_of(i * PER, PER), PER), :]
        for r in range(PER):
            at = slice(128 * r, 128 * r + 128)
            right = bv[i, :, at] * value[r : r + 1, :]
            for a in range(16):
                high, low = split(right * bu[i, a : a + 1, at])
                wbuf[16 * a : 16 * a + 16, at] = high
                wbuf[256 + 16 * a : 272 + 16 * a, at] = low
        acc[...] += lax.dot_general(
            wbuf[...], onehot[i], (((1,), (1,)), ((), ())), preferred_element_type=F32
        )

    for c in range(2):
        for k in range(2):
            cols = slice(128 * k, 128 * k + 128)
            block = acc[128 * c : 128 * c + 128, cols] + acc[256 + 128 * c : 384 + 128 * c, cols]
            grad[pl.ds(2 * c + k, 128, stride=4), :] = block.T

    rs1 = []
    for k in range(1, n_slab):
        their = lax.rem(s + k, n_slab)
        copy = pltpu.make_async_remote_copy(
            grad.at[pl.ds(pl.multiple_of(their * (4 * n_patch), 4 * n_patch), 4 * n_patch)],
            part1.at[k],
            rs1_send.at[k],
            rs1_recv.at[k],
            on_slab(k),
            MESH,
        )
        copy.start()
        rs1.append(copy)

    halo_wait(3, w1, halo3)

    @pl.loop(0, NZ)
    def _(z):
        centre, total = around(3, w1, z)
        for q in range(NQ):
            for c in range(NC):
                later = adj1[z, q, c]
                ast[c, z, pl.ds(q, 8, stride=NQ), :] = (
                    later + total[q][c] - 6.0 * centre[q][c] + hfld[z, q, c] * later
                )

    for c in range(NC):
        copy = pltpu.make_async_copy(
            ast.at[c], aout_hbm.at[:, :, pl.ds(128 * c, 128)], out_sem.at[1, c]
        )
        copy.start()
        stores.append(copy)

    for copy in rs1:
        copy.wait()
    total = grad[mine, :]
    for k in range(1, n_slab):
        total = total + part1[k]
    part2_src[...] = total.reshape(n_patch, 4, 128)
    rs2 = []
    for k in range(1, n_patch):
        copy = pltpu.make_async_remote_copy(
            part2_src.at[lax.rem(t + k, n_patch)],
            part2.at[k],
            rs2_send.at[k],
            rs2_recv.at[k],
            on_patch(k),
            MESH,
        )
        copy.start()
        rs2.append(copy)
    for copy in rs2:
        copy.wait()
    total = part2_src[t]
    for k in range(1, n_patch):
        total = total + part2[k]
    gout_ref[:, 0:128] = total[0:2]
    gout_ref[:, 128:256] = total[2:4]
    for copy in stores:
        copy.wait()


def hand_out(a_in, b_in, c_in, a_out, b_out, c_out, sem):
    copies = [
        pltpu.make_async_copy(src.at[pl.ds(4 * k, 4)], dst.at[pl.ds(4 * k, 4)], sem.at[4 * n + k])
        for n, (src, dst) in enumerate(((a_in, a_out), (b_in, b_out)))
        for k in range(4)
    ]
    copies.append(pltpu.make_async_copy(c_in, c_out, sem.at[8]))
    for copy in copies:
        copy.start()
    for copy in copies:
        copy.wait()


def local(n_slab, n_patch, temp, cond, cell, pid, u, v, observed, points):
    field = (NZ,) + PLANE
    padded = (NZ + 2,) + PLANE
    natural = (NC, NZ, 32, 128)
    vmem = pltpu.VMEM
    dma = pltpu.SemaphoreType.DMA
    scratch = [
        vmem(natural, F32),
        vmem(natural, F32),
        vmem(natural, F32),
        vmem(natural, F32),
        vmem(padded, F32),
        vmem(padded, F32),
        vmem(padded, F32),
        vmem(padded, F32),
        vmem(field, F32),
        vmem(field, F32),
        vmem(field, F32),
        vmem(field, F32),
        vmem(field, F32),
        vmem(field, F32),
        vmem(field, F32),
        vmem(field, jnp.int32),
        vmem((5, ROWS, 128), jnp.int32),
        vmem((2, ROWS, 128), F32),
        vmem((4, 2, NZ * NC, 128), F32),
        vmem((4, 2, NZ * NC, 128), F32),
        vmem((4, 128), F32),
        vmem((n_patch, 4, 128), F32),
        vmem((4 * n_slab * n_patch, 128), F32),
        vmem((512, 256), BF16),
        vmem((NCHUNK, 256, CHUNK), BF16),
        vmem((NCHUNK, 16, CHUNK), F32),
        vmem((NCHUNK, 16, CHUNK), F32),
        vmem((512, CHUNK), BF16),
        vmem((ROWS, 128), F32),
        vmem((ROWS, 128), F32),
        vmem((512, 256), F32),
        vmem((4 * n_slab * n_patch, 128), F32),
        vmem((n_slab, 4 * n_patch, 128), F32),
        vmem((n_patch, 4, 128), F32),
        vmem((n_patch, 4, 128), F32),
        dma((2, NC)),
        dma((2, NC)),
        dma((n_patch,)),
        dma((n_patch,)),
        dma((n_slab,)),
        dma((n_slab,)),
        dma((n_slab,)),
        dma((n_slab,)),
        dma((n_patch,)),
        dma((n_patch,)),
        dma((4, 4)),
        dma((4, 4)),
    ]
    whole = pl.BlockSpec(memory_space=pltpu.VMEM)
    anywhere = pl.BlockSpec(memory_space=pl.ANY)
    rows = (ROWS, 128)
    final, adjoint, points_out = pl.pallas_call(
        functools.partial(kernel, n_slab, n_patch),
        out_shape=(
            jax.ShapeDtypeStruct(temp.shape, F32),
            jax.ShapeDtypeStruct(temp.shape, F32),
            jax.ShapeDtypeStruct(points.shape, F32),
        ),
        in_specs=[anywhere, anywhere] + [whole] * 6,
        out_specs=(anywhere, anywhere, whole),
        scratch_shapes=scratch,
        compiler_params=pltpu.CompilerParams(
            collective_id=0, has_side_effects=True, vmem_limit_bytes=56 * 1024 * 1024
        ),
        name="adjoint",
    )(
        temp,
        cond,
        cell.reshape(rows),
        pid.reshape(rows),
        u.reshape(rows),
        v.reshape(rows),
        observed.reshape(rows),
        points,
    )
    return pl.pallas_call(
        hand_out,
        out_shape=(
            jax.ShapeDtypeStruct(temp.shape, F32),
            jax.ShapeDtypeStruct(temp.shape, F32),
            jax.ShapeDtypeStruct(points.shape, F32),
        ),
        in_specs=[anywhere] * 3,
        out_specs=(anywhere,) * 3,
        scratch_shapes=[dma((9,))],
        name="hand_out",
    )(final, adjoint, points_out)


def solution(mesh):
    in_specs = (
        P("slab", "patch", None),
        P("slab", "patch", None),
        P(("slab", "patch")),
        P(("slab", "patch"), None),
        P(("slab", "patch")),
        P(("slab", "patch")),
        P(("slab", "patch")),
        P(("slab", "patch"), None),
    )
    out_specs = (P("slab", "patch", None), P("slab", "patch", None), P(("slab", "patch"), None))
    return jax.shard_map(
        functools.partial(local, mesh.shape["slab"], mesh.shape["patch"]),
        mesh=mesh,
        in_specs=in_specs,
        out_specs=out_specs,
        check_vma=False,
    )
```

```python
import functools

import jax
import jax.numpy as jnp
from jax import lax
from jax.experimental import pallas as pl
from jax.experimental.pallas import tpu as pltpu
from jax.sharding import PartitionSpec as P

MESH = pl.DeviceIdType.MESH
F32 = jnp.float32
BF16 = jnp.bfloat16
NZ = 16
NQ = 4
NC = 4
PLANE = (NQ, NC, 8, 128)
ROWS = 128
CHUNK = 1024
PER = CHUNK // 128
NCHUNK = ROWS * 128 // CHUNK


def iota(shape, dim):
    return lax.broadcasted_iota(jnp.int32, shape, dim)


def lanes(x, index):
    return jnp.take_along_axis(x, index, axis=1, mode="promise_in_bounds")


def basis_weights(param):
    y = jnp.abs((3.0 + 13.0 * param) - (iota((16, 128), 0) + 2).astype(F32))
    wide = jnp.maximum(2.0 - y, 0.0)
    narrow = jnp.maximum(1.0 - y, 0.0)
    return wide * wide * wide * (1.0 / 6.0) - narrow * narrow * narrow * (4.0 / 6.0)


def split(x):
    high = x.astype(BF16)
    return high, (x - high.astype(F32)).astype(BF16)


def kernel(
    n_slab,
    n_patch,
    temp_hbm,
    cond_hbm,
    cell_ref,
    pid_ref,
    u_ref,
    v_ref,
    obs_ref,
    cp_ref,
    tout_hbm,
    aout_hbm,
    gout_ref,
    tin,
    cin,
    tst,
    ast,
    t0,
    t1,
    w2,
    w1,
    cond,
    hfld,
    cntf,
    obsf,
    pre1,
    adj2,
    adj1,
    inv,
    chain,
    summed,
    ysend,
    yrecv,
    cp_src,
    cp_row,
    cp_all,
    lhs,
    onehot,
    bu,
    bv,
    wbuf,
    htc,
    sens,
    acc,
    grad,
    part1,
    part2_src,
    part2,
    in_sem,
    out_sem,
    ag1_send,
    ag1_recv,
    ag2_send,
    ag2_recv,
    rs1_send,
    rs1_recv,
    rs2_send,
    rs2_recv,
    halo_send,
    halo_recv,
):
    s = lax.axis_index("slab")
    t = lax.axis_index("patch")

    def on_slab(k):
        return (lax.rem(s + k, n_slab), t)

    def on_patch(k):
        return (s, lax.rem(t + k, n_patch))

    loads = []
    for a, (src, dst) in enumerate(((temp_hbm, tin), (cond_hbm, cin))):
        for c in range(NC):
            copy = pltpu.make_async_copy(
                src.at[:, :, pl.ds(128 * c, 128)], dst.at[c], in_sem.at[a, c]
            )
            copy.start()
            loads.append(copy)

    barrier = pltpu.get_barrier_semaphore()
    for k in range(1, n_slab):
        pl.semaphore_signal(barrier, inc=1, device_id=on_slab(k), device_id_type=MESH)
    for k in range(1, n_patch):
        pl.semaphore_signal(barrier, inc=1, device_id=on_patch(k), device_id_type=MESH)
    cp_src[0:2, :] = cp_ref[:, 0:128]
    cp_src[2:4, :] = cp_ref[:, 128:256]
    cp_row[t] = cp_src[...]
    pl.semaphore_wait(barrier, n_slab + n_patch - 2)

    ag1 = []
    for k in range(1, n_patch):
        copy = pltpu.make_async_remote_copy(
            cp_src, cp_row.at[t], ag1_send.at[k], ag1_recv.at[k], on_patch(k), MESH
        )
        copy.start()
        ag1.append(copy)

    def halo_copies(e, field):
        return [
            pltpu.make_async_remote_copy(
                field.at[NZ],
                field.at[0],
                halo_send.at[e, 0],
                halo_recv.at[e, 0],
                on_slab(1),
                MESH,
            ),
            pltpu.make_async_remote_copy(
                field.at[1],
                field.at[NZ + 1],
                halo_send.at[e, 1],
                halo_recv.at[e, 1],
                on_slab(n_slab - 1),
                MESH,
            ),
            pltpu.make_async_remote_copy(
                ysend.at[e, 1],
                yrecv.at[e, 0],
                halo_send.at[e, 2],
                halo_recv.at[e, 2],
                on_patch(1),
                MESH,
            ),
            pltpu.make_async_remote_copy(
                ysend.at[e, 0],
                yrecv.at[e, 1],
                halo_send.at[e, 3],
                halo_recv.at[e, 3],
                on_patch(n_patch - 1),
                MESH,
            ),
        ]

    def halo_start(e, field):
        copies = halo_copies(e, field)
        for copy in copies:
            copy.start()
        return copies

    def halo_wait(e, field, copies):
        for copy in copies:
            copy.wait()

        @pl.when(s == 0)
        def _():
            field[0] = jnp.zeros(PLANE, F32)

        @pl.when(s == n_slab - 1)
        def _():
            field[NZ + 1] = jnp.zeros(PLANE, F32)

        @pl.when(t == 0)
        def _():
            yrecv[e, 0] = jnp.zeros((NZ * NC, 128), F32)

        @pl.when(t == n_patch - 1)
        def _():
            yrecv[e, 1] = jnp.zeros((NZ * NC, 128), F32)

    def put(e, field, z, plane):
        for q in range(NQ):
            for c in range(NC):
                field[z + 1, q, c] = plane[q][c]
        for c in range(NC):
            ysend[e, 0, pl.ds(z * NC + c, 1), :] = plane[0][c][0:1, :]
            ysend[e, 1, pl.ds(z * NC + c, 1), :] = plane[NQ - 1][c][7:8, :]

    lane = iota((8, 128), 1)
    row8 = iota((8, 128), 0)

    def around(e, field, z):
        centre = [[field[z + 1, q, c] for c in range(NC)] for q in range(NQ)]
        total = [[None] * NC for _ in range(NQ)]
        for q in range(NQ):
            right = [pltpu.roll(centre[q][c], 127, 1) for c in range(NC)]
            left = [pltpu.roll(centre[q][c], 1, 1) for c in range(NC)]
            for c in range(NC):
                after = right[c + 1] if c + 1 < NC else 0.0
                before = left[c - 1] if c else 0.0
                x = jnp.where(lane == 127, after, right[c]) + jnp.where(
                    lane == 0, before, left[c]
                )
                if q + 1 < NQ:
                    y_up = centre[q + 1][c]
                else:
                    edge = yrecv[e, 1, pl.ds(z * NC + c, 1), :]
                    y_up = jnp.where(
                        row8 == 7, jnp.broadcast_to(edge, (8, 128)), pltpu.roll(centre[0][c], 7, 0)
                    )
                if q:
                    y_down = centre[q - 1][c]
                else:
                    edge = yrecv[e, 0, pl.ds(z * NC + c, 1), :]
                    y_down = jnp.where(
                        row8 == 0,
                        jnp.broadcast_to(edge, (8, 128)),
                        pltpu.roll(centre[NQ - 1][c], 1, 0),
                    )
                total[q][c] = (field[z, q, c] + field[z + 2, q, c]) + (y_up + y_down) + x
        return centre, total

    for copy in loads[:NC]:
        copy.wait()

    @pl.loop(0, NZ)
    def _(z):
        put(
            0,
            t0,
            z,
            [
                [tin[c, z, pl.ds(q, 8, stride=NQ), :] for c in range(NC)]
                for q in range(NQ)
            ],
        )

    halo0 = halo_start(0, t0)

    @pl.loop(0, NCHUNK)
    def _(i):
        rows = pl.ds(pl.multiple_of(i * PER, PER), PER)
        pid = pid_ref[rows, :]
        pid = ((pid & 1) * 128 + (pid >> 1)).astype(F32)
        uu = u_ref[rows, :]
        vv = v_ref[rows, :]
        places = iota((256, 128), 0).astype(F32).astype(BF16)
        for r in range(PER):
            at = slice(128 * r, 128 * r + 128)
            row = jnp.broadcast_to(pid[r : r + 1, :], (16, 128)).astype(BF16)
            for k in range(16):
                onehot[i, 16 * k : 16 * k + 16, at] = jnp.where(
                    places[16 * k : 16 * k + 16] == row, jnp.ones((), BF16), jnp.zeros((), BF16)
                )
            bu[i, :, at] = basis_weights(uu[r : r + 1, :])
            bv[i, :, at] = basis_weights(vv[r : r + 1, :])

    for copy in ag1:
        copy.wait()
    mine = pl.ds(pl.multiple_of(s * (4 * n_patch), 4 * n_patch), 4 * n_patch)
    cp_all[mine, :] = cp_row[...].reshape(4 * n_patch, 128)
    ag2 = []
    for k in range(1, n_slab):
        copy = pltpu.make_async_remote_copy(
            cp_all.at[mine], cp_all.at[mine], ag2_send.at[k], ag2_recv.at[k], on_slab(k), MESH
        )
        copy.start()
        ag2.append(copy)

    group = lane >> 5
    within = lane & 31
    for g in range(NZ):
        rows = slice(8 * g, 8 * g + 8)
        column = cell_ref[rows, :] & 511
        back = jnp.full((8, 128), -1, jnp.int32)
        for k in range(31, 0, -1):
            back = jnp.where(
                (pltpu.roll(column, k, 1) == column) & (within >= k), lane - k, back
            )
        chain[0, rows, :] = back
    for r in range(5):
        for g in range(NZ):
            rows = slice(8 * g, 8 * g + 8)
            back = chain[r, rows, :]
            index = back & 127
            count = jnp.ones((8, 128), F32) if r == 0 else summed[0, rows, :]
            seen = obs_ref[rows, :] if r == 0 else summed[1, rows, :]
            summed[0, rows, :] = count + jnp.where(back >= 0, lanes(count, index), 0.0)
            summed[1, rows, :] = seen + jnp.where(back >= 0, lanes(seen, index), 0.0)
            if r < 4:
                chain[r + 1, rows, :] = jnp.where(back >= 0, lanes(back, index), -1)

    def spread(z, values, dst):
        for q in range(NQ):
            src = jnp.where(group == q, values, 0.0)
            for c in range(NC):
                dst[z, q, c] = lanes(src, inv[z, q, c])

    lane16 = iota((16, 128), 1).astype(jnp.int16)

    @pl.loop(0, NZ // 2)
    def _(h):
        column = (cell_ref[pl.ds(pl.multiple_of(h * 16, 16), 16), :] & 511).astype(jnp.int16)
        for q in range(NQ):
            found = [jnp.full((16, 128), 32 * ((q + 1) % NQ), jnp.int16) for _ in range(NC)]
            for j in range(32):
                which = 32 * q + j
                off = jnp.broadcast_to(column[:, which : which + 1], (16, 128)) - lane16
                for c in range(NC):
                    found[c] = jnp.where(
                        off == jnp.int16(128 * c), jnp.int16(which), found[c]
                    )
            for c in range(NC):
                both = found[c].astype(jnp.int32)
                inv[2 * h, q, c] = both[0:8]
                inv[2 * h + 1, q, c] = both[8:16]
        for d in range(2):
            z = 2 * h + d
            rows = pl.ds(pl.multiple_of(z * 8, 8), 8)
            spread(z, summed[0, rows, :], cntf)
            spread(z, summed[1, rows, :], obsf)

    for copy in loads[NC:]:
        copy.wait()

    @pl.loop(0, NZ)
    def _(z):
        for q in range(NQ):
            for c in range(NC):
                cond[z, q, c] = cin[c, z, pl.ds(q, 8, stride=NQ), :]

    halo_wait(0, t0, halo0)

    @pl.loop(0, NZ)
    def _(z):
        centre, total = around(0, t0, z)
        for q in range(NQ):
            for c in range(NC):
                pre1[z, q, c] = centre[q][c] + cond[z, q, c] * (total[q][c] - 6.0 * centre[q][c])

    for copy in ag2:
        copy.wait()
    for c in range(2):
        for k in range(2):
            block = cp_all[pl.ds(2 * c + k, 128, stride=4), :].T
            high, low = split(block)
            lhs[128 * c : 128 * c + 128, 128 * k : 128 * k + 128] = high
            lhs[256 + 128 * c : 384 + 128 * c, 128 * k : 128 * k + 128] = low

    @pl.loop(0, NCHUNK)
    def _(i):
        for h in range(CHUNK // 256):
            at = slice(256 * h, 256 * h + 256)
            both = jnp.dot(lhs[...], onehot[i, :, at], preferred_element_type=F32)
            own = both[0:256] + both[256:512]
            total = own[0:16] * bu[i, 0:1, at]
            for a in range(1, 16):
                total = total + own[16 * a : 16 * a + 16] * bu[i, a : a + 1, at]
            value = -0.3 * jnp.sum(total * bv[i, :, at], axis=0, keepdims=True)
            for r in range(2):
                htc[pl.ds(i * PER + 2 * h + r, 1), :] = value[:, 128 * r : 128 * r + 128]

    for r in range(5):
        for g in range(NZ):
            rows = slice(8 * g, 8 * g + 8)
            back = chain[r, rows, :]
            value = htc[rows, :]
            htc[rows, :] = value + jnp.where(back >= 0, lanes(value, back & 127), 0.0)

    @pl.loop(0, NZ // 4)
    def _(h):
        for d in range(4):
            z = 4 * h + d
            spread(z, htc[pl.ds(pl.multiple_of(z * 8, 8), 8), :], hfld)
            put(
                1,
                t1,
                z,
                [
                    [pre1[z, q, c] + hfld[z, q, c] * t0[z + 1, q, c] for c in range(NC)]
                    for q in range(NQ)
                ],
            )

    halo1 = halo_start(1, t1)
    halo_wait(1, t1, halo1)

    @pl.loop(0, NZ)
    def _(z):
        centre, total = around(1, t1, z)
        weighted = [[None] * NC for _ in range(NQ)]
        for q in range(NQ):
            for c in range(NC):
                here = cond[z, q, c]
                last = (
                    centre[q][c]
                    + here * (total[q][c] - 6.0 * centre[q][c])
                    + hfld[z, q, c] * centre[q][c]
                )
                tst[c, z, pl.ds(q, 8, stride=NQ), :] = last
                adjoint = cntf[z, q, c] * last - obsf[z, q, c]
                adj2[z, q, c] = adjoint
                weighted[q][c] = here * adjoint
        put(2, w2, z, weighted)

    halo2 = halo_start(2, w2)
    stores = []
    for c in range(NC):
        copy = pltpu.make_async_copy(
            tst.at[c], tout_hbm.at[:, :, pl.ds(128 * c, 128)], out_sem.at[0, c]
        )
        copy.start()
        stores.append(copy)
    halo_wait(2, w2, halo2)

    @pl.loop(0, NZ)
    def _(z):
        centre, total = around(2, w2, z)
        rows = pl.ds(pl.multiple_of(z * 8, 8), 8)
        column = cell_ref[rows, :] & 511
        key = group * NC + (column >> 7)
        spot = column & 127
        picked = jnp.zeros((8, 128), F32)
        weighted = [[None] * NC for _ in range(NQ)]
        for q in range(NQ):
            for c in range(NC):
                later = adj2[z, q, c]
                adjoint = later + total[q][c] - 6.0 * centre[q][c] + hfld[z, q, c] * later
                adj1[z, q, c] = adjoint
                weighted[q][c] = cond[z, q, c] * adjoint
                product = later * t1[z + 1, q, c] + adjoint * t0[z + 1, q, c]
                picked = jnp.where(key == NC * q + c, lanes(product, spot), picked)
        sens[rows, :] = -0.3 * picked
        put(3, w1, z, weighted)

    halo3 = halo_start(3, w1)

    acc[...] = jnp.zeros((512, 256), F32)

    @pl.loop(0, NCHUNK)
    def _(i):
        value = sens[pl.ds(pl.multiple_of(i * PER, PER), PER), :]
        for r in range(PER):
            at = slice(128 * r, 128 * r + 128)
            right = bv[i, :, at] * value[r : r + 1, :]
            for a in range(16):
                high, low = split(right * bu[i, a : a + 1, at])
                wbuf[16 * a : 16 * a + 16, at] = high
                wbuf[256 + 16 * a : 272 + 16 * a, at] = low
        acc[...] += lax.dot_general(
            wbuf[...], onehot[i], (((1,), (1,)), ((), ())), preferred_element_type=F32
        )

    for c in range(2):
        for k in range(2):
            cols = slice(128 * k, 128 * k + 128)
            block = acc[128 * c : 128 * c + 128, cols] + acc[256 + 128 * c : 384 + 128 * c, cols]
            grad[pl.ds(2 * c + k, 128, stride=4), :] = block.T

    rs1 = []
    for k in range(1, n_slab):
        their = lax.rem(s + k, n_slab)
        copy = pltpu.make_async_remote_copy(
            grad.at[pl.ds(pl.multiple_of(their * (4 * n_patch), 4 * n_patch), 4 * n_patch)],
            part1.at[k],
            rs1_send.at[k],
            rs1_recv.at[k],
            on_slab(k),
            MESH,
        )
        copy.start()
        rs1.append(copy)

    halo_wait(3, w1, halo3)

    @pl.loop(0, NZ)
    def _(z):
        centre, total = around(3, w1, z)
        for q in range(NQ):
            for c in range(NC):
                later = adj1[z, q, c]
                ast[c, z, pl.ds(q, 8, stride=NQ), :] = (
                    later + total[q][c] - 6.0 * centre[q][c] + hfld[z, q, c] * later
                )

    for c in range(NC):
        copy = pltpu.make_async_copy(
            ast.at[c], aout_hbm.at[:, :, pl.ds(128 * c, 128)], out_sem.at[1, c]
        )
        copy.start()
        stores.append(copy)

    for copy in rs1:
        copy.wait()
    total = grad[mine, :]
    for k in range(1, n_slab):
        total = total + part1[k]
    part2_src[...] = total.reshape(n_patch, 4, 128)
    rs2 = []
    for k in range(1, n_patch):
        copy = pltpu.make_async_remote_copy(
            part2_src.at[lax.rem(t + k, n_patch)],
            part2.at[k],
            rs2_send.at[k],
            rs2_recv.at[k],
            on_patch(k),
            MESH,
        )
        copy.start()
        rs2.append(copy)
    for copy in rs2:
        copy.wait()
    total = part2_src[t]
    for k in range(1, n_patch):
        total = total + part2[k]
    gout_ref[:, 0:128] = total[0:2]
    gout_ref[:, 128:256] = total[2:4]
    for copy in stores:
        copy.wait()


def hand_out(a_in, b_in, c_in, a_out, b_out, c_out, held, small, in_sem, out_sem):
    pieces = []
    for n, (src, dst) in enumerate(((a_in, a_out), (b_in, b_out))):
        for k in range(4):
            part = pl.ds(4 * k, 4)
            pieces.append((src.at[part], held.at[n, part], dst.at[part]))
    pieces.append((c_in, small, c_out))
    loads = [
        pltpu.make_async_copy(src, mid, in_sem.at[k]) for k, (src, mid, _) in enumerate(pieces)
    ]
    stores = [
        pltpu.make_async_copy(mid, dst, out_sem.at[k]) for k, (_, mid, dst) in enumerate(pieces)
    ]
    for load in loads:
        load.start()
    for load, store in zip(loads, stores):
        load.wait()
        store.start()
    for store in stores:
        store.wait()


def local(n_slab, n_patch, temp, cond, cell, pid, u, v, observed, points):
    field = (NZ,) + PLANE
    padded = (NZ + 2,) + PLANE
    natural = (NC, NZ, 32, 128)
    vmem = pltpu.VMEM
    dma = pltpu.SemaphoreType.DMA
    scratch = [
        vmem(natural, F32),
        vmem(natural, F32),
        vmem(natural, F32),
        vmem(natural, F32),
        vmem(padded, F32),
        vmem(padded, F32),
        vmem(padded, F32),
        vmem(padded, F32),
        vmem(field, F32),
        vmem(field, F32),
        vmem(field, F32),
        vmem(field, F32),
        vmem(field, F32),
        vmem(field, F32),
        vmem(field, F32),
        vmem(field, jnp.int32),
        vmem((5, ROWS, 128), jnp.int32),
        vmem((2, ROWS, 128), F32),
        vmem((4, 2, NZ * NC, 128), F32),
        vmem((4, 2, NZ * NC, 128), F32),
        vmem((4, 128), F32),
        vmem((n_patch, 4, 128), F32),
        vmem((4 * n_slab * n_patch, 128), F32),
        vmem((512, 256), BF16),
        vmem((NCHUNK, 256, CHUNK), BF16),
        vmem((NCHUNK, 16, CHUNK), F32),
        vmem((NCHUNK, 16, CHUNK), F32),
        vmem((512, CHUNK), BF16),
        vmem((ROWS, 128), F32),
        vmem((ROWS, 128), F32),
        vmem((512, 256), F32),
        vmem((4 * n_slab * n_patch, 128), F32),
        vmem((n_slab, 4 * n_patch, 128), F32),
        vmem((n_patch, 4, 128), F32),
        vmem((n_patch, 4, 128), F32),
        dma((2, NC)),
        dma((2, NC)),
        dma((n_patch,)),
        dma((n_patch,)),
        dma((n_slab,)),
        dma((n_slab,)),
        dma((n_slab,)),
        dma((n_slab,)),
        dma((n_patch,)),
        dma((n_patch,)),
        dma((4, 4)),
        dma((4, 4)),
    ]
    whole = pl.BlockSpec(memory_space=pltpu.VMEM)
    anywhere = pl.BlockSpec(memory_space=pl.ANY)
    rows = (ROWS, 128)
    final, adjoint, points_out = pl.pallas_call(
        functools.partial(kernel, n_slab, n_patch),
        out_shape=(
            jax.ShapeDtypeStruct(temp.shape, F32),
            jax.ShapeDtypeStruct(temp.shape, F32),
            jax.ShapeDtypeStruct(points.shape, F32),
        ),
        in_specs=[anywhere, anywhere] + [whole] * 6,
        out_specs=(anywhere, anywhere, whole),
        scratch_shapes=scratch,
        compiler_params=pltpu.CompilerParams(
            collective_id=0, has_side_effects=True, vmem_limit_bytes=56 * 1024 * 1024
        ),
        name="adjoint",
    )(
        temp,
        cond,
        cell.reshape(rows),
        pid.reshape(rows),
        u.reshape(rows),
        v.reshape(rows),
        observed.reshape(rows),
        points,
    )
    return pl.pallas_call(
        hand_out,
        out_shape=(
            jax.ShapeDtypeStruct(temp.shape, F32),
            jax.ShapeDtypeStruct(temp.shape, F32),
            jax.ShapeDtypeStruct(points.shape, F32),
        ),
        in_specs=[anywhere] * 3,
        out_specs=(anywhere,) * 3,
        scratch_shapes=[
            vmem((2,) + temp.shape, F32),
            vmem(points.shape, F32),
            dma((9,)),
            dma((9,)),
        ],
        name="hand_out",
    )(final, adjoint, points_out)


def solution(mesh):
    in_specs = (
        P("slab", "patch", None),
        P("slab", "patch", None),
        P(("slab", "patch")),
        P(("slab", "patch"), None),
        P(("slab", "patch")),
        P(("slab", "patch")),
        P(("slab", "patch")),
        P(("slab", "patch"), None),
    )
    out_specs = (P("slab", "patch", None), P("slab", "patch", None), P(("slab", "patch"), None))
    return jax.shard_map(
        functools.partial(local, mesh.shape["slab"], mesh.shape["patch"]),
        mesh=mesh,
        in_specs=in_specs,
        out_specs=out_specs,
        check_vma=False,
    )
```

```python
import functools

import jax
import jax.numpy as jnp
from jax import lax
from jax.experimental import pallas as pl
from jax.experimental.pallas import tpu as pltpu
from jax.sharding import PartitionSpec as P

MESH = pl.DeviceIdType.MESH
F32 = jnp.float32
BF16 = jnp.bfloat16
NZ = 16
NQ = 4
NC = 4
PLANE = (NQ, NC, 8, 128)
ROWS = 128
CHUNK = 1024
PER = CHUNK // 128
NCHUNK = ROWS * 128 // CHUNK


def iota(shape, dim):
    return lax.broadcasted_iota(jnp.int32, shape, dim)


def lanes(x, index):
    return jnp.take_along_axis(x, index, axis=1, mode="promise_in_bounds")


def basis_weights(param):
    y = jnp.abs((3.0 + 13.0 * param) - (iota((16, 128), 0) + 2).astype(F32))
    wide = jnp.maximum(2.0 - y, 0.0)
    narrow = jnp.maximum(1.0 - y, 0.0)
    return wide * wide * wide * (1.0 / 6.0) - narrow * narrow * narrow * (4.0 / 6.0)


def split(x):
    high = x.astype(BF16)
    return high, (x - high.astype(F32)).astype(BF16)


def kernel(
    n_slab,
    n_patch,
    temp_hbm,
    cond_hbm,
    cell_ref,
    pid_ref,
    u_ref,
    v_ref,
    obs_ref,
    cp_ref,
    tout_hbm,
    aout_hbm,
    gout_ref,
    tin,
    cin,
    tst,
    ast,
    t0,
    t1,
    w2,
    w1,
    cond,
    hfld,
    cntf,
    obsf,
    pre1,
    adj2,
    adj1,
    inv,
    chain,
    summed,
    ysend,
    yrecv,
    cp_src,
    cp_row,
    cp_all,
    lhs,
    onehot,
    bu,
    bv,
    wbuf,
    htc,
    sens,
    acc,
    grad,
    part1,
    part2_src,
    part2,
    in_sem,
    out_sem,
    ag1_send,
    ag1_recv,
    ag2_send,
    ag2_recv,
    rs1_send,
    rs1_recv,
    rs2_send,
    rs2_recv,
    halo_send,
    halo_recv,
):
    s = lax.axis_index("slab")
    t = lax.axis_index("patch")

    def on_slab(k):
        return (lax.rem(s + k, n_slab), t)

    def on_patch(k):
        return (s, lax.rem(t + k, n_patch))

    loads = []
    for a, (src, dst) in enumerate(((temp_hbm, tin), (cond_hbm, cin))):
        for c in range(NC):
            copy = pltpu.make_async_copy(
                src.at[:, :, pl.ds(128 * c, 128)], dst.at[c], in_sem.at[a, c]
            )
            copy.start()
            loads.append(copy)

    barrier = pltpu.get_barrier_semaphore()
    for k in range(1, n_slab):
        pl.semaphore_signal(barrier, inc=1, device_id=on_slab(k), device_id_type=MESH)
    for k in range(1, n_patch):
        pl.semaphore_signal(barrier, inc=1, device_id=on_patch(k), device_id_type=MESH)
    cp_src[0:2, :] = cp_ref[:, 0:128]
    cp_src[2:4, :] = cp_ref[:, 128:256]
    cp_row[t] = cp_src[...]
    pl.semaphore_wait(barrier, n_slab + n_patch - 2)

    ag1 = []
    for k in range(1, n_patch):
        copy = pltpu.make_async_remote_copy(
            cp_src, cp_row.at[t], ag1_send.at[k], ag1_recv.at[k], on_patch(k), MESH
        )
        copy.start()
        ag1.append(copy)

    def along(e, field, up):
        return pltpu.make_async_remote_copy(
            field.at[NZ if up else 1],
            field.at[0 if up else NZ + 1],
            halo_send.at[e, 8 + up],
            halo_recv.at[e, 8 + up],
            on_slab(1 if up else n_slab - 1),
            MESH,
        )

    def across(e, up, g):
        rows = pl.ds(0, NZ * NC) if g < 0 else pl.ds(16 * g, 16)
        slot = max(g, 0) * 2 + up
        return pltpu.make_async_remote_copy(
            ysend.at[e, up, rows],
            yrecv.at[e, 1 - up, rows],
            halo_send.at[e, slot],
            halo_recv.at[e, slot],
            on_patch(1 if up else n_patch - 1),
            MESH,
        )

    def along_wait(e, field, up):
        along(e, field, up).wait()

        @pl.when(s == (0 if up else n_slab - 1))
        def _():
            field[0 if up else NZ + 1] = jnp.zeros(PLANE, F32)

    def across_start(e, g):
        across(e, 1, g).start()
        across(e, 0, g).start()

    def across_wait(e, g):
        across(e, 1, g).wait()
        across(e, 0, g).wait()
        first, size = (0, NZ * NC) if g < 0 else (16 * g, 16)

        @pl.when(t == 0)
        def _():
            yrecv[e, 0, first : first + size, :] = jnp.zeros((size, 128), F32)

        @pl.when(t == n_patch - 1)
        def _():
            yrecv[e, 1, first : first + size, :] = jnp.zeros((size, 128), F32)

    def halo_start(e, field):
        along(e, field, 1).start()
        along(e, field, 0).start()
        across_start(e, -1)

    def halo_wait(e, field):
        along_wait(e, field, 1)
        along_wait(e, field, 0)
        across_wait(e, -1)

    def put(e, field, z, plane):
        for q in range(NQ):
            for c in range(NC):
                field[z + 1, q, c] = plane[q][c]
        for c in range(NC):
            ysend[e, 0, pl.ds(z * NC + c, 1), :] = plane[0][c][0:1, :]
            ysend[e, 1, pl.ds(z * NC + c, 1), :] = plane[NQ - 1][c][7:8, :]

    lane = iota((8, 128), 1)
    row8 = iota((8, 128), 0)

    def around(e, field, z):
        centre = [[field[z + 1, q, c] for c in range(NC)] for q in range(NQ)]
        total = [[None] * NC for _ in range(NQ)]
        for q in range(NQ):
            right = [pltpu.roll(centre[q][c], 127, 1) for c in range(NC)]
            left = [pltpu.roll(centre[q][c], 1, 1) for c in range(NC)]
            for c in range(NC):
                after = right[c + 1] if c + 1 < NC else 0.0
                before = left[c - 1] if c else 0.0
                x = jnp.where(lane == 127, after, right[c]) + jnp.where(
                    lane == 0, before, left[c]
                )
                if q + 1 < NQ:
                    y_up = centre[q + 1][c]
                else:
                    edge = yrecv[e, 1, pl.ds(z * NC + c, 1), :]
                    y_up = jnp.where(
                        row8 == 7, jnp.broadcast_to(edge, (8, 128)), pltpu.roll(centre[0][c], 7, 0)
                    )
                if q:
                    y_down = centre[q - 1][c]
                else:
                    edge = yrecv[e, 0, pl.ds(z * NC + c, 1), :]
                    y_down = jnp.where(
                        row8 == 0,
                        jnp.broadcast_to(edge, (8, 128)),
                        pltpu.roll(centre[NQ - 1][c], 1, 0),
                    )
                total[q][c] = (field[z, q, c] + field[z + 2, q, c]) + (y_up + y_down) + x
        return centre, total

    for copy in loads[:NC]:
        copy.wait()

    @pl.loop(0, NZ)
    def _(z):
        put(
            0,
            t0,
            z,
            [
                [tin[c, z, pl.ds(q, 8, stride=NQ), :] for c in range(NC)]
                for q in range(NQ)
            ],
        )

    halo_start(0, t0)

    @pl.loop(0, NCHUNK)
    def _(i):
        rows = pl.ds(pl.multiple_of(i * PER, PER), PER)
        pid = pid_ref[rows, :]
        pid = ((pid & 1) * 128 + (pid >> 1)).astype(F32)
        uu = u_ref[rows, :]
        vv = v_ref[rows, :]
        places = iota((256, 128), 0).astype(F32).astype(BF16)
        for r in range(PER):
            at = slice(128 * r, 128 * r + 128)
            row = jnp.broadcast_to(pid[r : r + 1, :], (16, 128)).astype(BF16)
            for k in range(16):
                onehot[i, 16 * k : 16 * k + 16, at] = jnp.where(
                    places[16 * k : 16 * k + 16] == row, jnp.ones((), BF16), jnp.zeros((), BF16)
                )
            bu[i, :, at] = basis_weights(uu[r : r + 1, :])
            bv[i, :, at] = basis_weights(vv[r : r + 1, :])

    for copy in ag1:
        copy.wait()
    mine = pl.ds(pl.multiple_of(s * (4 * n_patch), 4 * n_patch), 4 * n_patch)
    cp_all[mine, :] = cp_row[...].reshape(4 * n_patch, 128)
    ag2 = []
    for k in range(1, n_slab):
        copy = pltpu.make_async_remote_copy(
            cp_all.at[mine], cp_all.at[mine], ag2_send.at[k], ag2_recv.at[k], on_slab(k), MESH
        )
        copy.start()
        ag2.append(copy)

    group = lane >> 5
    within = lane & 31
    for g in range(NZ):
        rows = slice(8 * g, 8 * g + 8)
        column = cell_ref[rows, :] & 511
        back = jnp.full((8, 128), -1, jnp.int32)
        for k in range(31, 0, -1):
            back = jnp.where(
                (pltpu.roll(column, k, 1) == column) & (within >= k), lane - k, back
            )
        chain[0, rows, :] = back
    for r in range(5):
        for g in range(NZ):
            rows = slice(8 * g, 8 * g + 8)
            back = chain[r, rows, :]
            index = back & 127
            count = jnp.ones((8, 128), F32) if r == 0 else summed[0, rows, :]
            seen = obs_ref[rows, :] if r == 0 else summed[1, rows, :]
            summed[0, rows, :] = count + jnp.where(back >= 0, lanes(count, index), 0.0)
            summed[1, rows, :] = seen + jnp.where(back >= 0, lanes(seen, index), 0.0)
            if r < 4:
                chain[r + 1, rows, :] = jnp.where(back >= 0, lanes(back, index), -1)

    def spread(z, values, dst):
        for q in range(NQ):
            src = jnp.where(group == q, values, 0.0)
            for c in range(NC):
                dst[z, q, c] = lanes(src, inv[z, q, c])

    lane16 = iota((16, 128), 1).astype(jnp.int16)

    @pl.loop(0, NZ // 2)
    def _(h):
        column = (cell_ref[pl.ds(pl.multiple_of(h * 16, 16), 16), :] & 511).astype(jnp.int16)
        for q in range(NQ):
            found = [jnp.full((16, 128), 32 * ((q + 1) % NQ), jnp.int16) for _ in range(NC)]
            for j in range(32):
                which = 32 * q + j
                off = jnp.broadcast_to(column[:, which : which + 1], (16, 128)) - lane16
                for c in range(NC):
                    found[c] = jnp.where(
                        off == jnp.int16(128 * c), jnp.int16(which), found[c]
                    )
            for c in range(NC):
                both = found[c].astype(jnp.int32)
                inv[2 * h, q, c] = both[0:8]
                inv[2 * h + 1, q, c] = both[8:16]
        for d in range(2):
            z = 2 * h + d
            rows = pl.ds(pl.multiple_of(z * 8, 8), 8)
            spread(z, summed[0, rows, :], cntf)
            spread(z, summed[1, rows, :], obsf)

    for copy in loads[NC:]:
        copy.wait()

    @pl.loop(0, NZ)
    def _(z):
        for q in range(NQ):
            for c in range(NC):
                cond[z, q, c] = cin[c, z, pl.ds(q, 8, stride=NQ), :]

    halo_wait(0, t0)

    @pl.loop(0, NZ)
    def _(z):
        centre, total = around(0, t0, z)
        for q in range(NQ):
            for c in range(NC):
                pre1[z, q, c] = centre[q][c] + cond[z, q, c] * (total[q][c] - 6.0 * centre[q][c])

    for copy in ag2:
        copy.wait()
    for c in range(2):
        for k in range(2):
            block = cp_all[pl.ds(2 * c + k, 128, stride=4), :].T
            high, low = split(block)
            lhs[128 * c : 128 * c + 128, 128 * k : 128 * k + 128] = high
            lhs[256 + 128 * c : 384 + 128 * c, 128 * k : 128 * k + 128] = low

    def face_rows(z):
        return pl.ds(pl.multiple_of(z * 8, 8), 8)

    def coefficients(z):
        for h in range(CHUNK // 256):
            at = slice(256 * h, 256 * h + 256)
            both = jnp.dot(lhs[...], onehot[z, :, at], preferred_element_type=F32)
            own = both[0:256] + both[256:512]
            total = own[0:16] * bu[z, 0:1, at]
            for a in range(1, 16):
                total = total + own[16 * a : 16 * a + 16] * bu[z, a : a + 1, at]
            value = -0.3 * jnp.sum(total * bv[z, :, at], axis=0, keepdims=True)
            for r in range(2):
                htc[pl.ds(z * PER + 2 * h + r, 1), :] = value[:, 128 * r : 128 * r + 128]

    def first_step(z):
        value = htc[face_rows(z), :]
        for r in range(5):
            back = chain[r, face_rows(z), :]
            value = value + jnp.where(back >= 0, lanes(value, back & 127), 0.0)
        plane = [[None] * NC for _ in range(NQ)]
        for q in range(NQ):
            src = jnp.where(group == q, value, 0.0)
            for c in range(NC):
                here = lanes(src, inv[z, q, c])
                hfld[z, q, c] = here
                plane[q][c] = pre1[z, q, c] + here * t0[z + 1, q, c]
        put(1, t1, z, plane)

    def second_step(z):
        centre, total = around(1, t1, z)
        weighted = [[None] * NC for _ in range(NQ)]
        for q in range(NQ):
            for c in range(NC):
                here = cond[z, q, c]
                last = (
                    centre[q][c]
                    + here * (total[q][c] - 6.0 * centre[q][c])
                    + hfld[z, q, c] * centre[q][c]
                )
                tst[c, z, pl.ds(q, 8, stride=NQ), :] = last
                adjoint = cntf[z, q, c] * last - obsf[z, q, c]
                adj2[z, q, c] = adjoint
                weighted[q][c] = here * adjoint
        put(2, w2, z, weighted)

    def first_back(z):
        centre, total = around(2, w2, z)
        column = cell_ref[face_rows(z), :] & 511
        key = group * NC + (column >> 7)
        spot = column & 127
        picked = jnp.zeros((8, 128), F32)
        weighted = [[None] * NC for _ in range(NQ)]
        for q in range(NQ):
            for c in range(NC):
                later = adj2[z, q, c]
                adjoint = later + total[q][c] - 6.0 * centre[q][c] + hfld[z, q, c] * later
                adj1[z, q, c] = adjoint
                weighted[q][c] = cond[z, q, c] * adjoint
                product = later * t1[z + 1, q, c] + adjoint * t0[z + 1, q, c]
                picked = jnp.where(key == NC * q + c, lanes(product, spot), picked)
        sens[face_rows(z), :] = -0.3 * picked
        put(3, w1, z, weighted)

    def gradient(z):
        value = sens[face_rows(z), :]
        for r in range(PER):
            at = slice(128 * r, 128 * r + 128)
            right = bv[z, :, at] * value[r : r + 1, :]
            for a in range(16):
                high, low = split(right * bu[z, a : a + 1, at])
                wbuf[16 * a : 16 * a + 16, at] = high
                wbuf[256 + 16 * a : 272 + 16 * a, at] = low
        acc[...] += lax.dot_general(
            wbuf[...], onehot[z], (((1,), (1,)), ((), ())), preferred_element_type=F32
        )

    coefficients(NZ - 1)

    @pl.loop(0, 5)
    def _(k):
        first_step(lax.rem(k + NZ - 1, NZ))
        coefficients(k)

    along(1, t1, 1).start()
    along(1, t1, 0).start()
    across_start(1, 0)

    @pl.loop(5, 9)
    def _(k):
        first_step(k - 1)
        coefficients(k)

    across_start(1, 1)
    along_wait(1, t1, 1)
    across_wait(1, 0)

    @pl.loop(9, 13)
    def _(k):
        second_step(k - 9)
        first_step(k - 1)
        coefficients(k)

    across_start(1, 2)
    along(2, w2, 0).start()
    across_start(2, 0)
    across_wait(1, 1)

    @pl.loop(13, 15)
    def _(k):
        second_step(2 * k - 22)
        second_step(2 * k - 21)
        first_step(k - 1)
        coefficients(k)

    first_step(NZ - 2)
    across_start(1, 3)
    across_start(2, 1)

    acc[...] = jnp.zeros((512, 256), F32)
    across_wait(2, 0)
    first_back(1)
    across_wait(1, 2)

    @pl.loop(1, 3)
    def _(j):
        gradient(j)
        first_back(j + 1)
        second_step(2 * j + 6)
        second_step(2 * j + 7)

    across_start(2, 2)
    along_wait(1, t1, 0)
    across_wait(1, 3)
    across_wait(2, 1)

    @pl.loop(3, 7)
    def _(j):
        gradient(j)
        first_back(j + 1)
        second_step(j + 9)

    along(2, w2, 1).start()
    across_start(2, 3)
    stores = []
    for c in range(NC):
        copy = pltpu.make_async_copy(
            tst.at[c], tout_hbm.at[:, :, pl.ds(128 * c, 128)], out_sem.at[0, c]
        )
        copy.start()
        stores.append(copy)
    across_wait(2, 2)

    @pl.loop(7, 11)
    def _(j):
        gradient(j)
        first_back(j + 1)

    along_wait(2, w2, 0)
    across_wait(2, 3)

    @pl.loop(11, 15)
    def _(j):
        gradient(j)
        first_back(j + 1)

    along_wait(2, w2, 1)
    gradient(NZ - 1)
    first_back(0)
    halo_start(3, w1)
    gradient(0)

    for c in range(2):
        for k in range(2):
            cols = slice(128 * k, 128 * k + 128)
            block = acc[128 * c : 128 * c + 128, cols] + acc[256 + 128 * c : 384 + 128 * c, cols]
            grad[pl.ds(2 * c + k, 128, stride=4), :] = block.T

    rs1 = []
    for k in range(1, n_slab):
        their = lax.rem(s + k, n_slab)
        copy = pltpu.make_async_remote_copy(
            grad.at[pl.ds(pl.multiple_of(their * (4 * n_patch), 4 * n_patch), 4 * n_patch)],
            part1.at[k],
            rs1_send.at[k],
            rs1_recv.at[k],
            on_slab(k),
            MESH,
        )
        copy.start()
        rs1.append(copy)

    halo_wait(3, w1)

    @pl.loop(0, NZ)
    def _(z):
        centre, total = around(3, w1, z)
        for q in range(NQ):
            for c in range(NC):
                later = adj1[z, q, c]
                ast[c, z, pl.ds(q, 8, stride=NQ), :] = (
                    later + total[q][c] - 6.0 * centre[q][c] + hfld[z, q, c] * later
                )

    for c in range(NC):
        copy = pltpu.make_async_copy(
            ast.at[c], aout_hbm.at[:, :, pl.ds(128 * c, 128)], out_sem.at[1, c]
        )
        copy.start()
        stores.append(copy)

    for copy in rs1:
        copy.wait()
    total = grad[mine, :]
    for k in range(1, n_slab):
        total = total + part1[k]
    part2_src[...] = total.reshape(n_patch, 4, 128)
    rs2 = []
    for k in range(1, n_patch):
        copy = pltpu.make_async_remote_copy(
            part2_src.at[lax.rem(t + k, n_patch)],
            part2.at[k],
            rs2_send.at[k],
            rs2_recv.at[k],
            on_patch(k),
            MESH,
        )
        copy.start()
        rs2.append(copy)
    for copy in rs2:
        copy.wait()
    total = part2_src[t]
    for k in range(1, n_patch):
        total = total + part2[k]
    gout_ref[:, 0:128] = total[0:2]
    gout_ref[:, 128:256] = total[2:4]
    for copy in stores:
        copy.wait()


def hand_out(a_in, b_in, c_in, a_out, b_out, c_out, held, small, in_sem, out_sem):
    pieces = []
    for n, (src, dst) in enumerate(((a_in, a_out), (b_in, b_out))):
        for k in range(4):
            part = pl.ds(4 * k, 4)
            pieces.append((src.at[part], held.at[n, part], dst.at[part]))
    pieces.append((c_in, small, c_out))
    loads = [
        pltpu.make_async_copy(src, mid, in_sem.at[k]) for k, (src, mid, _) in enumerate(pieces)
    ]
    stores = [
        pltpu.make_async_copy(mid, dst, out_sem.at[k]) for k, (_, mid, dst) in enumerate(pieces)
    ]
    for load in loads:
        load.start()
    for load, store in zip(loads, stores):
        load.wait()
        store.start()
    for store in stores:
        store.wait()


def local(n_slab, n_patch, temp, cond, cell, pid, u, v, observed, points):
    field = (NZ,) + PLANE
    padded = (NZ + 2,) + PLANE
    natural = (NC, NZ, 32, 128)
    vmem = pltpu.VMEM
    dma = pltpu.SemaphoreType.DMA
    scratch = [
        vmem(natural, F32),
        vmem(natural, F32),
        vmem(natural, F32),
        vmem(natural, F32),
        vmem(padded, F32),
        vmem(padded, F32),
        vmem(padded, F32),
        vmem(padded, F32),
        vmem(field, F32),
        vmem(field, F32),
        vmem(field, F32),
        vmem(field, F32),
        vmem(field, F32),
        vmem(field, F32),
        vmem(field, F32),
        vmem(field, jnp.int32),
        vmem((5, ROWS, 128), jnp.int32),
        vmem((2, ROWS, 128), F32),
        vmem((4, 2, NZ * NC, 128), F32),
        vmem((4, 2, NZ * NC, 128), F32),
        vmem((4, 128), F32),
        vmem((n_patch, 4, 128), F32),
        vmem((4 * n_slab * n_patch, 128), F32),
        vmem((512, 256), BF16),
        vmem((NCHUNK, 256, CHUNK), BF16),
        vmem((NCHUNK, 16, CHUNK), F32),
        vmem((NCHUNK, 16, CHUNK), F32),
        vmem((512, CHUNK), BF16),
        vmem((ROWS, 128), F32),
        vmem((ROWS, 128), F32),
        vmem((512, 256), F32),
        vmem((4 * n_slab * n_patch, 128), F32),
        vmem((n_slab, 4 * n_patch, 128), F32),
        vmem((n_patch, 4, 128), F32),
        vmem((n_patch, 4, 128), F32),
        dma((2, NC)),
        dma((2, NC)),
        dma((n_patch,)),
        dma((n_patch,)),
        dma((n_slab,)),
        dma((n_slab,)),
        dma((n_slab,)),
        dma((n_slab,)),
        dma((n_patch,)),
        dma((n_patch,)),
        dma((4, 10)),
        dma((4, 10)),
    ]
    whole = pl.BlockSpec(memory_space=pltpu.VMEM)
    anywhere = pl.BlockSpec(memory_space=pl.ANY)
    rows = (ROWS, 128)
    final, adjoint, points_out = pl.pallas_call(
        functools.partial(kernel, n_slab, n_patch),
        out_shape=(
            jax.ShapeDtypeStruct(temp.shape, F32),
            jax.ShapeDtypeStruct(temp.shape, F32),
            jax.ShapeDtypeStruct(points.shape, F32),
        ),
        in_specs=[anywhere, anywhere] + [whole] * 6,
        out_specs=(anywhere, anywhere, whole),
        scratch_shapes=scratch,
        compiler_params=pltpu.CompilerParams(
            collective_id=0, has_side_effects=True, vmem_limit_bytes=56 * 1024 * 1024
        ),
        name="adjoint",
    )(
        temp,
        cond,
        cell.reshape(rows),
        pid.reshape(rows),
        u.reshape(rows),
        v.reshape(rows),
        observed.reshape(rows),
        points,
    )
    return pl.pallas_call(
        hand_out,
        out_shape=(
            jax.ShapeDtypeStruct(temp.shape, F32),
            jax.ShapeDtypeStruct(temp.shape, F32),
            jax.ShapeDtypeStruct(points.shape, F32),
        ),
        in_specs=[anywhere] * 3,
        out_specs=(anywhere,) * 3,
        scratch_shapes=[
            vmem((2,) + temp.shape, F32),
            vmem(points.shape, F32),
            dma((9,)),
            dma((9,)),
        ],
        name="hand_out",
    )(final, adjoint, points_out)


def solution(mesh):
    in_specs = (
        P("slab", "patch", None),
        P("slab", "patch", None),
        P(("slab", "patch")),
        P(("slab", "patch"), None),
        P(("slab", "patch")),
        P(("slab", "patch")),
        P(("slab", "patch")),
        P(("slab", "patch"), None),
    )
    out_specs = (P("slab", "patch", None), P("slab", "patch", None), P(("slab", "patch"), None))
    return jax.shard_map(
        functools.partial(local, mesh.shape["slab"], mesh.shape["patch"]),
        mesh=mesh,
        in_specs=in_specs,
        out_specs=out_specs,
        check_vma=False,
    )
```

```python
import functools

import jax
import jax.numpy as jnp
from jax import lax
from jax.experimental import pallas as pl
from jax.experimental.pallas import tpu as pltpu
from jax.sharding import PartitionSpec as P

MESH = pl.DeviceIdType.MESH
F32 = jnp.float32
BF16 = jnp.bfloat16
NZ = 16
NQ = 4
NC = 4
PLANE = (NQ, NC, 8, 128)
ROWS = 128
CHUNK = 1024
PER = CHUNK // 128
NCHUNK = ROWS * 128 // CHUNK


def iota(shape, dim):
    return lax.broadcasted_iota(jnp.int32, shape, dim)


def lanes(x, index):
    return jnp.take_along_axis(x, index, axis=1, mode="promise_in_bounds")


def basis_weights(param):
    y = jnp.abs((3.0 + 13.0 * param) - (iota((16, 128), 0) + 2).astype(F32))
    wide = jnp.maximum(2.0 - y, 0.0)
    narrow = jnp.maximum(1.0 - y, 0.0)
    return wide * wide * wide * (1.0 / 6.0) - narrow * narrow * narrow * (4.0 / 6.0)


def split(x):
    high = x.astype(BF16)
    return high, (x - high.astype(F32)).astype(BF16)


def kernel(
    n_slab,
    n_patch,
    temp_hbm,
    cond_hbm,
    cell_hbm,
    pid_hbm,
    u_hbm,
    v_hbm,
    obs_hbm,
    cp_hbm,
    tst,
    ast,
    gout_ref,
    tin,
    cin,
    cell_ref,
    pid_ref,
    u_ref,
    v_ref,
    obs_ref,
    cp_ref,
    t0,
    t1,
    w2,
    w1,
    cond,
    hfld,
    cntf,
    obsf,
    adj2,
    adj1,
    inv,
    chain,
    summed,
    ysend,
    yrecv,
    cp_src,
    cp_row,
    cp_all,
    lhs,
    onehot,
    bu,
    bv,
    wbuf,
    htc,
    sens,
    acc,
    grad,
    part1,
    part2_src,
    part2,
    in_sem,
    ag1_send,
    ag1_recv,
    ag2_send,
    ag2_recv,
    rs1_send,
    rs1_recv,
    rs2_send,
    rs2_recv,
    halo_send,
    halo_recv,
):
    s = lax.axis_index("slab")
    t = lax.axis_index("patch")

    def on_slab(k):
        return (lax.rem(s + k, n_slab), t)

    def on_patch(k):
        return (s, lax.rem(t + k, n_patch))

    load_cp = pltpu.make_async_copy(cp_hbm, cp_ref, in_sem.at[2 * NC + 5])
    load_cp.start()
    barrier = pltpu.get_barrier_semaphore()
    for k in range(1, n_patch):
        pl.semaphore_signal(barrier, inc=1, device_id=on_patch(k), device_id_type=MESH)
    for k in range(1, n_slab):
        pl.semaphore_signal(barrier, inc=1, device_id=on_slab(k), device_id_type=MESH)
    loads = []
    for a, (src, dst) in enumerate(((temp_hbm, tin), (cond_hbm, cin))):
        for c in range(NC):
            loads.append(
                pltpu.make_async_copy(
                    src.at[:, :, pl.ds(128 * c, 128)], dst.at[c], in_sem.at[NC * a + c]
                )
            )
    small = ((pid_hbm, pid_ref), (u_hbm, u_ref), (v_hbm, v_ref), (cell_hbm, cell_ref), (obs_hbm, obs_ref))
    for k, (src, dst) in enumerate(small):
        loads.append(pltpu.make_async_copy(src, dst, in_sem.at[2 * NC + k]))
    for copy in loads[:NC] + loads[2 * NC :] + loads[NC : 2 * NC]:
        copy.start()
    load_cp.wait()
    cp_src[0:2, :] = cp_ref[:, 0:128]
    cp_src[2:4, :] = cp_ref[:, 128:256]
    cp_row[t] = cp_src[...]
    pl.semaphore_wait(barrier, n_slab + n_patch - 2)

    ag1 = []
    for k in range(1, n_patch):
        copy = pltpu.make_async_remote_copy(
            cp_src, cp_row.at[t], ag1_send.at[k], ag1_recv.at[k], on_patch(k), MESH
        )
        copy.start()
        ag1.append(copy)

    def along(e, field, up):
        return pltpu.make_async_remote_copy(
            field.at[NZ if up else 1],
            field.at[0 if up else NZ + 1],
            halo_send.at[e, 8 + up],
            halo_recv.at[e, 8 + up],
            on_slab(1 if up else n_slab - 1),
            MESH,
        )

    def across(e, up, g):
        rows = pl.ds(0, NZ * NC) if g < 0 else pl.ds(16 * g, 16)
        slot = max(g, 0) * 2 + up
        return pltpu.make_async_remote_copy(
            ysend.at[e, up, rows],
            yrecv.at[e, 1 - up, rows],
            halo_send.at[e, slot],
            halo_recv.at[e, slot],
            on_patch(1 if up else n_patch - 1),
            MESH,
        )

    def along_wait(e, field, up):
        along(e, field, up).wait()

        @pl.when(s == (0 if up else n_slab - 1))
        def _():
            field[0 if up else NZ + 1] = jnp.zeros(PLANE, F32)

    def across_start(e, g):
        across(e, 1, g).start()
        across(e, 0, g).start()

    def across_wait(e, g):
        across(e, 1, g).wait()
        across(e, 0, g).wait()
        first, size = (0, NZ * NC) if g < 0 else (16 * g, 16)

        @pl.when(t == 0)
        def _():
            yrecv[e, 0, first : first + size, :] = jnp.zeros((size, 128), F32)

        @pl.when(t == n_patch - 1)
        def _():
            yrecv[e, 1, first : first + size, :] = jnp.zeros((size, 128), F32)

    def halo_start(e, field):
        along(e, field, 1).start()
        along(e, field, 0).start()
        across_start(e, -1)

    def halo_wait(e, field):
        along_wait(e, field, 1)
        along_wait(e, field, 0)
        across_wait(e, -1)

    def put(e, field, z, plane):
        for q in range(NQ):
            for c in range(NC):
                field[z + 1, q, c] = plane[q][c]
        for c in range(NC):
            ysend[e, 0, pl.ds(z * NC + c, 1), :] = plane[0][c][0:1, :]
            ysend[e, 1, pl.ds(z * NC + c, 1), :] = plane[NQ - 1][c][7:8, :]

    lane = iota((8, 128), 1)
    row8 = iota((8, 128), 0)

    def around(e, field, z):
        centre = [[field[z + 1, q, c] for c in range(NC)] for q in range(NQ)]
        total = [[None] * NC for _ in range(NQ)]
        for q in range(NQ):
            right = [pltpu.roll(centre[q][c], 127, 1) for c in range(NC)]
            left = [pltpu.roll(centre[q][c], 1, 1) for c in range(NC)]
            for c in range(NC):
                after = right[c + 1] if c + 1 < NC else 0.0
                before = left[c - 1] if c else 0.0
                x = jnp.where(lane == 127, after, right[c]) + jnp.where(
                    lane == 0, before, left[c]
                )
                if q + 1 < NQ:
                    y_up = centre[q + 1][c]
                else:
                    edge = yrecv[e, 1, pl.ds(z * NC + c, 1), :]
                    y_up = jnp.where(
                        row8 == 7, jnp.broadcast_to(edge, (8, 128)), pltpu.roll(centre[0][c], 7, 0)
                    )
                if q:
                    y_down = centre[q - 1][c]
                else:
                    edge = yrecv[e, 0, pl.ds(z * NC + c, 1), :]
                    y_down = jnp.where(
                        row8 == 0,
                        jnp.broadcast_to(edge, (8, 128)),
                        pltpu.roll(centre[NQ - 1][c], 1, 0),
                    )
                total[q][c] = (field[z, q, c] + field[z + 2, q, c]) + (y_up + y_down) + x
        return centre, total

    for copy in loads[:NC]:
        copy.wait()

    @pl.loop(0, NZ)
    def _(z):
        put(
            0,
            t0,
            z,
            [
                [tin[c, z, pl.ds(q, 8, stride=NQ), :] for c in range(NC)]
                for q in range(NQ)
            ],
        )

    halo_start(0, t0)
    for copy in loads[2 * NC :]:
        copy.wait()

    @pl.loop(0, NCHUNK)
    def _(i):
        rows = pl.ds(pl.multiple_of(i * PER, PER), PER)
        pid = pid_ref[rows, :]
        pid = ((pid & 1) * 128 + (pid >> 1)).astype(F32)
        uu = u_ref[rows, :]
        vv = v_ref[rows, :]
        places = iota((256, 128), 0).astype(F32).astype(BF16)
        for r in range(PER):
            at = slice(128 * r, 128 * r + 128)
            row = jnp.broadcast_to(pid[r : r + 1, :], (16, 128)).astype(BF16)
            for k in range(16):
                onehot[i, 16 * k : 16 * k + 16, at] = jnp.where(
                    places[16 * k : 16 * k + 16] == row, jnp.ones((), BF16), jnp.zeros((), BF16)
                )
            bu[i, :, at] = basis_weights(uu[r : r + 1, :])
            bv[i, :, at] = basis_weights(vv[r : r + 1, :])

    for copy in ag1:
        copy.wait()
    mine = pl.ds(pl.multiple_of(s * (4 * n_patch), 4 * n_patch), 4 * n_patch)
    cp_all[mine, :] = cp_row[...].reshape(4 * n_patch, 128)
    ag2 = []
    for k in range(1, n_slab):
        copy = pltpu.make_async_remote_copy(
            cp_all.at[mine], cp_all.at[mine], ag2_send.at[k], ag2_recv.at[k], on_slab(k), MESH
        )
        copy.start()
        ag2.append(copy)

    group = lane >> 5
    within = lane & 31
    for g in range(NZ):
        rows = slice(8 * g, 8 * g + 8)
        column = cell_ref[rows, :] & 511
        back = jnp.full((8, 128), -1, jnp.int32)
        for k in range(31, 0, -1):
            back = jnp.where(
                (pltpu.roll(column, k, 1) == column) & (within >= k), lane - k, back
            )
        chain[0, rows, :] = back
    for r in range(5):
        for g in range(NZ):
            rows = slice(8 * g, 8 * g + 8)
            back = chain[r, rows, :]
            index = back & 127
            count = jnp.ones((8, 128), F32) if r == 0 else summed[0, rows, :]
            seen = obs_ref[rows, :] if r == 0 else summed[1, rows, :]
            summed[0, rows, :] = count + jnp.where(back >= 0, lanes(count, index), 0.0)
            summed[1, rows, :] = seen + jnp.where(back >= 0, lanes(seen, index), 0.0)
            if r < 4:
                chain[r + 1, rows, :] = jnp.where(back >= 0, lanes(back, index), -1)

    lane16 = iota((16, 128), 1).astype(jnp.int16)

    @pl.loop(0, NZ // 2)
    def _(h):
        column = (cell_ref[pl.ds(pl.multiple_of(h * 16, 16), 16), :] & 511).astype(jnp.int16)
        for q in range(NQ):
            found = [jnp.full((16, 128), 32 * ((q + 1) % NQ), jnp.int16) for _ in range(NC)]
            for j in range(32):
                which = 32 * q + j
                off = jnp.broadcast_to(column[:, which : which + 1], (16, 128)) - lane16
                for c in range(NC):
                    found[c] = jnp.where(
                        off == jnp.int16(128 * c), jnp.int16(which), found[c]
                    )
            for c in range(NC):
                both = found[c].astype(jnp.int32)
                inv[2 * h, q, c] = both[0:8]
                inv[2 * h + 1, q, c] = both[8:16]

    for copy in loads[NC : 2 * NC]:
        copy.wait()
    halo_wait(0, t0)

    for copy in ag2:
        copy.wait()
    for c in range(2):
        for k in range(2):
            block = cp_all[pl.ds(2 * c + k, 128, stride=4), :].T
            high, low = split(block)
            lhs[128 * c : 128 * c + 128, 128 * k : 128 * k + 128] = high
            lhs[256 + 128 * c : 384 + 128 * c, 128 * k : 128 * k + 128] = low

    def face_rows(z):
        return pl.ds(pl.multiple_of(z * 8, 8), 8)

    def coefficients(z):
        for h in range(CHUNK // 256):
            at = slice(256 * h, 256 * h + 256)
            both = jnp.dot(lhs[...], onehot[z, :, at], preferred_element_type=F32)
            own = both[0:256] + both[256:512]
            total = own[0:16] * bu[z, 0:1, at]
            for a in range(1, 16):
                total = total + own[16 * a : 16 * a + 16] * bu[z, a : a + 1, at]
            value = -0.3 * jnp.sum(total * bv[z, :, at], axis=0, keepdims=True)
            for r in range(2):
                htc[pl.ds(z * PER + 2 * h + r, 1), :] = value[:, 128 * r : 128 * r + 128]

    def first_step(z):
        value = htc[face_rows(z), :]
        for r in range(5):
            back = chain[r, face_rows(z), :]
            value = value + jnp.where(back >= 0, lanes(value, back & 127), 0.0)
        count = summed[0, face_rows(z), :]
        seen = summed[1, face_rows(z), :]
        centre, total = around(0, t0, z)
        plane = [[None] * NC for _ in range(NQ)]
        for q in range(NQ):
            mine = group == q
            sources = [jnp.where(mine, x, 0.0) for x in (value, count, seen)]
            for c in range(NC):
                index = inv[z, q, c]
                here = lanes(sources[0], index)
                hfld[z, q, c] = here
                cntf[z, q, c] = lanes(sources[1], index)
                obsf[z, q, c] = lanes(sources[2], index)
                diffusion = cin[c, z, pl.ds(q, 8, stride=NQ), :]
                cond[z, q, c] = diffusion
                now = centre[q][c]
                plane[q][c] = now + diffusion * (total[q][c] - 6.0 * now) + here * now
        put(1, t1, z, plane)

    def second_step(z):
        centre, total = around(1, t1, z)
        weighted = [[None] * NC for _ in range(NQ)]
        for q in range(NQ):
            for c in range(NC):
                here = cond[z, q, c]
                last = (
                    centre[q][c]
                    + here * (total[q][c] - 6.0 * centre[q][c])
                    + hfld[z, q, c] * centre[q][c]
                )
                tst[c, z, pl.ds(q, 8, stride=NQ), :] = last
                adjoint = cntf[z, q, c] * last - obsf[z, q, c]
                adj2[z, q, c] = adjoint
                weighted[q][c] = here * adjoint
        put(2, w2, z, weighted)

    def first_back(z):
        centre, total = around(2, w2, z)
        column = cell_ref[face_rows(z), :] & 511
        key = group * NC + (column >> 7)
        spot = column & 127
        picked = jnp.zeros((8, 128), F32)
        weighted = [[None] * NC for _ in range(NQ)]
        for q in range(NQ):
            for c in range(NC):
                later = adj2[z, q, c]
                adjoint = later + total[q][c] - 6.0 * centre[q][c] + hfld[z, q, c] * later
                adj1[z, q, c] = adjoint
                weighted[q][c] = cond[z, q, c] * adjoint
                product = later * t1[z + 1, q, c] + adjoint * t0[z + 1, q, c]
                picked = jnp.where(key == NC * q + c, lanes(product, spot), picked)
        sens[face_rows(z), :] = -0.3 * picked
        put(3, w1, z, weighted)

    def gradient(z):
        value = sens[face_rows(z), :]
        for r in range(PER):
            at = slice(128 * r, 128 * r + 128)
            right = bv[z, :, at] * value[r : r + 1, :]
            for a in range(16):
                high, low = split(right * bu[z, a : a + 1, at])
                wbuf[16 * a : 16 * a + 16, at] = high
                wbuf[256 + 16 * a : 272 + 16 * a, at] = low
        acc[...] += lax.dot_general(
            wbuf[...], onehot[z], (((1,), (1,)), ((), ())), preferred_element_type=F32
        )

    coefficients(NZ - 1)

    @pl.loop(0, 5)
    def _(k):
        first_step(lax.rem(k + NZ - 1, NZ))
        coefficients(k)

    along(1, t1, 1).start()
    along(1, t1, 0).start()
    across_start(1, 0)

    @pl.loop(5, 9)
    def _(k):
        first_step(k - 1)
        coefficients(k)

    across_start(1, 1)
    along_wait(1, t1, 1)
    across_wait(1, 0)

    @pl.loop(9, 13)
    def _(k):
        second_step(k - 9)
        first_step(k - 1)
        coefficients(k)

    across_start(1, 2)
    along(2, w2, 0).start()
    across_start(2, 0)
    across_wait(1, 1)

    @pl.loop(13, 15)
    def _(k):
        second_step(2 * k - 22)
        second_step(2 * k - 21)
        first_step(k - 1)
        coefficients(k)

    first_step(NZ - 2)
    across_start(1, 3)
    across_start(2, 1)

    acc[...] = jnp.zeros((512, 256), F32)
    across_wait(2, 0)
    first_back(1)

    @pl.loop(1, 3)
    def _(j):
        gradient(j)
        first_back(j + 1)

    across_wait(1, 2)
    across_wait(2, 1)

    @pl.loop(3, 5)
    def _(j):
        gradient(j)
        first_back(j + 1)
        second_step(2 * j + 2)
        second_step(2 * j + 3)

    across_start(2, 2)
    along_wait(1, t1, 0)
    across_wait(1, 3)

    @pl.loop(5, 7)
    def _(j):
        gradient(j)
        first_back(j + 1)
        second_step(2 * j + 2)
        second_step(2 * j + 3)

    along(2, w2, 1).start()
    across_start(2, 3)
    across_wait(2, 2)

    @pl.loop(7, 11)
    def _(j):
        gradient(j)
        first_back(j + 1)

    along_wait(2, w2, 0)
    across_wait(2, 3)

    @pl.loop(11, 15)
    def _(j):
        gradient(j)
        first_back(j + 1)

    along_wait(2, w2, 1)
    gradient(NZ - 1)
    first_back(0)
    halo_start(3, w1)
    gradient(0)

    for c in range(2):
        for k in range(2):
            cols = slice(128 * k, 128 * k + 128)
            block = acc[128 * c : 128 * c + 128, cols] + acc[256 + 128 * c : 384 + 128 * c, cols]
            grad[pl.ds(2 * c + k, 128, stride=4), :] = block.T

    rs1 = []
    for k in range(1, n_slab):
        their = lax.rem(s + k, n_slab)
        copy = pltpu.make_async_remote_copy(
            grad.at[pl.ds(pl.multiple_of(their * (4 * n_patch), 4 * n_patch), 4 * n_patch)],
            part1.at[k],
            rs1_send.at[k],
            rs1_recv.at[k],
            on_slab(k),
            MESH,
        )
        copy.start()
        rs1.append(copy)

    halo_wait(3, w1)

    @pl.loop(0, NZ)
    def _(z):
        centre, total = around(3, w1, z)
        for q in range(NQ):
            for c in range(NC):
                later = adj1[z, q, c]
                ast[c, z, pl.ds(q, 8, stride=NQ), :] = (
                    later + total[q][c] - 6.0 * centre[q][c] + hfld[z, q, c] * later
                )

    for copy in rs1:
        copy.wait()
    total = grad[mine, :]
    for k in range(1, n_slab):
        total = total + part1[k]
    part2_src[...] = total.reshape(n_patch, 4, 128)
    rs2 = []
    for k in range(1, n_patch):
        copy = pltpu.make_async_remote_copy(
            part2_src.at[lax.rem(t + k, n_patch)],
            part2.at[k],
            rs2_send.at[k],
            rs2_recv.at[k],
            on_patch(k),
            MESH,
        )
        copy.start()
        rs2.append(copy)
    for copy in rs2:
        copy.wait()
    total = part2_src[t]
    for k in range(1, n_patch):
        total = total + part2[k]
    gout_ref[:, 0:128] = total[0:2]
    gout_ref[:, 128:256] = total[2:4]


def hand_out(a_in, b_in, c_in, a_out, b_out, c_out, sem):
    copies = [pltpu.make_async_copy(c_in, c_out, sem.at[2 * NC])]
    for n, (src, dst) in enumerate(((a_in, a_out), (b_in, b_out))):
        for c in range(NC):
            copies.append(
                pltpu.make_async_copy(
                    src.at[c], dst.at[:, :, pl.ds(128 * c, 128)], sem.at[NC * n + c]
                )
            )
    for copy in copies:
        copy.start()
    for copy in copies:
        copy.wait()


def local(n_slab, n_patch, temp, cond, cell, pid, u, v, observed, points):
    field = (NZ,) + PLANE
    padded = (NZ + 2,) + PLANE
    natural = (NC, NZ, 32, 128)
    vmem = pltpu.VMEM
    dma = pltpu.SemaphoreType.DMA
    scratch = [
        vmem(natural, F32),
        vmem(natural, F32),
        vmem((ROWS, 128), jnp.int32),
        vmem((ROWS, 128), jnp.int32),
        vmem((ROWS, 128), F32),
        vmem((ROWS, 128), F32),
        vmem((ROWS, 128), F32),
        vmem(points.shape, F32),
        vmem(padded, F32),
        vmem(padded, F32),
        vmem(padded, F32),
        vmem(padded, F32),
        vmem(field, F32),
        vmem(field, F32),
        vmem(field, F32),
        vmem(field, F32),
        vmem(field, F32),
        vmem(field, F32),
        vmem(field, jnp.int32),
        vmem((5, ROWS, 128), jnp.int32),
        vmem((2, ROWS, 128), F32),
        vmem((4, 2, NZ * NC, 128), F32),
        vmem((4, 2, NZ * NC, 128), F32),
        vmem((4, 128), F32),
        vmem((n_patch, 4, 128), F32),
        vmem((4 * n_slab * n_patch, 128), F32),
        vmem((512, 256), BF16),
        vmem((NCHUNK, 256, CHUNK), BF16),
        vmem((NCHUNK, 16, CHUNK), F32),
        vmem((NCHUNK, 16, CHUNK), F32),
        vmem((512, CHUNK), BF16),
        vmem((ROWS, 128), F32),
        vmem((ROWS, 128), F32),
        vmem((512, 256), F32),
        vmem((4 * n_slab * n_patch, 128), F32),
        vmem((n_slab, 4 * n_patch, 128), F32),
        vmem((n_patch, 4, 128), F32),
        vmem((n_patch, 4, 128), F32),
        dma((2 * NC + 6,)),
        dma((n_patch,)),
        dma((n_patch,)),
        dma((n_slab,)),
        dma((n_slab,)),
        dma((n_slab,)),
        dma((n_slab,)),
        dma((n_patch,)),
        dma((n_patch,)),
        dma((4, 10)),
        dma((4, 10)),
    ]
    whole = pl.BlockSpec(memory_space=pltpu.VMEM)
    anywhere = pl.BlockSpec(memory_space=pl.ANY)
    rows = (ROWS, 128)
    final, adjoint, points_out = pl.pallas_call(
        functools.partial(kernel, n_slab, n_patch),
        out_shape=(vmem(natural, F32), vmem(natural, F32), vmem(points.shape, F32)),
        in_specs=[anywhere] * 8,
        out_specs=(whole,) * 3,
        scratch_shapes=scratch,
        compiler_params=pltpu.CompilerParams(
            collective_id=0, has_side_effects=True, vmem_limit_bytes=56 * 1024 * 1024
        ),
        name="adjoint",
    )(
        temp,
        cond,
        cell.reshape(rows),
        pid.reshape(rows),
        u.reshape(rows),
        v.reshape(rows),
        observed.reshape(rows),
        points,
    )
    return pl.pallas_call(
        hand_out,
        out_shape=(
            jax.ShapeDtypeStruct(temp.shape, F32),
            jax.ShapeDtypeStruct(temp.shape, F32),
            jax.ShapeDtypeStruct(points.shape, F32),
        ),
        in_specs=[whole] * 3,
        out_specs=(anywhere,) * 3,
        scratch_shapes=[dma((2 * NC + 1,))],
        name="hand_out",
    )(final, adjoint, points_out)


def solution(mesh):
    in_specs = (
        P("slab", "patch", None),
        P("slab", "patch", None),
        P(("slab", "patch")),
        P(("slab", "patch"), None),
        P(("slab", "patch")),
        P(("slab", "patch")),
        P(("slab", "patch")),
        P(("slab", "patch"), None),
    )
    out_specs = (P("slab", "patch", None), P("slab", "patch", None), P(("slab", "patch"), None))
    return jax.shard_map(
        functools.partial(local, mesh.shape["slab"], mesh.shape["patch"]),
        mesh=mesh,
        in_specs=in_specs,
        out_specs=out_specs,
        check_vma=False,
    )
```

```python
import functools

import jax
import jax.numpy as jnp
from jax import lax
from jax.experimental import pallas as pl
from jax.experimental.pallas import tpu as pltpu
from jax.sharding import PartitionSpec as P

MESH = pl.DeviceIdType.MESH
F32 = jnp.float32
BF16 = jnp.bfloat16
NZ = 16
NQ = 4
NC = 4
PLANE = (NQ, NC, 8, 128)
ROWS = 128
CHUNK = 1024
PER = CHUNK // 128
NCHUNK = ROWS * 128 // CHUNK


def iota(shape, dim):
    return lax.broadcasted_iota(jnp.int32, shape, dim)


def lanes(x, index):
    return jnp.take_along_axis(x, index, axis=1, mode="promise_in_bounds")


def basis_weights(param):
    y = jnp.abs((3.0 + 13.0 * param) - (iota((16, 128), 0) + 2).astype(F32))
    wide = jnp.maximum(2.0 - y, 0.0)
    narrow = jnp.maximum(1.0 - y, 0.0)
    return wide * wide * wide * (1.0 / 6.0) - narrow * narrow * narrow * (4.0 / 6.0)


def split(x):
    high = x.astype(BF16)
    return high, (x - high.astype(F32)).astype(BF16)


def kernel(
    n_slab,
    n_patch,
    temp_hbm,
    cond_hbm,
    cell_hbm,
    pid_hbm,
    u_hbm,
    v_hbm,
    obs_hbm,
    cp_hbm,
    tst,
    ast,
    gout_ref,
    tin,
    cin,
    cell_ref,
    pid_ref,
    u_ref,
    v_ref,
    obs_ref,
    cp_ref,
    t0,
    t1,
    w2,
    w1,
    cond,
    hfld,
    cntf,
    obsf,
    adj2,
    adj1,
    inv,
    chain,
    summed,
    ysend,
    yrecv,
    cp_src,
    cp_row,
    cp_all,
    lhs,
    onehot,
    bu,
    bv,
    wbuf,
    htc,
    sens,
    acc,
    grad,
    part1,
    part2_src,
    part2,
    in_sem,
    ag1_send,
    ag1_recv,
    ag2_send,
    ag2_recv,
    rs1_send,
    rs1_recv,
    rs2_send,
    rs2_recv,
    halo_send,
    halo_recv,
):
    s = lax.axis_index("slab")
    t = lax.axis_index("patch")

    def on_slab(k):
        return (lax.rem(s + k, n_slab), t)

    def on_patch(k):
        return (s, lax.rem(t + k, n_patch))

    load_cp = pltpu.make_async_copy(cp_hbm, cp_ref, in_sem.at[2 * NC + 5])
    load_cp.start()
    barrier = pltpu.get_barrier_semaphore()
    for k in range(1, n_patch):
        pl.semaphore_signal(barrier, inc=1, device_id=on_patch(k), device_id_type=MESH)
    for k in range(1, n_slab):
        pl.semaphore_signal(barrier, inc=1, device_id=on_slab(k), device_id_type=MESH)
    loads = []
    for a, (src, dst) in enumerate(((temp_hbm, tin), (cond_hbm, cin))):
        for c in range(NC):
            loads.append(
                pltpu.make_async_copy(
                    src.at[:, :, pl.ds(128 * c, 128)], dst.at[c], in_sem.at[NC * a + c]
                )
            )
    small = ((pid_hbm, pid_ref), (u_hbm, u_ref), (v_hbm, v_ref), (cell_hbm, cell_ref), (obs_hbm, obs_ref))
    for k, (src, dst) in enumerate(small):
        loads.append(pltpu.make_async_copy(src, dst, in_sem.at[2 * NC + k]))
    for copy in loads[:NC] + loads[2 * NC :] + loads[NC : 2 * NC]:
        copy.start()
    load_cp.wait()
    cp_src[0:2, :] = cp_ref[:, 0:128]
    cp_src[2:4, :] = cp_ref[:, 128:256]
    cp_row[t] = cp_src[...]
    pl.semaphore_wait(barrier, n_slab + n_patch - 2)

    ag1 = []
    for k in range(1, n_patch):
        copy = pltpu.make_async_remote_copy(
            cp_src, cp_row.at[t], ag1_send.at[k], ag1_recv.at[k], on_patch(k), MESH
        )
        copy.start()
        ag1.append(copy)

    def along(e, field, up):
        return pltpu.make_async_remote_copy(
            field.at[NZ if up else 1],
            field.at[0 if up else NZ + 1],
            halo_send.at[e, 8 + up],
            halo_recv.at[e, 8 + up],
            on_slab(1 if up else n_slab - 1),
            MESH,
        )

    def across(e, up, g):
        rows = pl.ds(0, NZ * NC) if g < 0 else pl.ds(16 * g, 16)
        slot = max(g, 0) * 2 + up
        return pltpu.make_async_remote_copy(
            ysend.at[e, up, rows],
            yrecv.at[e, 1 - up, rows],
            halo_send.at[e, slot],
            halo_recv.at[e, slot],
            on_patch(1 if up else n_patch - 1),
            MESH,
        )

    def along_wait(e, field, up):
        along(e, field, up).wait()

        @pl.when(s == (0 if up else n_slab - 1))
        def _():
            field[0 if up else NZ + 1] = jnp.zeros(PLANE, F32)

    def across_start(e, g):
        across(e, 1, g).start()
        across(e, 0, g).start()

    def across_wait(e, g):
        across(e, 1, g).wait()
        across(e, 0, g).wait()
        first, size = (0, NZ * NC) if g < 0 else (16 * g, 16)

        @pl.when(t == 0)
        def _():
            yrecv[e, 0, first : first + size, :] = jnp.zeros((size, 128), F32)

        @pl.when(t == n_patch - 1)
        def _():
            yrecv[e, 1, first : first + size, :] = jnp.zeros((size, 128), F32)

    def halo_start(e, field):
        along(e, field, 1).start()
        along(e, field, 0).start()
        across_start(e, -1)

    def halo_wait(e, field):
        along_wait(e, field, 1)
        along_wait(e, field, 0)
        across_wait(e, -1)

    def put(e, field, z, plane):
        for q in range(NQ):
            for c in range(NC):
                field[z + 1, q, c] = plane[q][c]
        for c in range(NC):
            ysend[e, 0, pl.ds(z * NC + c, 1), :] = plane[0][c][0:1, :]
            ysend[e, 1, pl.ds(z * NC + c, 1), :] = plane[NQ - 1][c][7:8, :]

    lane = iota((8, 128), 1)
    row8 = iota((8, 128), 0)

    def around(e, field, z):
        centre = [[field[z + 1, q, c] for c in range(NC)] for q in range(NQ)]
        total = [[None] * NC for _ in range(NQ)]
        for q in range(NQ):
            right = [pltpu.roll(centre[q][c], 127, 1) for c in range(NC)]
            left = [pltpu.roll(centre[q][c], 1, 1) for c in range(NC)]
            for c in range(NC):
                after = right[c + 1] if c + 1 < NC else 0.0
                before = left[c - 1] if c else 0.0
                x = jnp.where(lane == 127, after, right[c]) + jnp.where(
                    lane == 0, before, left[c]
                )
                if q + 1 < NQ:
                    y_up = centre[q + 1][c]
                else:
                    edge = yrecv[e, 1, pl.ds(z * NC + c, 1), :]
                    y_up = jnp.where(
                        row8 == 7, jnp.broadcast_to(edge, (8, 128)), pltpu.roll(centre[0][c], 7, 0)
                    )
                if q:
                    y_down = centre[q - 1][c]
                else:
                    edge = yrecv[e, 0, pl.ds(z * NC + c, 1), :]
                    y_down = jnp.where(
                        row8 == 0,
                        jnp.broadcast_to(edge, (8, 128)),
                        pltpu.roll(centre[NQ - 1][c], 1, 0),
                    )
                total[q][c] = (field[z, q, c] + field[z + 2, q, c]) + (y_up + y_down) + x
        return centre, total

    for copy in loads[:NC]:
        copy.wait()

    @pl.loop(0, NZ)
    def _(z):
        put(
            0,
            t0,
            z,
            [
                [tin[c, z, pl.ds(q, 8, stride=NQ), :] for c in range(NC)]
                for q in range(NQ)
            ],
        )

    halo_start(0, t0)
    for copy in loads[2 * NC :]:
        copy.wait()

    @pl.loop(0, NCHUNK)
    def _(i):
        rows = pl.ds(pl.multiple_of(i * PER, PER), PER)
        pid = pid_ref[rows, :]
        pid = ((pid & 1) * 128 + (pid >> 1)).astype(F32)
        uu = u_ref[rows, :]
        vv = v_ref[rows, :]
        places = iota((256, 128), 0).astype(F32).astype(BF16)
        for r in range(PER):
            at = slice(128 * r, 128 * r + 128)
            row = jnp.broadcast_to(pid[r : r + 1, :], (16, 128)).astype(BF16)
            for k in range(16):
                onehot[i, 16 * k : 16 * k + 16, at] = jnp.where(
                    places[16 * k : 16 * k + 16] == row, jnp.ones((), BF16), jnp.zeros((), BF16)
                )
            bu[i, :, at] = basis_weights(uu[r : r + 1, :])
            bv[i, :, at] = basis_weights(vv[r : r + 1, :])

    for copy in ag1:
        copy.wait()
    mine = pl.ds(pl.multiple_of(s * (4 * n_patch), 4 * n_patch), 4 * n_patch)
    cp_all[mine, :] = cp_row[...].reshape(4 * n_patch, 128)
    ag2 = []
    for k in range(1, n_slab):
        copy = pltpu.make_async_remote_copy(
            cp_all.at[mine], cp_all.at[mine], ag2_send.at[k], ag2_recv.at[k], on_slab(k), MESH
        )
        copy.start()
        ag2.append(copy)

    group = lane >> 5
    within = lane & 31
    for g in range(NZ):
        rows = slice(8 * g, 8 * g + 8)
        column = cell_ref[rows, :] & 511
        back = jnp.full((8, 128), -1, jnp.int32)
        for k in range(31, 0, -1):
            back = jnp.where(
                (pltpu.roll(column, k, 1) == column) & (within >= k), lane - k, back
            )
        chain[0, rows, :] = back
    for r in range(5):
        for g in range(NZ):
            rows = slice(8 * g, 8 * g + 8)
            back = chain[r, rows, :]
            index = back & 127
            count = jnp.ones((8, 128), F32) if r == 0 else summed[0, rows, :]
            seen = obs_ref[rows, :] if r == 0 else summed[1, rows, :]
            summed[0, rows, :] = count + jnp.where(back >= 0, lanes(count, index), 0.0)
            summed[1, rows, :] = seen + jnp.where(back >= 0, lanes(seen, index), 0.0)
            if r < 4:
                chain[r + 1, rows, :] = jnp.where(back >= 0, lanes(back, index), -1)

    lane16 = iota((16, 128), 1).astype(jnp.int16)

    @pl.loop(0, NZ // 2)
    def _(h):
        column = (cell_ref[pl.ds(pl.multiple_of(h * 16, 16), 16), :] & 511).astype(jnp.int16)
        for q in range(NQ):
            found = [jnp.full((16, 128), 32 * ((q + 1) % NQ), jnp.int16) for _ in range(NC)]
            for j in range(32):
                which = 32 * q + j
                off = jnp.broadcast_to(column[:, which : which + 1], (16, 128)) - lane16
                for c in range(NC):
                    found[c] = jnp.where(
                        off == jnp.int16(128 * c), jnp.int16(which), found[c]
                    )
            for c in range(NC):
                both = found[c].astype(jnp.int32)
                inv[2 * h, q, c] = both[0:8]
                inv[2 * h + 1, q, c] = both[8:16]

    for copy in loads[NC : 2 * NC]:
        copy.wait()
    halo_wait(0, t0)

    for copy in ag2:
        copy.wait()
    for c in range(2):
        for k in range(2):
            block = cp_all[pl.ds(2 * c + k, 128, stride=4), :].T
            high, low = split(block)
            lhs[128 * c : 128 * c + 128, 128 * k : 128 * k + 128] = high
            lhs[256 + 128 * c : 384 + 128 * c, 128 * k : 128 * k + 128] = low

    def face_rows(z):
        return pl.ds(pl.multiple_of(z * 8, 8), 8)

    def coefficients(z):
        for h in range(CHUNK // 256):
            at = slice(256 * h, 256 * h + 256)
            both = jnp.dot(lhs[...], onehot[z, :, at], preferred_element_type=F32)
            own = both[0:256] + both[256:512]
            total = own[0:16] * bu[z, 0:1, at]
            for a in range(1, 16):
                total = total + own[16 * a : 16 * a + 16] * bu[z, a : a + 1, at]
            value = -0.3 * jnp.sum(total * bv[z, :, at], axis=0, keepdims=True)
            for r in range(2):
                htc[pl.ds(z * PER + 2 * h + r, 1), :] = value[:, 128 * r : 128 * r + 128]

    def first_step(z):
        value = htc[face_rows(z), :]
        for r in range(5):
            back = chain[r, face_rows(z), :]
            value = value + jnp.where(back >= 0, lanes(value, back & 127), 0.0)
        count = summed[0, face_rows(z), :]
        seen = summed[1, face_rows(z), :]
        centre, total = around(0, t0, z)
        plane = [[None] * NC for _ in range(NQ)]
        for q in range(NQ):
            mine = group == q
            sources = [jnp.where(mine, x, 0.0) for x in (value, count, seen)]
            for c in range(NC):
                index = inv[z, q, c]
                here = lanes(sources[0], index)
                hfld[z, q, c] = here
                cntf[z, q, c] = lanes(sources[1], index)
                obsf[z, q, c] = lanes(sources[2], index)
                diffusion = cin[c, z, pl.ds(q, 8, stride=NQ), :]
                cond[z, q, c] = diffusion
                now = centre[q][c]
                plane[q][c] = now + diffusion * (total[q][c] - 6.0 * now) + here * now
        put(1, t1, z, plane)

    def second_step(z):
        centre, total = around(1, t1, z)
        weighted = [[None] * NC for _ in range(NQ)]
        for q in range(NQ):
            for c in range(NC):
                here = cond[z, q, c]
                last = (
                    centre[q][c]
                    + here * (total[q][c] - 6.0 * centre[q][c])
                    + hfld[z, q, c] * centre[q][c]
                )
                tst[c, z, pl.ds(q, 8, stride=NQ), :] = last
                adjoint = cntf[z, q, c] * last - obsf[z, q, c]
                adj2[z, q, c] = adjoint
                weighted[q][c] = here * adjoint
        put(2, w2, z, weighted)

    def first_back(z):
        centre, total = around(2, w2, z)
        column = cell_ref[face_rows(z), :] & 511
        key = group * NC + (column >> 7)
        spot = column & 127
        picked = jnp.zeros((8, 128), F32)
        weighted = [[None] * NC for _ in range(NQ)]
        for q in range(NQ):
            for c in range(NC):
                later = adj2[z, q, c]
                adjoint = later + total[q][c] - 6.0 * centre[q][c] + hfld[z, q, c] * later
                adj1[z, q, c] = adjoint
                weighted[q][c] = cond[z, q, c] * adjoint
                product = later * t1[z + 1, q, c] + adjoint * t0[z + 1, q, c]
                picked = jnp.where(key == NC * q + c, lanes(product, spot), picked)
        sens[face_rows(z), :] = -0.3 * picked
        put(3, w1, z, weighted)

    def gradient(z):
        value = sens[face_rows(z), :]
        for r in range(PER):
            at = slice(128 * r, 128 * r + 128)
            right = bv[z, :, at] * value[r : r + 1, :]
            for a in range(16):
                high, low = split(right * bu[z, a : a + 1, at])
                wbuf[16 * a : 16 * a + 16, at] = high
                wbuf[256 + 16 * a : 272 + 16 * a, at] = low
        acc[...] += lax.dot_general(
            wbuf[...], onehot[z], (((1,), (1,)), ((), ())), preferred_element_type=F32
        )

    coefficients(NZ - 1)

    @pl.loop(0, 5)
    def _(k):
        first_step(lax.rem(k + NZ - 1, NZ))
        coefficients(k)

    along(1, t1, 1).start()
    along(1, t1, 0).start()
    across_start(1, 0)

    @pl.loop(5, 9)
    def _(k):
        first_step(k - 1)
        coefficients(k)

    across_start(1, 1)

    @pl.loop(9, 12)
    def _(k):
        first_step(k - 1)
        coefficients(k)

    along_wait(1, t1, 1)
    across_wait(1, 0)

    @pl.loop(12, 14)
    def _(k):
        second_step(2 * k - 24)
        second_step(2 * k - 23)
        first_step(k - 1)
        coefficients(k)

    across_start(1, 2)
    along(2, w2, 0).start()
    across_start(2, 0)
    across_wait(1, 1)

    @pl.loop(14, 15)
    def _(k):
        second_step(k - 10)
        second_step(k - 9)
        first_step(k - 1)
        coefficients(k)

    first_step(NZ - 2)
    across_start(1, 3)
    second_step(6)
    second_step(7)
    across_start(2, 1)

    acc[...] = jnp.zeros((512, 256), F32)
    across_wait(2, 0)
    first_back(1)
    across_wait(1, 2)

    @pl.loop(1, 3)
    def _(j):
        gradient(j)
        first_back(j + 1)
        second_step(2 * j + 6)
        second_step(2 * j + 7)

    across_start(2, 2)
    across_wait(2, 1)
    along_wait(1, t1, 0)
    across_wait(1, 3)

    @pl.loop(3, 5)
    def _(j):
        gradient(j)
        first_back(j + 1)
        second_step(2 * j + 6)
        second_step(2 * j + 7)

    along(2, w2, 1).start()
    across_start(2, 3)

    @pl.loop(5, 7)
    def _(j):
        gradient(j)
        first_back(j + 1)

    across_wait(2, 2)

    @pl.loop(7, 11)
    def _(j):
        gradient(j)
        first_back(j + 1)

    along_wait(2, w2, 0)
    across_wait(2, 3)

    @pl.loop(11, 15)
    def _(j):
        gradient(j)
        first_back(j + 1)

    along_wait(2, w2, 1)
    gradient(NZ - 1)
    first_back(0)
    halo_start(3, w1)
    gradient(0)

    for c in range(2):
        for k in range(2):
            cols = slice(128 * k, 128 * k + 128)
            block = acc[128 * c : 128 * c + 128, cols] + acc[256 + 128 * c : 384 + 128 * c, cols]
            grad[pl.ds(2 * c + k, 128, stride=4), :] = block.T

    rs1 = []
    for k in range(1, n_slab):
        their = lax.rem(s + k, n_slab)
        copy = pltpu.make_async_remote_copy(
            grad.at[pl.ds(pl.multiple_of(their * (4 * n_patch), 4 * n_patch), 4 * n_patch)],
            part1.at[k],
            rs1_send.at[k],
            rs1_recv.at[k],
            on_slab(k),
            MESH,
        )
        copy.start()
        rs1.append(copy)

    halo_wait(3, w1)

    @pl.loop(0, NZ)
    def _(z):
        centre, total = around(3, w1, z)
        for q in range(NQ):
            for c in range(NC):
                later = adj1[z, q, c]
                ast[c, z, pl.ds(q, 8, stride=NQ), :] = (
                    later + total[q][c] - 6.0 * centre[q][c] + hfld[z, q, c] * later
                )

    for copy in rs1:
        copy.wait()
    total = grad[mine, :]
    for k in range(1, n_slab):
        total = total + part1[k]
    part2_src[...] = total.reshape(n_patch, 4, 128)
    rs2 = []
    for k in range(1, n_patch):
        copy = pltpu.make_async_remote_copy(
            part2_src.at[lax.rem(t + k, n_patch)],
            part2.at[k],
            rs2_send.at[k],
            rs2_recv.at[k],
            on_patch(k),
            MESH,
        )
        copy.start()
        rs2.append(copy)
    for copy in rs2:
        copy.wait()
    total = part2_src[t]
    for k in range(1, n_patch):
        total = total + part2[k]
    gout_ref[:, 0:128] = total[0:2]
    gout_ref[:, 128:256] = total[2:4]


def hand_out(a_in, b_in, c_in, a_out, b_out, c_out, sem):
    copies = [pltpu.make_async_copy(c_in, c_out, sem.at[2 * NC])]
    for n, (src, dst) in enumerate(((a_in, a_out), (b_in, b_out))):
        for c in range(NC):
            copies.append(
                pltpu.make_async_copy(
                    src.at[c], dst.at[:, :, pl.ds(128 * c, 128)], sem.at[NC * n + c]
                )
            )
    for copy in copies:
        copy.start()
    for copy in copies:
        copy.wait()


def local(n_slab, n_patch, temp, cond, cell, pid, u, v, observed, points):
    field = (NZ,) + PLANE
    padded = (NZ + 2,) + PLANE
    natural = (NC, NZ, 32, 128)
    vmem = pltpu.VMEM
    dma = pltpu.SemaphoreType.DMA
    scratch = [
        vmem(natural, F32),
        vmem(natural, F32),
        vmem((ROWS, 128), jnp.int32),
        vmem((ROWS, 128), jnp.int32),
        vmem((ROWS, 128), F32),
        vmem((ROWS, 128), F32),
        vmem((ROWS, 128), F32),
        vmem(points.shape, F32),
        vmem(padded, F32),
        vmem(padded, F32),
        vmem(padded, F32),
        vmem(padded, F32),
        vmem(field, F32),
        vmem(field, F32),
        vmem(field, F32),
        vmem(field, F32),
        vmem(field, F32),
        vmem(field, F32),
        vmem(field, jnp.int32),
        vmem((5, ROWS, 128), jnp.int32),
        vmem((2, ROWS, 128), F32),
        vmem((4, 2, NZ * NC, 128), F32),
        vmem((4, 2, NZ * NC, 128), F32),
        vmem((4, 128), F32),
        vmem((n_patch, 4, 128), F32),
        vmem((4 * n_slab * n_patch, 128), F32),
        vmem((512, 256), BF16),
        vmem((NCHUNK, 256, CHUNK), BF16),
        vmem((NCHUNK, 16, CHUNK), F32),
        vmem((NCHUNK, 16, CHUNK), F32),
        vmem((512, CHUNK), BF16),
        vmem((ROWS, 128), F32),
        vmem((ROWS, 128), F32),
        vmem((512, 256), F32),
        vmem((4 * n_slab * n_patch, 128), F32),
        vmem((n_slab, 4 * n_patch, 128), F32),
        vmem((n_patch, 4, 128), F32),
        vmem((n_patch, 4, 128), F32),
        dma((2 * NC + 6,)),
        dma((n_patch,)),
        dma((n_patch,)),
        dma((n_slab,)),
        dma((n_slab,)),
        dma((n_slab,)),
        dma((n_slab,)),
        dma((n_patch,)),
        dma((n_patch,)),
        dma((4, 10)),
        dma((4, 10)),
    ]
    whole = pl.BlockSpec(memory_space=pltpu.VMEM)
    anywhere = pl.BlockSpec(memory_space=pl.ANY)
    rows = (ROWS, 128)
    final, adjoint, points_out = pl.pallas_call(
        functools.partial(kernel, n_slab, n_patch),
        out_shape=(vmem(natural, F32), vmem(natural, F32), vmem(points.shape, F32)),
        in_specs=[anywhere] * 8,
        out_specs=(whole,) * 3,
        scratch_shapes=scratch,
        compiler_params=pltpu.CompilerParams(
            collective_id=0, has_side_effects=True, vmem_limit_bytes=56 * 1024 * 1024
        ),
        name="adjoint",
    )(
        temp,
        cond,
        cell.reshape(rows),
        pid.reshape(rows),
        u.reshape(rows),
        v.reshape(rows),
        observed.reshape(rows),
        points,
    )
    return pl.pallas_call(
        hand_out,
        out_shape=(
            jax.ShapeDtypeStruct(temp.shape, F32),
            jax.ShapeDtypeStruct(temp.shape, F32),
            jax.ShapeDtypeStruct(points.shape, F32),
        ),
        in_specs=[whole] * 3,
        out_specs=(anywhere,) * 3,
        scratch_shapes=[dma((2 * NC + 1,))],
        name="hand_out",
    )(*(pltpu.with_memory_space_constraint(x, pltpu.VMEM) for x in (final, adjoint, points_out)))


def solution(mesh):
    in_specs = (
        P("slab", "patch", None),
        P("slab", "patch", None),
        P(("slab", "patch")),
        P(("slab", "patch"), None),
        P(("slab", "patch")),
        P(("slab", "patch")),
        P(("slab", "patch")),
        P(("slab", "patch"), None),
    )
    out_specs = (P("slab", "patch", None), P("slab", "patch", None), P(("slab", "patch"), None))
    return jax.shard_map(
        functools.partial(local, mesh.shape["slab"], mesh.shape["patch"]),
        mesh=mesh,
        in_specs=in_specs,
        out_specs=out_specs,
        check_vma=False,
    )
```

```python
import functools

import jax
import jax.numpy as jnp
from jax import lax
from jax.experimental import pallas as pl
from jax.experimental.pallas import tpu as pltpu
from jax.sharding import PartitionSpec as P

MESH = pl.DeviceIdType.MESH
F32 = jnp.float32
BF16 = jnp.bfloat16
NZ = 16
NQ = 4
NC = 4
PLANE = (NQ, NC, 8, 128)
ROWS = 128
CHUNK = 1024
PER = CHUNK // 128
NCHUNK = ROWS * 128 // CHUNK


def iota(shape, dim):
    return lax.broadcasted_iota(jnp.int32, shape, dim)


def lanes(x, index):
    return jnp.take_along_axis(x, index, axis=1, mode="promise_in_bounds")


def basis_weights(param):
    y = jnp.abs((3.0 + 13.0 * param) - (iota((16, 128), 0) + 2).astype(F32))
    wide = jnp.maximum(2.0 - y, 0.0)
    narrow = jnp.maximum(1.0 - y, 0.0)
    return wide * wide * wide * (1.0 / 6.0) - narrow * narrow * narrow * (4.0 / 6.0)


def split(x):
    high = x.astype(BF16)
    return high, (x - high.astype(F32)).astype(BF16)


def kernel(
    n_slab,
    n_patch,
    temp_hbm,
    cond_hbm,
    cell_hbm,
    pid_hbm,
    u_hbm,
    v_hbm,
    obs_hbm,
    cp_hbm,
    tst,
    ast,
    gout_ref,
    tin,
    cin,
    cell_ref,
    pid_ref,
    u_ref,
    v_ref,
    obs_ref,
    cp_ref,
    t0,
    t1,
    w2,
    w1,
    cond,
    hfld,
    cntf,
    obsf,
    adj2,
    adj1,
    inv,
    chain,
    summed,
    ysend,
    yrecv,
    cp_src,
    cp_row,
    cp_all,
    lhs,
    onehot,
    bu,
    bv,
    wbuf,
    htc,
    sens,
    acc,
    grad,
    part1,
    part2_src,
    part2,
    in_sem,
    ag1_send,
    ag1_recv,
    ag2_send,
    ag2_recv,
    rs1_send,
    rs1_recv,
    rs2_send,
    rs2_recv,
    halo_send,
    halo_recv,
):
    s = lax.axis_index("slab")
    t = lax.axis_index("patch")

    def on_slab(k):
        return (lax.rem(s + k, n_slab), t)

    def on_patch(k):
        return (s, lax.rem(t + k, n_patch))

    load_cp = pltpu.make_async_copy(cp_hbm, cp_ref, in_sem.at[2 * NC + 5])
    load_cp.start()
    barrier = pltpu.get_barrier_semaphore()
    for k in range(1, n_patch):
        pl.semaphore_signal(barrier, inc=1, device_id=on_patch(k), device_id_type=MESH)
    for k in range(1, n_slab):
        pl.semaphore_signal(barrier, inc=1, device_id=on_slab(k), device_id_type=MESH)
    loads = []
    for a, (src, dst) in enumerate(((temp_hbm, tin), (cond_hbm, cin))):
        for c in range(NC):
            loads.append(
                pltpu.make_async_copy(
                    src.at[:, :, pl.ds(128 * c, 128)], dst.at[c], in_sem.at[NC * a + c]
                )
            )
    small = ((pid_hbm, pid_ref), (u_hbm, u_ref), (v_hbm, v_ref), (cell_hbm, cell_ref), (obs_hbm, obs_ref))
    for k, (src, dst) in enumerate(small):
        loads.append(pltpu.make_async_copy(src, dst, in_sem.at[2 * NC + k]))
    for copy in loads[:NC] + loads[2 * NC :] + loads[NC : 2 * NC]:
        copy.start()
    load_cp.wait()
    cp_src[0:2, :] = cp_ref[:, 0:128]
    cp_src[2:4, :] = cp_ref[:, 128:256]
    cp_row[t] = cp_src[...]
    pl.semaphore_wait(barrier, n_slab + n_patch - 2)

    ag1 = []
    for k in range(1, n_patch):
        copy = pltpu.make_async_remote_copy(
            cp_src, cp_row.at[t], ag1_send.at[k], ag1_recv.at[k], on_patch(k), MESH
        )
        copy.start()
        ag1.append(copy)

    def along(e, field, up):
        return pltpu.make_async_remote_copy(
            field.at[NZ if up else 1],
            field.at[0 if up else NZ + 1],
            halo_send.at[e, 8 + up],
            halo_recv.at[e, 8 + up],
            on_slab(1 if up else n_slab - 1),
            MESH,
        )

    def across(e, up, g):
        rows = pl.ds(0, NZ * NC) if g < 0 else pl.ds(16 * g, 16)
        slot = max(g, 0) * 2 + up
        return pltpu.make_async_remote_copy(
            ysend.at[e, up, rows],
            yrecv.at[e, 1 - up, rows],
            halo_send.at[e, slot],
            halo_recv.at[e, slot],
            on_patch(1 if up else n_patch - 1),
            MESH,
        )

    def along_wait(e, field, up):
        along(e, field, up).wait()

        @pl.when(s == (0 if up else n_slab - 1))
        def _():
            field[0 if up else NZ + 1] = jnp.zeros(PLANE, F32)

    def across_start(e, g):
        across(e, 1, g).start()
        across(e, 0, g).start()

    def across_wait(e, g):
        across(e, 1, g).wait()
        across(e, 0, g).wait()
        first, size = (0, NZ * NC) if g < 0 else (16 * g, 16)

        @pl.when(t == 0)
        def _():
            yrecv[e, 0, first : first + size, :] = jnp.zeros((size, 128), F32)

        @pl.when(t == n_patch - 1)
        def _():
            yrecv[e, 1, first : first + size, :] = jnp.zeros((size, 128), F32)

    def halo_start(e, field):
        along(e, field, 1).start()
        along(e, field, 0).start()
        across_start(e, -1)

    def halo_wait(e, field):
        along_wait(e, field, 1)
        along_wait(e, field, 0)
        across_wait(e, -1)

    def put(e, field, z, plane):
        for q in range(NQ):
            for c in range(NC):
                field[z + 1, q, c] = plane[q][c]
        for c in range(NC):
            ysend[e, 0, pl.ds(z * NC + c, 1), :] = plane[0][c][0:1, :]
            ysend[e, 1, pl.ds(z * NC + c, 1), :] = plane[NQ - 1][c][7:8, :]

    lane = iota((8, 128), 1)
    row8 = iota((8, 128), 0)

    def around(e, field, z):
        centre = [[field[z + 1, q, c] for c in range(NC)] for q in range(NQ)]
        total = [[None] * NC for _ in range(NQ)]
        for q in range(NQ):
            right = [pltpu.roll(centre[q][c], 127, 1) for c in range(NC)]
            left = [pltpu.roll(centre[q][c], 1, 1) for c in range(NC)]
            for c in range(NC):
                after = right[c + 1] if c + 1 < NC else 0.0
                before = left[c - 1] if c else 0.0
                x = jnp.where(lane == 127, after, right[c]) + jnp.where(
                    lane == 0, before, left[c]
                )
                if q + 1 < NQ:
                    y_up = centre[q + 1][c]
                else:
                    edge = yrecv[e, 1, pl.ds(z * NC + c, 1), :]
                    y_up = jnp.where(
                        row8 == 7, jnp.broadcast_to(edge, (8, 128)), pltpu.roll(centre[0][c], 7, 0)
                    )
                if q:
                    y_down = centre[q - 1][c]
                else:
                    edge = yrecv[e, 0, pl.ds(z * NC + c, 1), :]
                    y_down = jnp.where(
                        row8 == 0,
                        jnp.broadcast_to(edge, (8, 128)),
                        pltpu.roll(centre[NQ - 1][c], 1, 0),
                    )
                total[q][c] = (field[z, q, c] + field[z + 2, q, c]) + (y_up + y_down) + x
        return centre, total

    for copy in loads[:NC]:
        copy.wait()

    @pl.loop(0, NZ)
    def _(z):
        put(
            0,
            t0,
            z,
            [
                [tin[c, z, pl.ds(q, 8, stride=NQ), :] for c in range(NC)]
                for q in range(NQ)
            ],
        )

    halo_start(0, t0)
    for copy in loads[2 * NC :]:
        copy.wait()

    @pl.loop(0, NCHUNK)
    def _(i):
        rows = pl.ds(pl.multiple_of(i * PER, PER), PER)
        pid = pid_ref[rows, :]
        pid = ((pid & 1) * 128 + (pid >> 1)).astype(F32)
        uu = u_ref[rows, :]
        vv = v_ref[rows, :]
        places = iota((256, 128), 0).astype(F32).astype(BF16)
        for r in range(PER):
            at = slice(128 * r, 128 * r + 128)
            row = jnp.broadcast_to(pid[r : r + 1, :], (16, 128)).astype(BF16)
            for k in range(16):
                onehot[i, 16 * k : 16 * k + 16, at] = jnp.where(
                    places[16 * k : 16 * k + 16] == row, jnp.ones((), BF16), jnp.zeros((), BF16)
                )
            bu[i, :, at] = basis_weights(uu[r : r + 1, :])
            bv[i, :, at] = basis_weights(vv[r : r + 1, :])

    for copy in ag1:
        copy.wait()
    mine = pl.ds(pl.multiple_of(s * (4 * n_patch), 4 * n_patch), 4 * n_patch)
    cp_all[mine, :] = cp_row[...].reshape(4 * n_patch, 128)
    ag2 = []
    for k in range(1, n_slab):
        copy = pltpu.make_async_remote_copy(
            cp_all.at[mine], cp_all.at[mine], ag2_send.at[k], ag2_recv.at[k], on_slab(k), MESH
        )
        copy.start()
        ag2.append(copy)

    group = lane >> 5
    within = lane & 31
    for g in range(NZ):
        rows = slice(8 * g, 8 * g + 8)
        column = cell_ref[rows, :] & 511
        back = jnp.full((8, 128), -1, jnp.int32)
        for k in range(31, 0, -1):
            back = jnp.where(
                (pltpu.roll(column, k, 1) == column) & (within >= k), lane - k, back
            )
        chain[0, rows, :] = back
    for r in range(5):
        for g in range(NZ):
            rows = slice(8 * g, 8 * g + 8)
            back = chain[r, rows, :]
            index = back & 127
            count = jnp.ones((8, 128), F32) if r == 0 else summed[0, rows, :]
            seen = obs_ref[rows, :] if r == 0 else summed[1, rows, :]
            summed[0, rows, :] = count + jnp.where(back >= 0, lanes(count, index), 0.0)
            summed[1, rows, :] = seen + jnp.where(back >= 0, lanes(seen, index), 0.0)
            if r < 4:
                chain[r + 1, rows, :] = jnp.where(back >= 0, lanes(back, index), -1)

    lane16 = iota((16, 128), 1).astype(jnp.int16)

    @pl.loop(0, NZ // 2)
    def _(h):
        column = (cell_ref[pl.ds(pl.multiple_of(h * 16, 16), 16), :] & 511).astype(jnp.int16)
        for q in range(NQ):
            found = [jnp.full((16, 128), 32 * ((q + 1) % NQ), jnp.int16) for _ in range(NC)]
            for j in range(32):
                which = 32 * q + j
                off = jnp.broadcast_to(column[:, which : which + 1], (16, 128)) - lane16
                for c in range(NC):
                    found[c] = jnp.where(
                        off == jnp.int16(128 * c), jnp.int16(which), found[c]
                    )
            for c in range(NC):
                both = found[c].astype(jnp.int32)
                inv[2 * h, q, c] = both[0:8]
                inv[2 * h + 1, q, c] = both[8:16]

    for copy in loads[NC : 2 * NC]:
        copy.wait()
    halo_wait(0, t0)

    for copy in ag2:
        copy.wait()
    for c in range(2):
        for k in range(2):
            block = cp_all[pl.ds(2 * c + k, 128, stride=4), :].T
            high, low = split(block)
            lhs[128 * c : 128 * c + 128, 128 * k : 128 * k + 128] = high
            lhs[256 + 128 * c : 384 + 128 * c, 128 * k : 128 * k + 128] = low

    def face_rows(z):
        return pl.ds(pl.multiple_of(z * 8, 8), 8)

    def coefficients(z):
        for h in range(CHUNK // 256):
            at = slice(256 * h, 256 * h + 256)
            both = jnp.dot(lhs[...], onehot[z, :, at], preferred_element_type=F32)
            own = both[0:256] + both[256:512]
            total = own[0:16] * bu[z, 0:1, at]
            for a in range(1, 16):
                total = total + own[16 * a : 16 * a + 16] * bu[z, a : a + 1, at]
            value = -0.3 * jnp.sum(total * bv[z, :, at], axis=0, keepdims=True)
            for r in range(2):
                htc[pl.ds(z * PER + 2 * h + r, 1), :] = value[:, 128 * r : 128 * r + 128]

    def first_step(z):
        value = htc[face_rows(z), :]
        for r in range(5):
            back = chain[r, face_rows(z), :]
            value = value + jnp.where(back >= 0, lanes(value, back & 127), 0.0)
        count = summed[0, face_rows(z), :]
        seen = summed[1, face_rows(z), :]
        centre, total = around(0, t0, z)
        plane = [[None] * NC for _ in range(NQ)]
        for q in range(NQ):
            mine = group == q
            sources = [jnp.where(mine, x, 0.0) for x in (value, count, seen)]
            for c in range(NC):
                index = inv[z, q, c]
                here = lanes(sources[0], index)
                hfld[z, q, c] = here
                cntf[z, q, c] = lanes(sources[1], index)
                obsf[z, q, c] = lanes(sources[2], index)
                diffusion = cin[c, z, pl.ds(q, 8, stride=NQ), :]
                cond[z, q, c] = diffusion
                now = centre[q][c]
                plane[q][c] = now + diffusion * (total[q][c] - 6.0 * now) + here * now
        put(1, t1, z, plane)

    def second_step(z):
        centre, total = around(1, t1, z)
        weighted = [[None] * NC for _ in range(NQ)]
        for q in range(NQ):
            for c in range(NC):
                here = cond[z, q, c]
                last = (
                    centre[q][c]
                    + here * (total[q][c] - 6.0 * centre[q][c])
                    + hfld[z, q, c] * centre[q][c]
                )
                tst[c, z, pl.ds(q, 8, stride=NQ), :] = last
                adjoint = cntf[z, q, c] * last - obsf[z, q, c]
                adj2[z, q, c] = adjoint
                weighted[q][c] = here * adjoint
        put(2, w2, z, weighted)

    def first_back(z):
        centre, total = around(2, w2, z)
        column = cell_ref[face_rows(z), :] & 511
        key = group * NC + (column >> 7)
        spot = column & 127
        picked = jnp.zeros((8, 128), F32)
        weighted = [[None] * NC for _ in range(NQ)]
        for q in range(NQ):
            for c in range(NC):
                later = adj2[z, q, c]
                adjoint = later + total[q][c] - 6.0 * centre[q][c] + hfld[z, q, c] * later
                adj1[z, q, c] = adjoint
                weighted[q][c] = cond[z, q, c] * adjoint
                product = later * t1[z + 1, q, c] + adjoint * t0[z + 1, q, c]
                picked = jnp.where(key == NC * q + c, lanes(product, spot), picked)
        sens[face_rows(z), :] = -0.3 * picked
        put(3, w1, z, weighted)

    def second_back(z):
        centre, total = around(3, w1, z)
        for q in range(NQ):
            for c in range(NC):
                later = adj1[z, q, c]
                ast[c, z, pl.ds(q, 8, stride=NQ), :] = (
                    later + total[q][c] - 6.0 * centre[q][c] + hfld[z, q, c] * later
                )

    def gradient(z):
        value = sens[face_rows(z), :]
        for r in range(PER):
            at = slice(128 * r, 128 * r + 128)
            right = bv[z, :, at] * value[r : r + 1, :]
            for a in range(16):
                high, low = split(right * bu[z, a : a + 1, at])
                wbuf[16 * a : 16 * a + 16, at] = high
                wbuf[256 + 16 * a : 272 + 16 * a, at] = low
        acc[...] += lax.dot_general(
            wbuf[...], onehot[z], (((1,), (1,)), ((), ())), preferred_element_type=F32
        )

    coefficients(NZ - 1)

    @pl.loop(0, 5)
    def _(k):
        first_step(lax.rem(k + NZ - 1, NZ))
        coefficients(k)

    along(1, t1, 1).start()
    along(1, t1, 0).start()
    across_start(1, 0)

    @pl.loop(5, 9)
    def _(k):
        first_step(k - 1)
        coefficients(k)

    across_start(1, 1)

    @pl.loop(9, 11)
    def _(k):
        first_step(k - 1)
        coefficients(k)

    along_wait(1, t1, 1)
    across_wait(1, 0)

    @pl.loop(11, 13)
    def _(k):
        second_step(2 * k - 22)
        second_step(2 * k - 21)
        first_step(k - 1)
        coefficients(k)

    across_start(1, 2)
    along(2, w2, 0).start()
    across_start(2, 0)
    across_wait(1, 1)

    @pl.loop(13, 15)
    def _(k):
        second_step(2 * k - 22)
        second_step(2 * k - 21)
        first_step(k - 1)
        coefficients(k)

    across_start(2, 1)
    first_step(NZ - 2)
    across_start(1, 3)

    acc[...] = jnp.zeros((512, 256), F32)
    across_wait(2, 0)
    first_back(1)
    across_wait(1, 2)

    @pl.loop(1, 3)
    def _(j):
        gradient(j)
        first_back(j + 1)
        second_step(2 * j + 6)
        second_step(2 * j + 7)

    across_start(2, 2)
    across_wait(2, 1)
    along_wait(1, t1, 0)
    across_wait(1, 3)

    @pl.loop(3, 5)
    def _(j):
        gradient(j)
        first_back(j + 1)
        second_step(2 * j + 6)
        second_step(2 * j + 7)

    along(2, w2, 1).start()
    across_start(2, 3)

    @pl.loop(5, 7)
    def _(j):
        gradient(j)
        first_back(j + 1)

    across_start(3, 1)
    across_wait(2, 2)

    @pl.loop(7, 11)
    def _(j):
        gradient(j)
        first_back(j + 1)

    across_start(3, 2)
    along_wait(2, w2, 0)
    across_wait(2, 3)
    across_wait(3, 1)

    @pl.loop(11, 15)
    def _(j):
        gradient(j)
        first_back(j + 1)
        second_back(j - 7)

    along(3, w1, 1).start()
    across_start(3, 3)
    along_wait(2, w2, 1)
    gradient(NZ - 1)
    first_back(0)
    along(3, w1, 0).start()
    across_start(3, 0)
    gradient(0)

    for c in range(2):
        for k in range(2):
            cols = slice(128 * k, 128 * k + 128)
            block = acc[128 * c : 128 * c + 128, cols] + acc[256 + 128 * c : 384 + 128 * c, cols]
            grad[pl.ds(2 * c + k, 128, stride=4), :] = block.T

    rs1 = []
    for k in range(1, n_slab):
        their = lax.rem(s + k, n_slab)
        copy = pltpu.make_async_remote_copy(
            grad.at[pl.ds(pl.multiple_of(their * (4 * n_patch), 4 * n_patch), 4 * n_patch)],
            part1.at[k],
            rs1_send.at[k],
            rs1_recv.at[k],
            on_slab(k),
            MESH,
        )
        copy.start()
        rs1.append(copy)

    across_wait(3, 2)
    across_wait(3, 3)

    @pl.loop(8, 15)
    def _(z):
        second_back(z)

    for copy in rs1:
        copy.wait()
    total = grad[mine, :]
    for k in range(1, n_slab):
        total = total + part1[k]
    part2_src[...] = total.reshape(n_patch, 4, 128)
    rs2 = []
    for k in range(1, n_patch):
        copy = pltpu.make_async_remote_copy(
            part2_src.at[lax.rem(t + k, n_patch)],
            part2.at[k],
            rs2_send.at[k],
            rs2_recv.at[k],
            on_patch(k),
            MESH,
        )
        copy.start()
        rs2.append(copy)
    along_wait(3, w1, 1)
    along_wait(3, w1, 0)
    across_wait(3, 0)

    @pl.loop(0, 5)
    def _(k):
        second_back(lax.rem(k + NZ - 1, NZ))

    for copy in rs2:
        copy.wait()
    total = part2_src[t]
    for k in range(1, n_patch):
        total = total + part2[k]
    gout_ref[:, 0:128] = total[0:2]
    gout_ref[:, 128:256] = total[2:4]


def hand_out(a_in, b_in, c_in, a_out, b_out, c_out, sem):
    copies = [pltpu.make_async_copy(c_in, c_out, sem.at[2 * NC])]
    for n, (src, dst) in enumerate(((a_in, a_out), (b_in, b_out))):
        for c in range(NC):
            copies.append(
                pltpu.make_async_copy(
                    src.at[c], dst.at[:, :, pl.ds(128 * c, 128)], sem.at[NC * n + c]
                )
            )
    for copy in copies:
        copy.start()
    for copy in copies:
        copy.wait()


def local(n_slab, n_patch, temp, cond, cell, pid, u, v, observed, points):
    field = (NZ,) + PLANE
    padded = (NZ + 2,) + PLANE
    natural = (NC, NZ, 32, 128)
    vmem = pltpu.VMEM
    dma = pltpu.SemaphoreType.DMA
    scratch = [
        vmem(natural, F32),
        vmem(natural, F32),
        vmem((ROWS, 128), jnp.int32),
        vmem((ROWS, 128), jnp.int32),
        vmem((ROWS, 128), F32),
        vmem((ROWS, 128), F32),
        vmem((ROWS, 128), F32),
        vmem(points.shape, F32),
        vmem(padded, F32),
        vmem(padded, F32),
        vmem(padded, F32),
        vmem(padded, F32),
        vmem(field, F32),
        vmem(field, F32),
        vmem(field, F32),
        vmem(field, F32),
        vmem(field, F32),
        vmem(field, F32),
        vmem(field, jnp.int32),
        vmem((5, ROWS, 128), jnp.int32),
        vmem((2, ROWS, 128), F32),
        vmem((4, 2, NZ * NC, 128), F32),
        vmem((4, 2, NZ * NC, 128), F32),
        vmem((4, 128), F32),
        vmem((n_patch, 4, 128), F32),
        vmem((4 * n_slab * n_patch, 128), F32),
        vmem((512, 256), BF16),
        vmem((NCHUNK, 256, CHUNK), BF16),
        vmem((NCHUNK, 16, CHUNK), F32),
        vmem((NCHUNK, 16, CHUNK), F32),
        vmem((512, CHUNK), BF16),
        vmem((ROWS, 128), F32),
        vmem((ROWS, 128), F32),
        vmem((512, 256), F32),
        vmem((4 * n_slab * n_patch, 128), F32),
        vmem((n_slab, 4 * n_patch, 128), F32),
        vmem((n_patch, 4, 128), F32),
        vmem((n_patch, 4, 128), F32),
        dma((2 * NC + 6,)),
        dma((n_patch,)),
        dma((n_patch,)),
        dma((n_slab,)),
        dma((n_slab,)),
        dma((n_slab,)),
        dma((n_slab,)),
        dma((n_patch,)),
        dma((n_patch,)),
        dma((4, 10)),
        dma((4, 10)),
    ]
    whole = pl.BlockSpec(memory_space=pltpu.VMEM)
    anywhere = pl.BlockSpec(memory_space=pl.ANY)
    rows = (ROWS, 128)
    final, adjoint, points_out = pl.pallas_call(
        functools.partial(kernel, n_slab, n_patch),
        out_shape=(vmem(natural, F32), vmem(natural, F32), vmem(points.shape, F32)),
        in_specs=[anywhere] * 8,
        out_specs=(whole,) * 3,
        scratch_shapes=scratch,
        compiler_params=pltpu.CompilerParams(
            collective_id=0, has_side_effects=True, vmem_limit_bytes=56 * 1024 * 1024
        ),
        name="adjoint",
    )(
        temp,
        cond,
        cell.reshape(rows),
        pid.reshape(rows),
        u.reshape(rows),
        v.reshape(rows),
        observed.reshape(rows),
        points,
    )
    return pl.pallas_call(
        hand_out,
        out_shape=(
            jax.ShapeDtypeStruct(temp.shape, F32),
            jax.ShapeDtypeStruct(temp.shape, F32),
            jax.ShapeDtypeStruct(points.shape, F32),
        ),
        in_specs=[whole] * 3,
        out_specs=(anywhere,) * 3,
        scratch_shapes=[dma((2 * NC + 1,))],
        name="hand_out",
    )(*(pltpu.with_memory_space_constraint(x, pltpu.VMEM) for x in (final, adjoint, points_out)))


def solution(mesh):
    in_specs = (
        P("slab", "patch", None),
        P("slab", "patch", None),
        P(("slab", "patch")),
        P(("slab", "patch"), None),
        P(("slab", "patch")),
        P(("slab", "patch")),
        P(("slab", "patch")),
        P(("slab", "patch"), None),
    )
    out_specs = (P("slab", "patch", None), P("slab", "patch", None), P(("slab", "patch"), None))
    return jax.shard_map(
        functools.partial(local, mesh.shape["slab"], mesh.shape["patch"]),
        mesh=mesh,
        in_specs=in_specs,
        out_specs=out_specs,
        check_vma=False,
    )
```

```python
import functools

import jax
import jax.numpy as jnp
from jax import lax
from jax.experimental import pallas as pl
from jax.experimental.pallas import tpu as pltpu
from jax.sharding import PartitionSpec as P

MESH = pl.DeviceIdType.MESH
F32 = jnp.float32
BF16 = jnp.bfloat16
NZ = 16
NQ = 4
NC = 4
PLANE = (NQ, NC, 8, 128)
ROWS = 128
CHUNK = 1024
PER = CHUNK // 128
NCHUNK = ROWS * 128 // CHUNK


def iota(shape, dim):
    return lax.broadcasted_iota(jnp.int32, shape, dim)


def lanes(x, index):
    return jnp.take_along_axis(x, index, axis=1, mode="promise_in_bounds")


def basis_weights(param):
    y = jnp.abs((3.0 + 13.0 * param) - (iota((16, 128), 0) + 2).astype(F32))
    wide = jnp.maximum(2.0 - y, 0.0)
    narrow = jnp.maximum(1.0 - y, 0.0)
    return wide * wide * wide * (1.0 / 6.0) - narrow * narrow * narrow * (4.0 / 6.0)


def split(x):
    high = x.astype(BF16)
    return high, (x - high.astype(F32)).astype(BF16)


def kernel(
    n_slab,
    n_patch,
    temp_hbm,
    cond_hbm,
    cell_hbm,
    pid_hbm,
    u_hbm,
    v_hbm,
    obs_hbm,
    cp_hbm,
    tst,
    ast,
    gout_ref,
    tin,
    cin,
    cell_ref,
    pid_ref,
    u_ref,
    v_ref,
    obs_ref,
    cp_ref,
    t0,
    t1,
    w2,
    w1,
    cond,
    hfld,
    cntf,
    obsf,
    adj2,
    adj1,
    inv,
    chain,
    summed,
    ysend,
    yrecv,
    cp_src,
    cp_row,
    cp_all,
    lhs,
    onehot,
    bu,
    bv,
    wbuf,
    htc,
    sens,
    acc,
    grad,
    part1,
    part2_src,
    part2,
    in_sem,
    ag1_send,
    ag1_recv,
    ag2_send,
    ag2_recv,
    rs1_send,
    rs1_recv,
    rs2_send,
    rs2_recv,
    halo_send,
    halo_recv,
):
    s = lax.axis_index("slab")
    t = lax.axis_index("patch")

    def on_slab(k):
        return (lax.rem(s + k, n_slab), t)

    def on_patch(k):
        return (s, lax.rem(t + k, n_patch))

    load_cp = pltpu.make_async_copy(cp_hbm, cp_ref, in_sem.at[2 * NC + 5])
    load_cp.start()
    barrier = pltpu.get_barrier_semaphore()
    for k in range(1, n_patch):
        pl.semaphore_signal(barrier, inc=1, device_id=on_patch(k), device_id_type=MESH)
    for k in range(1, n_slab):
        pl.semaphore_signal(barrier, inc=1, device_id=on_slab(k), device_id_type=MESH)
    loads = []
    for a, (src, dst) in enumerate(((temp_hbm, tin), (cond_hbm, cin))):
        for c in range(NC):
            loads.append(
                pltpu.make_async_copy(
                    src.at[:, :, pl.ds(128 * c, 128)], dst.at[c], in_sem.at[NC * a + c]
                )
            )
    small = ((pid_hbm, pid_ref), (u_hbm, u_ref), (v_hbm, v_ref), (cell_hbm, cell_ref), (obs_hbm, obs_ref))
    for k, (src, dst) in enumerate(small):
        loads.append(pltpu.make_async_copy(src, dst, in_sem.at[2 * NC + k]))
    for copy in loads[:NC] + loads[2 * NC :] + loads[NC : 2 * NC]:
        copy.start()
    load_cp.wait()
    cp_src[0:2, :] = cp_ref[:, 0:128]
    cp_src[2:4, :] = cp_ref[:, 128:256]
    cp_row[s] = cp_src[...]
    pl.semaphore_wait(barrier, n_slab + n_patch - 2)

    ag1 = []
    for k in range(1, n_slab):
        copy = pltpu.make_async_remote_copy(
            cp_src, cp_row.at[s], ag1_send.at[k], ag1_recv.at[k], on_slab(k), MESH
        )
        copy.start()
        ag1.append(copy)

    def along(e, field, up):
        return pltpu.make_async_remote_copy(
            field.at[NZ if up else 1],
            field.at[0 if up else NZ + 1],
            halo_send.at[e, 8 + up],
            halo_recv.at[e, 8 + up],
            on_slab(1 if up else n_slab - 1),
            MESH,
        )

    def across(e, up, g):
        rows = pl.ds(0, NZ * NC) if g < 0 else pl.ds(16 * g, 16)
        slot = max(g, 0) * 2 + up
        return pltpu.make_async_remote_copy(
            ysend.at[e, up, rows],
            yrecv.at[e, 1 - up, rows],
            halo_send.at[e, slot],
            halo_recv.at[e, slot],
            on_patch(1 if up else n_patch - 1),
            MESH,
        )

    def along_wait(e, field, up):
        along(e, field, up).wait()

        @pl.when(s == (0 if up else n_slab - 1))
        def _():
            field[0 if up else NZ + 1] = jnp.zeros(PLANE, F32)

    def across_start(e, g):
        across(e, 1, g).start()
        across(e, 0, g).start()

    def across_wait(e, g):
        across(e, 1, g).wait()
        across(e, 0, g).wait()
        first, size = (0, NZ * NC) if g < 0 else (16 * g, 16)

        @pl.when(t == 0)
        def _():
            yrecv[e, 0, first : first + size, :] = jnp.zeros((size, 128), F32)

        @pl.when(t == n_patch - 1)
        def _():
            yrecv[e, 1, first : first + size, :] = jnp.zeros((size, 128), F32)

    def halo_start(e, field):
        along(e, field, 1).start()
        along(e, field, 0).start()
        across_start(e, -1)

    def halo_wait(e, field):
        along_wait(e, field, 1)
        along_wait(e, field, 0)
        across_wait(e, -1)

    def put(e, field, z, plane):
        for q in range(NQ):
            for c in range(NC):
                field[z + 1, q, c] = plane[q][c]
        for c in range(NC):
            ysend[e, 0, pl.ds(z * NC + c, 1), :] = plane[0][c][0:1, :]
            ysend[e, 1, pl.ds(z * NC + c, 1), :] = plane[NQ - 1][c][7:8, :]

    lane = iota((8, 128), 1)
    row8 = iota((8, 128), 0)

    def around(e, field, z):
        centre = [[field[z + 1, q, c] for c in range(NC)] for q in range(NQ)]
        total = [[None] * NC for _ in range(NQ)]
        for q in range(NQ):
            right = [pltpu.roll(centre[q][c], 127, 1) for c in range(NC)]
            left = [pltpu.roll(centre[q][c], 1, 1) for c in range(NC)]
            for c in range(NC):
                after = right[c + 1] if c + 1 < NC else 0.0
                before = left[c - 1] if c else 0.0
                x = jnp.where(lane == 127, after, right[c]) + jnp.where(
                    lane == 0, before, left[c]
                )
                if q + 1 < NQ:
                    y_up = centre[q + 1][c]
                else:
                    edge = yrecv[e, 1, pl.ds(z * NC + c, 1), :]
                    y_up = jnp.where(
                        row8 == 7, jnp.broadcast_to(edge, (8, 128)), pltpu.roll(centre[0][c], 7, 0)
                    )
                if q:
                    y_down = centre[q - 1][c]
                else:
                    edge = yrecv[e, 0, pl.ds(z * NC + c, 1), :]
                    y_down = jnp.where(
                        row8 == 0,
                        jnp.broadcast_to(edge, (8, 128)),
                        pltpu.roll(centre[NQ - 1][c], 1, 0),
                    )
                total[q][c] = (field[z, q, c] + field[z + 2, q, c]) + (y_up + y_down) + x
        return centre, total

    for copy in loads[:NC]:
        copy.wait()

    @pl.loop(0, NZ)
    def _(z):
        put(
            0,
            t0,
            z,
            [
                [tin[c, z, pl.ds(q, 8, stride=NQ), :] for c in range(NC)]
                for q in range(NQ)
            ],
        )

    halo_start(0, t0)
    for copy in loads[2 * NC :]:
        copy.wait()

    @pl.loop(0, NCHUNK)
    def _(i):
        rows = pl.ds(pl.multiple_of(i * PER, PER), PER)
        pid = pid_ref[rows, :]
        owner = pid >> 1
        owner = lax.rem(owner, n_patch) * n_slab + lax.div(owner, n_patch)
        pid = ((pid & 1) * 128 + owner).astype(F32)
        uu = u_ref[rows, :]
        vv = v_ref[rows, :]
        places = iota((256, 128), 0).astype(F32).astype(BF16)
        for r in range(PER):
            at = slice(128 * r, 128 * r + 128)
            row = jnp.broadcast_to(pid[r : r + 1, :], (16, 128)).astype(BF16)
            for k in range(16):
                onehot[i, 16 * k : 16 * k + 16, at] = jnp.where(
                    places[16 * k : 16 * k + 16] == row, jnp.ones((), BF16), jnp.zeros((), BF16)
                )
            bu[i, :, at] = basis_weights(uu[r : r + 1, :])
            bv[i, :, at] = basis_weights(vv[r : r + 1, :])

    for copy in ag1:
        copy.wait()
    mine = pl.ds(pl.multiple_of(t * (4 * n_slab), 4 * n_slab), 4 * n_slab)
    cp_all[mine, :] = cp_row[...].reshape(4 * n_slab, 128)
    ag2 = []
    for k in range(1, n_patch):
        copy = pltpu.make_async_remote_copy(
            cp_all.at[mine], cp_all.at[mine], ag2_send.at[k], ag2_recv.at[k], on_patch(k), MESH
        )
        copy.start()
        ag2.append(copy)

    group = lane >> 5
    within = lane & 31
    for g in range(NZ):
        rows = slice(8 * g, 8 * g + 8)
        column = cell_ref[rows, :] & 511
        back = jnp.full((8, 128), -1, jnp.int32)
        for k in range(31, 0, -1):
            back = jnp.where(
                (pltpu.roll(column, k, 1) == column) & (within >= k), lane - k, back
            )
        chain[0, rows, :] = back
    for r in range(5):
        for g in range(NZ):
            rows = slice(8 * g, 8 * g + 8)
            back = chain[r, rows, :]
            index = back & 127
            count = jnp.ones((8, 128), F32) if r == 0 else summed[0, rows, :]
            seen = obs_ref[rows, :] if r == 0 else summed[1, rows, :]
            summed[0, rows, :] = count + jnp.where(back >= 0, lanes(count, index), 0.0)
            summed[1, rows, :] = seen + jnp.where(back >= 0, lanes(seen, index), 0.0)
            if r < 4:
                chain[r + 1, rows, :] = jnp.where(back >= 0, lanes(back, index), -1)

    lane16 = iota((16, 128), 1).astype(jnp.int16)

    @pl.loop(0, NZ // 2)
    def _(h):
        column = (cell_ref[pl.ds(pl.multiple_of(h * 16, 16), 16), :] & 511).astype(jnp.int16)
        for q in range(NQ):
            found = [jnp.full((16, 128), 32 * ((q + 1) % NQ), jnp.int16) for _ in range(NC)]
            for j in range(32):
                which = 32 * q + j
                off = jnp.broadcast_to(column[:, which : which + 1], (16, 128)) - lane16
                for c in range(NC):
                    found[c] = jnp.where(
                        off == jnp.int16(128 * c), jnp.int16(which), found[c]
                    )
            for c in range(NC):
                both = found[c].astype(jnp.int32)
                inv[2 * h, q, c] = both[0:8]
                inv[2 * h + 1, q, c] = both[8:16]

    for copy in loads[NC : 2 * NC]:
        copy.wait()
    halo_wait(0, t0)

    for copy in ag2:
        copy.wait()
    for c in range(2):
        for k in range(2):
            block = cp_all[pl.ds(2 * c + k, 128, stride=4), :].T
            high, low = split(block)
            lhs[128 * c : 128 * c + 128, 128 * k : 128 * k + 128] = high
            lhs[256 + 128 * c : 384 + 128 * c, 128 * k : 128 * k + 128] = low

    def face_rows(z):
        return pl.ds(pl.multiple_of(z * 8, 8), 8)

    def coefficients(z):
        for h in range(CHUNK // 256):
            at = slice(256 * h, 256 * h + 256)
            both = jnp.dot(lhs[...], onehot[z, :, at], preferred_element_type=F32)
            own = both[0:256] + both[256:512]
            total = own[0:16] * bu[z, 0:1, at]
            for a in range(1, 16):
                total = total + own[16 * a : 16 * a + 16] * bu[z, a : a + 1, at]
            value = -0.3 * jnp.sum(total * bv[z, :, at], axis=0, keepdims=True)
            for r in range(2):
                htc[pl.ds(z * PER + 2 * h + r, 1), :] = value[:, 128 * r : 128 * r + 128]

    def first_step(z):
        value = htc[face_rows(z), :]
        for r in range(5):
            back = chain[r, face_rows(z), :]
            value = value + jnp.where(back >= 0, lanes(value, back & 127), 0.0)
        count = summed[0, face_rows(z), :]
        seen = summed[1, face_rows(z), :]
        centre, total = around(0, t0, z)
        plane = [[None] * NC for _ in range(NQ)]
        for q in range(NQ):
            mine = group == q
            sources = [jnp.where(mine, x, 0.0) for x in (value, count, seen)]
            for c in range(NC):
                index = inv[z, q, c]
                here = lanes(sources[0], index)
                hfld[z, q, c] = here
                cntf[z, q, c] = lanes(sources[1], index)
                obsf[z, q, c] = lanes(sources[2], index)
                diffusion = cin[c, z, pl.ds(q, 8, stride=NQ), :]
                cond[z, q, c] = diffusion
                now = centre[q][c]
                plane[q][c] = now + diffusion * (total[q][c] - 6.0 * now) + here * now
        put(1, t1, z, plane)

    def second_step(z):
        centre, total = around(1, t1, z)
        weighted = [[None] * NC for _ in range(NQ)]
        for q in range(NQ):
            for c in range(NC):
                here = cond[z, q, c]
                last = (
                    centre[q][c]
                    + here * (total[q][c] - 6.0 * centre[q][c])
                    + hfld[z, q, c] * centre[q][c]
                )
                tst[c, z, pl.ds(q, 8, stride=NQ), :] = last
                adjoint = cntf[z, q, c] * last - obsf[z, q, c]
                adj2[z, q, c] = adjoint
                weighted[q][c] = here * adjoint
        put(2, w2, z, weighted)

    def first_back(z):
        centre, total = around(2, w2, z)
        column = cell_ref[face_rows(z), :] & 511
        key = group * NC + (column >> 7)
        spot = column & 127
        picked = jnp.zeros((8, 128), F32)
        weighted = [[None] * NC for _ in range(NQ)]
        for q in range(NQ):
            for c in range(NC):
                later = adj2[z, q, c]
                adjoint = later + total[q][c] - 6.0 * centre[q][c] + hfld[z, q, c] * later
                adj1[z, q, c] = adjoint
                weighted[q][c] = cond[z, q, c] * adjoint
                product = later * t1[z + 1, q, c] + adjoint * t0[z + 1, q, c]
                picked = jnp.where(key == NC * q + c, lanes(product, spot), picked)
        sens[face_rows(z), :] = -0.3 * picked
        put(3, w1, z, weighted)

    def second_back(z):
        centre, total = around(3, w1, z)
        for q in range(NQ):
            for c in range(NC):
                later = adj1[z, q, c]
                ast[c, z, pl.ds(q, 8, stride=NQ), :] = (
                    later + total[q][c] - 6.0 * centre[q][c] + hfld[z, q, c] * later
                )

    def gradient(z):
        value = sens[face_rows(z), :]
        for r in range(PER):
            at = slice(128 * r, 128 * r + 128)
            right = bv[z, :, at] * value[r : r + 1, :]
            for a in range(16):
                high, low = split(right * bu[z, a : a + 1, at])
                wbuf[16 * a : 16 * a + 16, at] = high
                wbuf[256 + 16 * a : 272 + 16 * a, at] = low
        acc[...] += lax.dot_general(
            wbuf[...], onehot[z], (((1,), (1,)), ((), ())), preferred_element_type=F32
        )

    coefficients(NZ - 1)

    @pl.loop(0, 5)
    def _(k):
        first_step(lax.rem(k + NZ - 1, NZ))
        coefficients(k)

    along(1, t1, 1).start()
    along(1, t1, 0).start()
    across_start(1, 0)

    @pl.loop(5, 9)
    def _(k):
        first_step(k - 1)
        coefficients(k)

    across_start(1, 1)

    @pl.loop(9, 11)
    def _(k):
        first_step(k - 1)
        coefficients(k)

    along_wait(1, t1, 1)
    across_wait(1, 0)

    @pl.loop(11, 13)
    def _(k):
        second_step(2 * k - 22)
        second_step(2 * k - 21)
        first_step(k - 1)
        coefficients(k)

    across_start(1, 2)
    along(2, w2, 0).start()
    across_start(2, 0)
    across_wait(1, 1)

    @pl.loop(13, 15)
    def _(k):
        second_step(2 * k - 22)
        second_step(2 * k - 21)
        first_step(k - 1)
        coefficients(k)

    across_start(2, 1)
    first_step(NZ - 2)
    across_start(1, 3)

    acc[...] = jnp.zeros((512, 256), F32)
    across_wait(2, 0)
    first_back(1)
    across_wait(1, 2)

    @pl.loop(1, 3)
    def _(j):
        gradient(j)
        first_back(j + 1)
        second_step(2 * j + 6)
        second_step(2 * j + 7)

    across_start(2, 2)
    across_wait(2, 1)
    along_wait(1, t1, 0)
    across_wait(1, 3)

    @pl.loop(3, 5)
    def _(j):
        gradient(j)
        first_back(j + 1)
        second_step(2 * j + 6)
        second_step(2 * j + 7)

    along(2, w2, 1).start()
    across_start(2, 3)

    @pl.loop(5, 7)
    def _(j):
        gradient(j)
        first_back(j + 1)

    across_start(3, 1)
    across_wait(2, 2)

    @pl.loop(7, 11)
    def _(j):
        gradient(j)
        first_back(j + 1)

    across_start(3, 2)
    along_wait(2, w2, 0)
    across_wait(2, 3)
    across_wait(3, 1)

    @pl.loop(11, 15)
    def _(j):
        gradient(j)
        first_back(j + 1)
        second_back(j - 7)

    along(3, w1, 1).start()
    across_start(3, 3)
    along_wait(2, w2, 1)
    gradient(NZ - 1)
    first_back(0)
    along(3, w1, 0).start()
    across_start(3, 0)
    gradient(0)

    for c in range(2):
        for k in range(2):
            cols = slice(128 * k, 128 * k + 128)
            block = acc[128 * c : 128 * c + 128, cols] + acc[256 + 128 * c : 384 + 128 * c, cols]
            grad[pl.ds(2 * c + k, 128, stride=4), :] = block.T

    rs1 = []
    for k in range(1, n_patch):
        their = lax.rem(t + k, n_patch)
        copy = pltpu.make_async_remote_copy(
            grad.at[pl.ds(pl.multiple_of(their * (4 * n_slab), 4 * n_slab), 4 * n_slab)],
            part1.at[k],
            rs1_send.at[k],
            rs1_recv.at[k],
            on_patch(k),
            MESH,
        )
        copy.start()
        rs1.append(copy)

    across_wait(3, 2)
    across_wait(3, 3)

    @pl.loop(8, 15)
    def _(z):
        second_back(z)

    for copy in rs1:
        copy.wait()
    total = grad[mine, :]
    for k in range(1, n_patch):
        total = total + part1[k]
    part2_src[...] = total.reshape(n_slab, 4, 128)
    rs2 = []
    for k in range(1, n_slab):
        copy = pltpu.make_async_remote_copy(
            part2_src.at[lax.rem(s + k, n_slab)],
            part2.at[k],
            rs2_send.at[k],
            rs2_recv.at[k],
            on_slab(k),
            MESH,
        )
        copy.start()
        rs2.append(copy)
    along_wait(3, w1, 1)
    along_wait(3, w1, 0)
    across_wait(3, 0)

    @pl.loop(0, 5)
    def _(k):
        second_back(lax.rem(k + NZ - 1, NZ))

    for copy in rs2:
        copy.wait()
    total = part2_src[s]
    for k in range(1, n_slab):
        total = total + part2[k]
    gout_ref[:, 0:128] = total[0:2]
    gout_ref[:, 128:256] = total[2:4]


def hand_out(a_in, b_in, c_in, a_out, b_out, c_out, sem):
    copies = [pltpu.make_async_copy(c_in, c_out, sem.at[2 * NC])]
    for n, (src, dst) in enumerate(((a_in, a_out), (b_in, b_out))):
        for c in range(NC):
            copies.append(
                pltpu.make_async_copy(
                    src.at[c], dst.at[:, :, pl.ds(128 * c, 128)], sem.at[NC * n + c]
                )
            )
    for copy in copies:
        copy.start()
    for copy in copies:
        copy.wait()


def local(n_slab, n_patch, temp, cond, cell, pid, u, v, observed, points):
    field = (NZ,) + PLANE
    padded = (NZ + 2,) + PLANE
    natural = (NC, NZ, 32, 128)
    vmem = pltpu.VMEM
    dma = pltpu.SemaphoreType.DMA
    scratch = [
        vmem(natural, F32),
        vmem(natural, F32),
        vmem((ROWS, 128), jnp.int32),
        vmem((ROWS, 128), jnp.int32),
        vmem((ROWS, 128), F32),
        vmem((ROWS, 128), F32),
        vmem((ROWS, 128), F32),
        vmem(points.shape, F32),
        vmem(padded, F32),
        vmem(padded, F32),
        vmem(padded, F32),
        vmem(padded, F32),
        vmem(field, F32),
        vmem(field, F32),
        vmem(field, F32),
        vmem(field, F32),
        vmem(field, F32),
        vmem(field, F32),
        vmem(field, jnp.int32),
        vmem((5, ROWS, 128), jnp.int32),
        vmem((2, ROWS, 128), F32),
        vmem((4, 2, NZ * NC, 128), F32),
        vmem((4, 2, NZ * NC, 128), F32),
        vmem((4, 128), F32),
        vmem((n_slab, 4, 128), F32),
        vmem((4 * n_slab * n_patch, 128), F32),
        vmem((512, 256), BF16),
        vmem((NCHUNK, 256, CHUNK), BF16),
        vmem((NCHUNK, 16, CHUNK), F32),
        vmem((NCHUNK, 16, CHUNK), F32),
        vmem((512, CHUNK), BF16),
        vmem((ROWS, 128), F32),
        vmem((ROWS, 128), F32),
        vmem((512, 256), F32),
        vmem((4 * n_slab * n_patch, 128), F32),
        vmem((n_patch, 4 * n_slab, 128), F32),
        vmem((n_slab, 4, 128), F32),
        vmem((n_slab, 4, 128), F32),
        dma((2 * NC + 6,)),
        dma((n_slab,)),
        dma((n_slab,)),
        dma((n_patch,)),
        dma((n_patch,)),
        dma((n_patch,)),
        dma((n_patch,)),
        dma((n_slab,)),
        dma((n_slab,)),
        dma((4, 10)),
        dma((4, 10)),
    ]
    whole = pl.BlockSpec(memory_space=pltpu.VMEM)
    anywhere = pl.BlockSpec(memory_space=pl.ANY)
    rows = (ROWS, 128)
    final, adjoint, points_out = pl.pallas_call(
        functools.partial(kernel, n_slab, n_patch),
        out_shape=(vmem(natural, F32), vmem(natural, F32), vmem(points.shape, F32)),
        in_specs=[anywhere] * 8,
        out_specs=(whole,) * 3,
        scratch_shapes=scratch,
        compiler_params=pltpu.CompilerParams(
            collective_id=0, has_side_effects=True, vmem_limit_bytes=56 * 1024 * 1024
        ),
        name="adjoint",
    )(
        temp,
        cond,
        cell.reshape(rows),
        pid.reshape(rows),
        u.reshape(rows),
        v.reshape(rows),
        observed.reshape(rows),
        points,
    )
    return pl.pallas_call(
        hand_out,
        out_shape=(
            jax.ShapeDtypeStruct(temp.shape, F32),
            jax.ShapeDtypeStruct(temp.shape, F32),
            jax.ShapeDtypeStruct(points.shape, F32),
        ),
        in_specs=[whole] * 3,
        out_specs=(anywhere,) * 3,
        scratch_shapes=[dma((2 * NC + 1,))],
        name="hand_out",
    )(*(pltpu.with_memory_space_constraint(x, pltpu.VMEM) for x in (final, adjoint, points_out)))


def solution(mesh):
    in_specs = (
        P("slab", "patch", None),
        P("slab", "patch", None),
        P(("slab", "patch")),
        P(("slab", "patch"), None),
        P(("slab", "patch")),
        P(("slab", "patch")),
        P(("slab", "patch")),
        P(("slab", "patch"), None),
    )
    out_specs = (P("slab", "patch", None), P("slab", "patch", None), P(("slab", "patch"), None))
    return jax.shard_map(
        functools.partial(local, mesh.shape["slab"], mesh.shape["patch"]),
        mesh=mesh,
        in_specs=in_specs,
        out_specs=out_specs,
        check_vma=False,
    )
```

```python
import functools

import jax
import jax.numpy as jnp
from jax import lax
from jax.experimental import pallas as pl
from jax.experimental.pallas import tpu as pltpu
from jax.sharding import PartitionSpec as P

MESH = pl.DeviceIdType.MESH
F32 = jnp.float32
BF16 = jnp.bfloat16
NZ = 16
NQ = 4
NC = 4
PLANE = (NQ, NC, 8, 128)
ROWS = 128
CHUNK = 1024
PER = CHUNK // 128
NCHUNK = ROWS * 128 // CHUNK


def iota(shape, dim):
    return lax.broadcasted_iota(jnp.int32, shape, dim)


def lanes(x, index):
    return jnp.take_along_axis(x, index, axis=1, mode="promise_in_bounds")


def basis_weights(param):
    y = jnp.abs((3.0 + 13.0 * param) - (iota((16, 128), 0) + 2).astype(F32))
    wide = jnp.maximum(2.0 - y, 0.0)
    narrow = jnp.maximum(1.0 - y, 0.0)
    return wide * wide * wide * (1.0 / 6.0) - narrow * narrow * narrow * (4.0 / 6.0)


def split(x):
    high = x.astype(BF16)
    return high, (x - high.astype(F32)).astype(BF16)


def kernel(
    n_slab,
    n_patch,
    temp_hbm,
    cond_hbm,
    cell_hbm,
    pid_hbm,
    u_hbm,
    v_hbm,
    obs_hbm,
    cp_hbm,
    tst,
    ast,
    gout_ref,
    tin,
    cin,
    cell_ref,
    pid_ref,
    u_ref,
    v_ref,
    obs_ref,
    cp_ref,
    t0,
    t1,
    w2,
    w1,
    cond,
    hfld,
    cntf,
    obsf,
    adj2,
    adj1,
    inv,
    chain,
    summed,
    ysend,
    yrecv,
    cp_src,
    cp_row,
    cp_all,
    lhs,
    onehot,
    bu,
    bv,
    wbuf,
    htc,
    sens,
    acc,
    grad,
    part1,
    part2_src,
    part2,
    in_sem,
    ag1_send,
    ag1_recv,
    ag2_send,
    ag2_recv,
    rs1_send,
    rs1_recv,
    rs2_send,
    rs2_recv,
    halo_send,
    halo_recv,
):
    s = lax.axis_index("slab")
    t = lax.axis_index("patch")

    def on_slab(k):
        return (lax.rem(s + k, n_slab), t)

    def on_patch(k):
        return (s, lax.rem(t + k, n_patch))

    load_cp = pltpu.make_async_copy(cp_hbm, cp_ref, in_sem.at[2 * NC + 5])
    load_cp.start()
    barrier = pltpu.get_barrier_semaphore()
    for k in range(1, n_patch):
        pl.semaphore_signal(barrier, inc=1, device_id=on_patch(k), device_id_type=MESH)
    for k in range(1, n_slab):
        pl.semaphore_signal(barrier, inc=1, device_id=on_slab(k), device_id_type=MESH)
    loads = []
    for a, (src, dst) in enumerate(((temp_hbm, tin), (cond_hbm, cin))):
        for c in range(NC):
            loads.append(
                pltpu.make_async_copy(
                    src.at[:, :, pl.ds(128 * c, 128)], dst.at[c], in_sem.at[NC * a + c]
                )
            )
    small = ((pid_hbm, pid_ref), (u_hbm, u_ref), (v_hbm, v_ref), (cell_hbm, cell_ref), (obs_hbm, obs_ref))
    for k, (src, dst) in enumerate(small):
        loads.append(pltpu.make_async_copy(src, dst, in_sem.at[2 * NC + k]))
    for copy in loads[:NC] + loads[2 * NC :] + loads[NC : 2 * NC]:
        copy.start()
    load_cp.wait()
    cp_src[0:2, :] = cp_ref[:, 0:128]
    cp_src[2:4, :] = cp_ref[:, 128:256]
    cp_row[s] = cp_src[...]
    pl.semaphore_wait(barrier, n_slab + n_patch - 2)

    ag1 = []
    for k in range(1, n_slab):
        copy = pltpu.make_async_remote_copy(
            cp_src, cp_row.at[s], ag1_send.at[k], ag1_recv.at[k], on_slab(k), MESH
        )
        copy.start()
        ag1.append(copy)

    def along(e, field, up):
        return pltpu.make_async_remote_copy(
            field.at[NZ if up else 1],
            field.at[0 if up else NZ + 1],
            halo_send.at[e, 8 + up],
            halo_recv.at[e, 8 + up],
            on_slab(1 if up else n_slab - 1),
            MESH,
        )

    def across(e, up, g):
        rows = pl.ds(0, NZ * NC) if g < 0 else pl.ds(16 * g, 16)
        slot = max(g, 0) * 2 + up
        return pltpu.make_async_remote_copy(
            ysend.at[e, up, rows],
            yrecv.at[e, 1 - up, rows],
            halo_send.at[e, slot],
            halo_recv.at[e, slot],
            on_patch(1 if up else n_patch - 1),
            MESH,
        )

    def along_wait(e, field, up):
        along(e, field, up).wait()

        @pl.when(s == (0 if up else n_slab - 1))
        def _():
            field[0 if up else NZ + 1] = jnp.zeros(PLANE, F32)

    def across_start(e, g):
        across(e, 1, g).start()
        across(e, 0, g).start()

    def across_wait(e, g):
        across(e, 1, g).wait()
        across(e, 0, g).wait()
        first, size = (0, NZ * NC) if g < 0 else (16 * g, 16)

        @pl.when(t == 0)
        def _():
            yrecv[e, 0, first : first + size, :] = jnp.zeros((size, 128), F32)

        @pl.when(t == n_patch - 1)
        def _():
            yrecv[e, 1, first : first + size, :] = jnp.zeros((size, 128), F32)

    def halo_start(e, field):
        along(e, field, 1).start()
        along(e, field, 0).start()
        across_start(e, -1)

    def halo_wait(e, field):
        along_wait(e, field, 1)
        along_wait(e, field, 0)
        across_wait(e, -1)

    def put(e, field, z, plane):
        for q in range(NQ):
            for c in range(NC):
                field[z + 1, q, c] = plane[q][c]
        for c in range(NC):
            ysend[e, 0, pl.ds(z * NC + c, 1), :] = plane[0][c][0:1, :]
            ysend[e, 1, pl.ds(z * NC + c, 1), :] = plane[NQ - 1][c][7:8, :]

    lane = iota((8, 128), 1)
    row8 = iota((8, 128), 0)

    def around(e, field, z):
        centre = [[field[z + 1, q, c] for c in range(NC)] for q in range(NQ)]
        total = [[None] * NC for _ in range(NQ)]
        for q in range(NQ):
            right = [pltpu.roll(centre[q][c], 127, 1) for c in range(NC)]
            left = [pltpu.roll(centre[q][c], 1, 1) for c in range(NC)]
            for c in range(NC):
                after = right[c + 1] if c + 1 < NC else 0.0
                before = left[c - 1] if c else 0.0
                x = jnp.where(lane == 127, after, right[c]) + jnp.where(
                    lane == 0, before, left[c]
                )
                if q + 1 < NQ:
                    y_up = centre[q + 1][c]
                else:
                    edge = yrecv[e, 1, pl.ds(z * NC + c, 1), :]
                    y_up = jnp.where(
                        row8 == 7, jnp.broadcast_to(edge, (8, 128)), pltpu.roll(centre[0][c], 7, 0)
                    )
                if q:
                    y_down = centre[q - 1][c]
                else:
                    edge = yrecv[e, 0, pl.ds(z * NC + c, 1), :]
                    y_down = jnp.where(
                        row8 == 0,
                        jnp.broadcast_to(edge, (8, 128)),
                        pltpu.roll(centre[NQ - 1][c], 1, 0),
                    )
                total[q][c] = (field[z, q, c] + field[z + 2, q, c]) + (y_up + y_down) + x
        return centre, total

    for copy in loads[:NC]:
        copy.wait()

    @pl.loop(0, NZ)
    def _(z):
        put(
            0,
            t0,
            z,
            [
                [tin[c, z, pl.ds(q, 8, stride=NQ), :] for c in range(NC)]
                for q in range(NQ)
            ],
        )

    halo_start(0, t0)
    for copy in loads[2 * NC :]:
        copy.wait()

    def prepare(i):
        rows = pl.ds(pl.multiple_of(i * PER, PER), PER)
        pid = pid_ref[rows, :]
        owner = pid >> 1
        owner = lax.rem(owner, n_patch) * n_slab + lax.div(owner, n_patch)
        pid = ((pid & 1) * 128 + owner).astype(F32)
        uu = u_ref[rows, :]
        vv = v_ref[rows, :]
        places = iota((256, 128), 0).astype(F32).astype(BF16)
        for r in range(PER):
            at = slice(128 * r, 128 * r + 128)
            row = jnp.broadcast_to(pid[r : r + 1, :], (16, 128)).astype(BF16)
            for k in range(16):
                onehot[i, 16 * k : 16 * k + 16, at] = jnp.where(
                    places[16 * k : 16 * k + 16] == row, jnp.ones((), BF16), jnp.zeros((), BF16)
                )
            bu[i, :, at] = basis_weights(uu[r : r + 1, :])
            bv[i, :, at] = basis_weights(vv[r : r + 1, :])

    pl.loop(0, NCHUNK // 2)(prepare)

    for copy in ag1:
        copy.wait()
    mine = pl.ds(pl.multiple_of(t * (4 * n_slab), 4 * n_slab), 4 * n_slab)
    cp_all[mine, :] = cp_row[...].reshape(4 * n_slab, 128)
    ag2 = []
    for k in range(1, n_patch):
        copy = pltpu.make_async_remote_copy(
            cp_all.at[mine], cp_all.at[mine], ag2_send.at[k], ag2_recv.at[k], on_patch(k), MESH
        )
        copy.start()
        ag2.append(copy)

    pl.loop(NCHUNK // 2, NCHUNK)(prepare)

    group = lane >> 5
    within = lane & 31
    for g in range(NZ):
        rows = slice(8 * g, 8 * g + 8)
        column = cell_ref[rows, :] & 511
        back = jnp.full((8, 128), -1, jnp.int32)
        for k in range(31, 0, -1):
            back = jnp.where(
                (pltpu.roll(column, k, 1) == column) & (within >= k), lane - k, back
            )
        chain[0, rows, :] = back
    for r in range(5):
        for g in range(NZ):
            rows = slice(8 * g, 8 * g + 8)
            back = chain[r, rows, :]
            index = back & 127
            count = jnp.ones((8, 128), F32) if r == 0 else summed[0, rows, :]
            seen = obs_ref[rows, :] if r == 0 else summed[1, rows, :]
            summed[0, rows, :] = count + jnp.where(back >= 0, lanes(count, index), 0.0)
            summed[1, rows, :] = seen + jnp.where(back >= 0, lanes(seen, index), 0.0)
            if r < 4:
                chain[r + 1, rows, :] = jnp.where(back >= 0, lanes(back, index), -1)

    lane16 = iota((16, 128), 1).astype(jnp.int16)

    @pl.loop(0, NZ // 2)
    def _(h):
        column = (cell_ref[pl.ds(pl.multiple_of(h * 16, 16), 16), :] & 511).astype(jnp.int16)
        for q in range(NQ):
            found = [jnp.full((16, 128), 32 * ((q + 1) % NQ), jnp.int16) for _ in range(NC)]
            for j in range(32):
                which = 32 * q + j
                off = jnp.broadcast_to(column[:, which : which + 1], (16, 128)) - lane16
                for c in range(NC):
                    found[c] = jnp.where(
                        off == jnp.int16(128 * c), jnp.int16(which), found[c]
                    )
            for c in range(NC):
                both = found[c].astype(jnp.int32)
                inv[2 * h, q, c] = both[0:8]
                inv[2 * h + 1, q, c] = both[8:16]

    for copy in loads[NC : 2 * NC]:
        copy.wait()
    halo_wait(0, t0)

    for copy in ag2:
        copy.wait()
    for c in range(2):
        for k in range(2):
            block = cp_all[pl.ds(2 * c + k, 128, stride=4), :].T
            high, low = split(block)
            lhs[128 * c : 128 * c + 128, 128 * k : 128 * k + 128] = high
            lhs[256 + 128 * c : 384 + 128 * c, 128 * k : 128 * k + 128] = low

    def face_rows(z):
        return pl.ds(pl.multiple_of(z * 8, 8), 8)

    def coefficients(z):
        for h in range(CHUNK // 256):
            at = slice(256 * h, 256 * h + 256)
            both = jnp.dot(lhs[...], onehot[z, :, at], preferred_element_type=F32)
            own = both[0:256] + both[256:512]
            total = own[0:16] * bu[z, 0:1, at]
            for a in range(1, 16):
                total = total + own[16 * a : 16 * a + 16] * bu[z, a : a + 1, at]
            value = -0.3 * jnp.sum(total * bv[z, :, at], axis=0, keepdims=True)
            for r in range(2):
                htc[pl.ds(z * PER + 2 * h + r, 1), :] = value[:, 128 * r : 128 * r + 128]

    def first_step(z):
        value = htc[face_rows(z), :]
        for r in range(5):
            back = chain[r, face_rows(z), :]
            value = value + jnp.where(back >= 0, lanes(value, back & 127), 0.0)
        count = summed[0, face_rows(z), :]
        seen = summed[1, face_rows(z), :]
        centre, total = around(0, t0, z)
        plane = [[None] * NC for _ in range(NQ)]
        for q in range(NQ):
            mine = group == q
            sources = [jnp.where(mine, x, 0.0) for x in (value, count, seen)]
            for c in range(NC):
                index = inv[z, q, c]
                here = lanes(sources[0], index)
                hfld[z, q, c] = here
                cntf[z, q, c] = lanes(sources[1], index)
                obsf[z, q, c] = lanes(sources[2], index)
                diffusion = cin[c, z, pl.ds(q, 8, stride=NQ), :]
                cond[z, q, c] = diffusion
                now = centre[q][c]
                plane[q][c] = now + diffusion * (total[q][c] - 6.0 * now) + here * now
        put(1, t1, z, plane)

    def second_step(z):
        centre, total = around(1, t1, z)
        weighted = [[None] * NC for _ in range(NQ)]
        for q in range(NQ):
            for c in range(NC):
                here = cond[z, q, c]
                last = (
                    centre[q][c]
                    + here * (total[q][c] - 6.0 * centre[q][c])
                    + hfld[z, q, c] * centre[q][c]
                )
                tst[c, z, pl.ds(q, 8, stride=NQ), :] = last
                adjoint = cntf[z, q, c] * last - obsf[z, q, c]
                adj2[z, q, c] = adjoint
                weighted[q][c] = here * adjoint
        put(2, w2, z, weighted)

    def first_back(z):
        centre, total = around(2, w2, z)
        column = cell_ref[face_rows(z), :] & 511
        key = group * NC + (column >> 7)
        spot = column & 127
        picked = jnp.zeros((8, 128), F32)
        weighted = [[None] * NC for _ in range(NQ)]
        for q in range(NQ):
            for c in range(NC):
                later = adj2[z, q, c]
                adjoint = later + total[q][c] - 6.0 * centre[q][c] + hfld[z, q, c] * later
                adj1[z, q, c] = adjoint
                weighted[q][c] = cond[z, q, c] * adjoint
                product = later * t1[z + 1, q, c] + adjoint * t0[z + 1, q, c]
                picked = jnp.where(key == NC * q + c, lanes(product, spot), picked)
        sens[face_rows(z), :] = -0.3 * picked
        put(3, w1, z, weighted)

    def second_back(z):
        centre, total = around(3, w1, z)
        for q in range(NQ):
            for c in range(NC):
                later = adj1[z, q, c]
                ast[c, z, pl.ds(q, 8, stride=NQ), :] = (
                    later + total[q][c] - 6.0 * centre[q][c] + hfld[z, q, c] * later
                )

    def gradient(z):
        value = sens[face_rows(z), :]
        for r in range(PER):
            at = slice(128 * r, 128 * r + 128)
            right = bv[z, :, at] * value[r : r + 1, :]
            for a in range(16):
                high, low = split(right * bu[z, a : a + 1, at])
                wbuf[16 * a : 16 * a + 16, at] = high
                wbuf[256 + 16 * a : 272 + 16 * a, at] = low
        acc[...] += lax.dot_general(
            wbuf[...], onehot[z], (((1,), (1,)), ((), ())), preferred_element_type=F32
        )

    coefficients(NZ - 1)

    @pl.loop(0, 5)
    def _(k):
        first_step(lax.rem(k + NZ - 1, NZ))
        coefficients(k)

    along(1, t1, 1).start()
    along(1, t1, 0).start()
    across_start(1, 0)

    @pl.loop(5, 9)
    def _(k):
        first_step(k - 1)
        coefficients(k)

    across_start(1, 1)

    @pl.loop(9, 11)
    def _(k):
        first_step(k - 1)
        coefficients(k)

    along_wait(1, t1, 1)
    across_wait(1, 0)

    @pl.loop(11, 13)
    def _(k):
        second_step(2 * k - 22)
        second_step(2 * k - 21)
        first_step(k - 1)
        coefficients(k)

    across_start(1, 2)
    along(2, w2, 0).start()
    across_start(2, 0)
    across_wait(1, 1)

    @pl.loop(13, 15)
    def _(k):
        second_step(2 * k - 22)
        second_step(2 * k - 21)
        first_step(k - 1)
        coefficients(k)

    across_start(2, 1)
    first_step(NZ - 2)
    across_start(1, 3)

    acc[...] = jnp.zeros((512, 256), F32)
    across_wait(2, 0)
    first_back(1)
    across_wait(1, 2)

    @pl.loop(1, 3)
    def _(j):
        gradient(j)
        first_back(j + 1)
        second_step(2 * j + 6)
        second_step(2 * j + 7)

    across_start(2, 2)
    across_wait(2, 1)
    along_wait(1, t1, 0)
    across_wait(1, 3)

    @pl.loop(3, 5)
    def _(j):
        gradient(j)
        first_back(j + 1)
        second_step(2 * j + 6)
        second_step(2 * j + 7)

    along(2, w2, 1).start()
    across_start(2, 3)

    @pl.loop(5, 7)
    def _(j):
        gradient(j)
        first_back(j + 1)

    across_start(3, 1)
    across_wait(2, 2)

    @pl.loop(7, 11)
    def _(j):
        gradient(j)
        first_back(j + 1)

    across_start(3, 2)
    along_wait(2, w2, 0)
    across_wait(2, 3)
    across_wait(3, 1)

    @pl.loop(11, 15)
    def _(j):
        gradient(j)
        first_back(j + 1)
        second_back(j - 7)

    along(3, w1, 1).start()
    across_start(3, 3)
    along_wait(2, w2, 1)
    gradient(NZ - 1)
    first_back(0)
    along(3, w1, 0).start()
    across_start(3, 0)
    gradient(0)

    for c in range(2):
        for k in range(2):
            cols = slice(128 * k, 128 * k + 128)
            block = acc[128 * c : 128 * c + 128, cols] + acc[256 + 128 * c : 384 + 128 * c, cols]
            grad[pl.ds(2 * c + k, 128, stride=4), :] = block.T

    rs1 = []
    for k in range(1, n_patch):
        their = lax.rem(t + k, n_patch)
        copy = pltpu.make_async_remote_copy(
            grad.at[pl.ds(pl.multiple_of(their * (4 * n_slab), 4 * n_slab), 4 * n_slab)],
            part1.at[k],
            rs1_send.at[k],
            rs1_recv.at[k],
            on_patch(k),
            MESH,
        )
        copy.start()
        rs1.append(copy)

    across_wait(3, 2)
    across_wait(3, 3)

    @pl.loop(8, 15)
    def _(z):
        second_back(z)

    for copy in rs1:
        copy.wait()
    total = grad[mine, :]
    for k in range(1, n_patch):
        total = total + part1[k]
    part2_src[...] = total.reshape(n_slab, 4, 128)
    rs2 = []
    for k in range(1, n_slab):
        copy = pltpu.make_async_remote_copy(
            part2_src.at[lax.rem(s + k, n_slab)],
            part2.at[k],
            rs2_send.at[k],
            rs2_recv.at[k],
            on_slab(k),
            MESH,
        )
        copy.start()
        rs2.append(copy)
    along_wait(3, w1, 1)
    along_wait(3, w1, 0)
    across_wait(3, 0)

    @pl.loop(0, 5)
    def _(k):
        second_back(lax.rem(k + NZ - 1, NZ))

    for copy in rs2:
        copy.wait()
    total = part2_src[s]
    for k in range(1, n_slab):
        total = total + part2[k]
    gout_ref[:, 0:128] = total[0:2]
    gout_ref[:, 128:256] = total[2:4]


def hand_out(a_in, b_in, c_in, a_out, b_out, c_out, sem):
    copies = [pltpu.make_async_copy(c_in, c_out, sem.at[2 * NC])]
    for n, (src, dst) in enumerate(((a_in, a_out), (b_in, b_out))):
        for c in range(NC):
            copies.append(
                pltpu.make_async_copy(
                    src.at[c], dst.at[:, :, pl.ds(128 * c, 128)], sem.at[NC * n + c]
                )
            )
    for copy in copies:
        copy.start()
    for copy in copies:
        copy.wait()


def local(n_slab, n_patch, temp, cond, cell, pid, u, v, observed, points):
    field = (NZ,) + PLANE
    padded = (NZ + 2,) + PLANE
    natural = (NC, NZ, 32, 128)
    vmem = pltpu.VMEM
    dma = pltpu.SemaphoreType.DMA
    scratch = [
        vmem(natural, F32),
        vmem(natural, F32),
        vmem((ROWS, 128), jnp.int32),
        vmem((ROWS, 128), jnp.int32),
        vmem((ROWS, 128), F32),
        vmem((ROWS, 128), F32),
        vmem((ROWS, 128), F32),
        vmem(points.shape, F32),
        vmem(padded, F32),
        vmem(padded, F32),
        vmem(padded, F32),
        vmem(padded, F32),
        vmem(field, F32),
        vmem(field, F32),
        vmem(field, F32),
        vmem(field, F32),
        vmem(field, F32),
        vmem(field, F32),
        vmem(field, jnp.int32),
        vmem((5, ROWS, 128), jnp.int32),
        vmem((2, ROWS, 128), F32),
        vmem((4, 2, NZ * NC, 128), F32),
        vmem((4, 2, NZ * NC, 128), F32),
        vmem((4, 128), F32),
        vmem((n_slab, 4, 128), F32),
        vmem((4 * n_slab * n_patch, 128), F32),
        vmem((512, 256), BF16),
        vmem((NCHUNK, 256, CHUNK), BF16),
        vmem((NCHUNK, 16, CHUNK), F32),
        vmem((NCHUNK, 16, CHUNK), F32),
        vmem((512, CHUNK), BF16),
        vmem((ROWS, 128), F32),
        vmem((ROWS, 128), F32),
        vmem((512, 256), F32),
        vmem((4 * n_slab * n_patch, 128), F32),
        vmem((n_patch, 4 * n_slab, 128), F32),
        vmem((n_slab, 4, 128), F32),
        vmem((n_slab, 4, 128), F32),
        dma((2 * NC + 6,)),
        dma((n_slab,)),
        dma((n_slab,)),
        dma((n_patch,)),
        dma((n_patch,)),
        dma((n_patch,)),
        dma((n_patch,)),
        dma((n_slab,)),
        dma((n_slab,)),
        dma((4, 10)),
        dma((4, 10)),
    ]
    whole = pl.BlockSpec(memory_space=pltpu.VMEM)
    anywhere = pl.BlockSpec(memory_space=pl.ANY)
    rows = (ROWS, 128)
    final, adjoint, points_out = pl.pallas_call(
        functools.partial(kernel, n_slab, n_patch),
        out_shape=(vmem(natural, F32), vmem(natural, F32), vmem(points.shape, F32)),
        in_specs=[anywhere] * 8,
        out_specs=(whole,) * 3,
        scratch_shapes=scratch,
        compiler_params=pltpu.CompilerParams(
            collective_id=0, has_side_effects=True, vmem_limit_bytes=56 * 1024 * 1024
        ),
        name="adjoint",
    )(
        temp,
        cond,
        cell.reshape(rows),
        pid.reshape(rows),
        u.reshape(rows),
        v.reshape(rows),
        observed.reshape(rows),
        points,
    )
    return pl.pallas_call(
        hand_out,
        out_shape=(
            jax.ShapeDtypeStruct(temp.shape, F32),
            jax.ShapeDtypeStruct(temp.shape, F32),
            jax.ShapeDtypeStruct(points.shape, F32),
        ),
        in_specs=[whole] * 3,
        out_specs=(anywhere,) * 3,
        scratch_shapes=[dma((2 * NC + 1,))],
        name="hand_out",
    )(*(pltpu.with_memory_space_constraint(x, pltpu.VMEM) for x in (final, adjoint, points_out)))


def solution(mesh):
    in_specs = (
        P("slab", "patch", None),
        P("slab", "patch", None),
        P(("slab", "patch")),
        P(("slab", "patch"), None),
        P(("slab", "patch")),
        P(("slab", "patch")),
        P(("slab", "patch")),
        P(("slab", "patch"), None),
    )
    out_specs = (P("slab", "patch", None), P("slab", "patch", None), P(("slab", "patch"), None))
    return jax.shard_map(
        functools.partial(local, mesh.shape["slab"], mesh.shape["patch"]),
        mesh=mesh,
        in_specs=in_specs,
        out_specs=out_specs,
        check_vma=False,
    )
```
